128 devices in a mesh: ctx: 64 (over x_lo, y, z, core), fsdp: 2 (over x_hi).
Axes of the slice: x: 4 (x_hi: 2, x_lo: 2; x = x_hi * 2 + x_lo), y: 4, z: 4, core: 2. Of those that a mesh axis runs over, the one named last changes fastest.
Arguments:
- layer_input: bfloat16 [2, 8192, 1024], P('fsdp', 'ctx'), may hold values from -6 to 6
- positions: int32 [2, 8192], P('fsdp', 'ctx'), may hold values from 0 to 16383, as said below
- routes: int32 [2, 8192, 8], P('fsdp', 'ctx'), may hold values from 0 to 31, all different within a row; in each aligned block of 128 rows (0 to 127, 128 to 255, ..., all dimensions but the last counted through in order) at most 48 rows name the same one
- attn_gain: float32 [1024], replicated, may hold values from 0.1 to 1.9
- w_query: bfloat16 [1024, 1024], P(('ctx', 'fsdp')), may hold values from -0.1875 to 0.1875
- w_key: bfloat16 [1024, 512], P(('ctx', 'fsdp')), may hold values from -0.1875 to 0.1875
- w_value: bfloat16 [1024, 512], P(('ctx', 'fsdp')), may hold values from -0.1875 to 0.1875
- query_gain: float32 [64], replicated, may hold values from 0.1 to 1.9
- key_gain: float32 [64], replicated, may hold values from 0.1 to 1.9
- w_output: bfloat16 [1024, 1024], P(('ctx', 'fsdp')), may hold values from -6 to 6
- ffn_gain: float32 [1024], replicated, may hold values from 0.1 to 1.9
- w_router: bfloat16 [1024, 32], P(('ctx', 'fsdp')), may hold values from -0.09375 to 0.09375
- w_gate: bfloat16 [64, 1024, 256], P('ctx', None, 'fsdp'), may hold values from -0.1875 to 0.1875
- w_up: bfloat16 [64, 1024, 256], P('ctx', None, 'fsdp'), may hold values from -0.1875 to 0.1875
- w_down: bfloat16 [64, 256, 1024], P('ctx', 'fsdp'), may hold values from -4 to 4
- cotangent: bfloat16 [2, 8192, 1024], P('fsdp', 'ctx'), may hold values from -6 to 6
Outputs:
- layer_output: bfloat16 [2, 8192, 1024], P('fsdp', 'ctx')
- grad_input: float32 [2, 8192, 1024], P('fsdp', 'ctx')
- grad_attn_gain: float32 [1024], P(('ctx', 'fsdp'))
- grad_query: float32 [1024, 1024], P(('ctx', 'fsdp'))
- grad_key: float32 [1024, 512], P(('ctx', 'fsdp'))
- grad_value: float32 [1024, 512], P(('ctx', 'fsdp'))
- grad_query_gain: float32 [64], replicated
- grad_key_gain: float32 [64], replicated
- grad_output: float32 [1024, 1024], P(('ctx', 'fsdp'))
- grad_ffn_gain: float32 [1024], P(('ctx', 'fsdp'))
- grad_router: float32 [1024, 32], P(('ctx', 'fsdp'))
- grad_gate: float32 [64, 1024, 256], P('ctx', None, 'fsdp')
- grad_up: float32 [64, 1024, 256], P('ctx', None, 'fsdp')
- grad_down: float32 [64, 256, 1024], P('ctx', 'fsdp')
The draws below stay inside these ranges and needn't reach their ends.
Inputs may be any that keep to these rules, and one draw needn't show every extreme that they name: Within each sequence positions strictly increase; the first is 0 and the last is 16383. `routes`: A token's 8 experts differ. Among the 128 tokens of one device, no expert is named by more than 48 of them.
All inputs are finite; a program needn't handle non-finite values.
Results may differ from the reference program's by a relative error of at most 0.023.
Values may be sent and summed in bfloat16 or wider, within the bound.
A program may use at most 256 MiB of HBM per device.

```python
import math
import jax
import jax.numpy as jnp
import numpy as np
from jax import lax

D = 1024
HEADS = 16
KV_HEADS = 8
HD = 64
FF = 512
TOP = 8
TOK_DEV = 128
LENGTH = 8192
BATCH = 2
TOKENS = 16384
EXPERTS = 32
CAP = 48


def draw_positions(key, part):
    key = jax.random.fold_in(key, 7)
    extra = jax.random.randint(key, (BATCH, LENGTH), 0, 2)
    places = jnp.arange(LENGTH, dtype=jnp.int32)[None, :]
    extra = jnp.where(places == 0, 0, jnp.where(places == LENGTH - 1, 1, extra))
    return (2 * places + extra).astype(jnp.int32)


def steps_of(stream_key, dims, split, least, largest):
    def one(position, shards_of):
        heights = jax.random.uniform(jax.random.fold_in(jax.random.fold_in(stream_key, 6), position), (shards_of,), jnp.float32, least / len(split), largest / len(split))
        return jnp.repeat(jnp.exp(heights), dims[position] // shards_of).reshape((-1,) + (1,) * (len(dims) - position - 1))

    gain = one(*split[0])
    for cut in split[1:]:
        gain = gain * one(*cut)
    return gain


def assign_block(rng, own, number, rows, amount, top, most, lean):
    ranking = jax.random.permutation(rng, amount)
    crowded, ordinary = shares(amount, rows * top, most, lean, True), shares(amount, rows * top, most, lean, False)
    places = jnp.arange(amount)

    def named(lengths, offset_by):
        used = int((lengths > 0).sum())
        fixed = max(1, used // 4)
        moved = fixed + (places - fixed + offset_by * (used - fixed)) % max(1, amount - fixed)
        return jnp.zeros((amount,), jnp.int32).at[ranking[jnp.where(places < fixed, places, moved)]].set(jnp.asarray(lengths, jnp.int32))

    lengths = jnp.where(number % 4 == 0, named(crowded, number // 4), named(ordinary, number - number // 4 - 1))
    mixed = jax.random.permutation(jax.random.fold_in(own, 3), amount)
    source_of, taker = mixed[0:amount // 2 * 2:2], mixed[1:amount // 2 * 2:2]
    margin = jnp.minimum(lengths[source_of] - 1, most - lengths[taker]) // 2
    margin = jnp.where((source_of == ranking[0]) | (taker == ranking[0]) | (lengths[taker] == 0), 0, jnp.maximum(margin, 0))
    moved = jax.random.randint(jax.random.fold_in(own, 4), (amount // 2,), 0, 1 << 20) % (margin + 1)
    lengths = lengths.at[source_of].add(-moved).at[taker].add(moved)
    members = jnp.searchsorted(jnp.cumsum(lengths), jnp.arange(rows * top), side="right").astype(jnp.int32)
    grid = members.reshape(top, rows).T
    grid = grid[jax.random.permutation(jax.random.fold_in(own, 1), rows)]
    offset_by = jax.random.randint(jax.random.fold_in(own, 2), (rows, 1), 0, top)
    return jnp.take_along_axis(grid, (jnp.arange(top)[None, :] + offset_by) % top, axis=1)


def shares(number_of, total, most, slope, full):
    weights = [(1 << 20) // math.isqrt(standing ** slope) + 1 for standing in range(1, number_of + 1)]
    largest = most if full else min(most, max(-(-total // number_of), total * weights[0] // sum(weights)))
    least = 1 if total - largest >= number_of - 1 else 0
    given, rest = [largest] + [least] * (number_of - 1), total - largest - least * (number_of - 1)
    while rest > 0:
        movable = [i for i in range(1, number_of) if given[i] < largest] or [i for i in range(1, number_of) if given[i] < most]
        whole, left = sum([weights[i] for i in movable]), rest
        for i in movable:
            addition = min(most - given[i], max(1, left * weights[i] // whole), rest)
            given[i] = given[i] + addition
            rest = rest - addition
    return np.array(given)


def gaussian(stream_key, extent, width, reach, pieces=(), kind=jnp.bfloat16):
    values = width * jax.random.normal(stream_key, extent, jnp.float32)
    if pieces:
        values = values * steps_of(stream_key, extent, pieces, -0.22, 0.18)
    return jnp.clip(values, -reach, reach).astype(kind)


def setup_inputs(seed: int = 0) -> dict:
    seeds = jax.random.split(jax.random.key(seed), 17)
    layer_input = gaussian(seeds[0], (BATCH, LENGTH, D), 1.0, 6.0, ((0, 2), (1, 64)))
    positions = draw_positions(jax.random.fold_in(seeds[16], 71), 0)
    routes_keys = jax.random.split(jax.random.fold_in(seeds[2], 1), BATCH * LENGTH // TOK_DEV)
    routes_turns = jax.random.permutation(jax.random.fold_in(seeds[2], 3), BATCH * LENGTH // TOK_DEV)
    routes = jax.vmap(lambda own, number: assign_block(jax.random.fold_in(seeds[2], 2), own, number, TOK_DEV, EXPERTS, TOP, CAP, 1))(routes_keys, routes_turns).reshape((BATCH, LENGTH, TOP))
    attn_gain = jnp.clip(1.0 + 0.18 * jax.random.normal(seeds[3], (D,), jnp.float32), 0.1, 1.9)
    w_query = gaussian(seeds[4], (D, D), D ** -0.5, 0.1875, ((0, 128),))
    w_key = gaussian(seeds[5], (D, KV_HEADS * HD), D ** -0.5, 0.1875, ((0, 128),))
    w_value = gaussian(seeds[6], (D, KV_HEADS * HD), D ** -0.5, 0.1875, ((0, 128),))
    query_gain = jnp.clip(1.0 + 0.18 * jax.random.normal(seeds[7], (HD,), jnp.float32), 0.1, 1.9)
    key_gain = jnp.clip(1.0 + 0.18 * jax.random.normal(seeds[8], (HD,), jnp.float32), 0.1, 1.9)
    w_output = gaussian(seeds[9], (D, D), (max(1, 3 * D // LENGTH)) ** -0.5, 6.0, ((0, 128),))
    ffn_gain = jnp.clip(1.0 + 0.18 * jax.random.normal(seeds[10], (D,), jnp.float32), 0.1, 1.9)
    w_router = gaussian(seeds[11], (D, EXPERTS), (4 * D) ** -0.5, 0.09375, ((0, 128),))
    w_gate = gaussian(seeds[12], (2 * EXPERTS, D, FF // 2), D ** -0.5, 0.1875, ((0, 64), (2, 2)))
    w_up = gaussian(seeds[13], (2 * EXPERTS, D, FF // 2), D ** -0.5, 0.1875, ((0, 64), (2, 2)))
    w_down = gaussian(seeds[14], (2 * EXPERTS, FF // 2, D), (max(1, FF * TOP // (2 * EXPERTS * EXPERTS))) ** -0.5, 4.0, ((0, 64), (1, 2)))
    cotangent = gaussian(seeds[15], (BATCH, LENGTH, D), 1.0, 6.0, ((0, 2), (1, 64)))
    return {"layer_input": layer_input, "positions": positions, "routes": routes, "attn_gain": attn_gain, "w_query": w_query, "w_key": w_key, "w_value": w_value, "query_gain": query_gain, "key_gain": key_gain, "w_output": w_output, "ffn_gain": ffn_gain, "w_router": w_router, "w_gate": w_gate, "w_up": w_up, "w_down": w_down, "cotangent": cotangent}


EPS = 1e-06
HIGH = lax.Precision.HIGHEST

@jax.custom_vjp
def low(v):
    return lax.optimization_barrier(v.astype(jnp.bfloat16)).astype(jnp.float32)

@jax.custom_vjp
def low_back(v):
    return v

def low_keep(v):
    return (low(v), None)

def low_pass(kept, grad):
    return (grad,)

def back_keep(v):
    return (v, None)

def back_low(kept, grad):
    return (low(grad),)
low.defvjp(low_keep, low_pass)
low_back.defvjp(back_keep, back_low)

def norm_rows(values_in):
    return values_in * lax.rsqrt(lax.optimization_barrier(jnp.mean(values_in * values_in, axis=-1, keepdims=True)) + EPS)

def rotate(vector, cosine, sine):
    half = vector.shape[-1] // 2
    first = vector[..., :half]
    second = vector[..., half:]
    return jnp.concatenate([first * cosine - second * sine, second * cosine + first * sine], axis=-1)

def rope_tables(positions):
    steps = jnp.arange(HD // 2, dtype=jnp.float32) * (2.0 / HD)
    inverse = jnp.power(50000.0, -steps)
    angles = positions.astype(jnp.float32)[..., None] * inverse
    return (jnp.cos(angles), jnp.sin(angles))

def attend(parts):
    queries, keys, values = parts
    share = HEADS // KV_HEADS
    block = math.gcd(LENGTH, 512)

    def one_block(query_block):
        raw = jnp.einsum('qjgd,kjd->jgqk', query_block, keys, precision=HIGH) * HD ** (-0.5)
        scores = low_back(raw)
        peak = lax.optimization_barrier(jnp.max(scores, axis=-1, keepdims=True))
        expo = jnp.exp(scores - peak)
        weights = expo / lax.optimization_barrier(jnp.sum(expo, axis=-1, keepdims=True))
        return jnp.einsum('jgqk,kjd->qjgd', low(weights), values, precision=HIGH)
    blocks = queries.reshape(LENGTH // block, block, KV_HEADS, share, HD)
    mixed = lax.map(jax.checkpoint(one_block), blocks)
    return mixed.reshape(LENGTH, HEADS, HD)

def reference(layer_input, positions, routes, attn_gain, w_query, w_key, w_value, query_gain, key_gain, w_output, ffn_gain, w_router, w_gate, w_up, w_down, cotangent):
    flat_routes = routes.reshape(-1).astype(jnp.int32)
    order = jnp.argsort(flat_routes, stable=True).astype(jnp.int32)
    hits = (flat_routes[:, None] == jnp.arange(EXPERTS, dtype=jnp.int32)[None, :]).astype(jnp.int32)
    counts = lax.optimization_barrier(jnp.sum(hits, axis=0)).astype(jnp.int32)
    starts = (jnp.cumsum(counts) - counts).astype(jnp.int32)
    bound = TOKENS // TOK_DEV * CAP
    padded = jnp.concatenate([order, jnp.zeros((bound,), jnp.int32)])
    picked = jax.vmap(lambda first: lax.dynamic_slice_in_dim(padded, first, bound))(starts).astype(jnp.int32)
    alive_slots = jnp.arange(bound, dtype=jnp.int32)[None, :] < counts[:, None]
    token_route = routes.reshape(TOKENS, TOP).astype(jnp.int32)
    cosine, sine = rope_tables(positions)
    cosine = cosine[:, :, None, :]
    sine = sine[:, :, None, :]
    shape = (BATCH, LENGTH, HEADS, HD)
    kv_shape = (BATCH, LENGTH, KV_HEADS, HD)

    def forward(input_f, attn_g, wq_f, wk_f, wv_f, query_g, key_g, wo_f, ffn_g, router_f, gate_f, up_f, down_f):
        gate_whole = gate_f.reshape(EXPERTS, 2, D, FF // 2).transpose(0, 2, 1, 3).reshape(EXPERTS, D, FF)
        up_whole = up_f.reshape(EXPERTS, 2, D, FF // 2).transpose(0, 2, 1, 3).reshape(EXPERTS, D, FF)
        down_whole = down_f.reshape(EXPERTS, FF, D)
        normed_in = low(norm_rows(input_f) * attn_g)
        query_raw = low_back(jnp.einsum('bld,de->ble', normed_in, wq_f, precision=HIGH))
        key_raw = low_back(jnp.einsum('bld,de->ble', normed_in, wk_f, precision=HIGH))
        values = low(low_back(jnp.einsum('bld,de->ble', normed_in, wv_f, precision=HIGH)))
        queries = low(rotate(norm_rows(query_raw.reshape(shape)) * query_g, cosine, sine))
        keys = low(rotate(norm_rows(key_raw.reshape(kv_shape)) * key_g, cosine, sine))
        mixed = lax.map(attend, (queries, keys, values.reshape(kv_shape)))
        attended = low(low_back(mixed.reshape(BATCH, LENGTH, D)))
        residual = input_f + low_back(jnp.einsum('bld,de->ble', attended, wo_f, precision=HIGH))
        normed_mid = low(norm_rows(residual) * ffn_g).reshape(TOKENS, D)
        logits = jnp.dot(normed_mid, router_f, precision=HIGH)
        peak = lax.optimization_barrier(jnp.max(logits, axis=-1, keepdims=True))
        expo = jnp.exp(logits - peak)
        router_probs = expo / lax.optimization_barrier(jnp.sum(expo, axis=-1, keepdims=True))
        gates = jnp.take_along_axis(router_probs, token_route, axis=1).reshape(-1)

        def expert(parts):
            gate_w, up_w, down_w, index, alive = parts
            expert_rows = low_back(normed_mid[index // TOP])
            gate_pre = low_back(jnp.dot(expert_rows, gate_w, precision=HIGH))
            up_pre = low_back(jnp.dot(expert_rows, up_w, precision=HIGH))
            hidden = low(gate_pre * jax.nn.sigmoid(gate_pre) * up_pre)
            result = low(low_back(jnp.dot(hidden, down_w, precision=HIGH)))
            weight = jnp.where(alive, gates[index], 0.0)
            return result * weight[:, None]
        contrib = lax.map(jax.checkpoint(expert), (gate_whole, up_whole, down_whole, picked, alive_slots))
        token_of = (picked // TOP).reshape(-1)
        mixture = jnp.zeros((TOKENS, D), jnp.float32).at[token_of].add(contrib.reshape(-1, D))
        return residual + mixture.reshape(BATCH, LENGTH, D)
    primals = tuple((item.astype(jnp.float32) for item in (layer_input, attn_gain, w_query, w_key, w_value, query_gain, key_gain, w_output, ffn_gain, w_router, w_gate, w_up, w_down)))
    result, pull = jax.vjp(forward, *primals)
    grads = pull(cotangent.astype(jnp.float32))
    return (result.astype(jnp.bfloat16), grads[0], grads[1], grads[2], grads[3], grads[4], grads[5], grads[6], grads[7], grads[8], grads[9], grads[10], grads[11], grads[12])
```

```python
import functools

import jax
import jax.numpy as jnp
from jax import lax
from jax.experimental import pallas as pl
from jax.experimental.pallas import tpu as pltpu
from jax.sharding import PartitionSpec as P

EPS = 1e-06
LOG2E = 1.4426950408889634
LN2 = 0.6931471805599453
MESH = pl.DeviceIdType.MESH
BF = jnp.bfloat16
F32 = jnp.float32
NT = (((1,), (1,)), ((), ()))
TN = (((0,), (0,)), ((), ()))
HBM = pl.BlockSpec(memory_space=pl.ANY)
VMEM = pl.BlockSpec(memory_space=pltpu.VMEM)
DMA = pltpu.SemaphoreType.DMA
STEPS = ((0, 0), (0, 1), (0, 3), (1, 0), (1, 1), (1, 3), (0, 2), (1, 2))


def dot(left, right, dims=(((1,), (0,)), ((), ()))):
    return lax.dot_general(left, right, dims, preferred_element_type=F32)


class Place:
    def __init__(self):
        ctx = lax.axis_index("ctx")
        self.f = lax.axis_index("fsdp")
        self.t = lax.rem(ctx, 8)
        self.g = lax.div(ctx, 8)
        self.core = lax.rem(ctx, 2)
        self.z = lax.rem(lax.div(ctx, 2), 4)
        self.y = lax.rem(self.g, 4)
        self.xl = lax.div(self.g, 4)
        self.chip = lax.div(ctx, 2)

    def tp(self, k):
        t = lax.rem(self.t + k, 8)
        return t, (self.g * 8 + t, self.f)

    def cp(self, k, back=False):
        a, b = STEPS[k]
        xl = lax.rem(self.xl + a, 2)
        y = lax.rem(self.y + (4 - b if back else b), 4)
        g = xl * 4 + y
        return g, (g * 8 + self.t, self.f)

    def gf(self, k):
        r = lax.rem(self.g * 2 + self.f + k, 16)
        return r, (lax.div(r, 2) * 8 + self.t, lax.rem(r, 2))

    def chips(self, k):
        a, b, c = k // 16, (k // 4) % 4, k % 4
        xl = lax.rem(self.xl + a, 2)
        y = lax.rem(self.y + b, 4)
        z = lax.rem(self.z + c, 4)
        e = (xl * 4 + y) * 4 + z
        return e, (e * 2 + self.core, self.f)

    def zpeer(self, c):
        z = lax.rem(self.z + c, 4)
        t = z * 2 + self.core
        return z, t, (self.g * 8 + t, self.f)

    def sibling(self):
        t = self.z * 2 + 1 - self.core
        return t, (self.g * 8 + t, self.f)

    def partner(self):
        return (self.g * 8 + self.t, 1 - self.f)


def greet(devices):
    sem = pltpu.get_barrier_semaphore()
    for d in devices:
        pl.semaphore_signal(sem, inc=1, device_id=d, device_id_type=MESH)
    return sem


def send(src, dst, send_sem, recv_sem, device):
    copy = pltpu.make_async_remote_copy(
        src_ref=src,
        dst_ref=dst,
        send_sem=send_sem,
        recv_sem=recv_sem,
        device_id=device,
        device_id_type=MESH,
    )
    copy.start()
    return copy


def local_copy(src, dst, sem):
    copy = pltpu.make_async_copy(src, dst, sem)
    copy.start()
    return copy


def landed(ref, sem):
    pltpu.make_async_copy(ref, ref, sem).wait()


def chips_all(p, src, dst, sends, recv):
    copies = []
    for k in range(1, 32):
        e, dev = p.chips(k)
        copies.append(send(src.at[e], dst.at[p.chip], sends.at[k], recv, dev))
    copies.append(local_copy(src.at[p.chip], dst.at[p.chip], sends.at[0]))
    return copies


def chips_done(copies, dst, recv):
    landed(dst.at[pl.ds(0, 31)], recv)
    for c in copies[:-1]:
        c.wait_send()
    copies[-1].wait()


def start_kernel(x, wp, pos, xg, wg, posg, wst, xs, xr, fs, fr, ps, pr, ws, wr, gs, gr, ls):
    p = Place()
    sem = greet([p.tp(k)[1] for k in range(1, 8)] + [p.gf(k)[1] for k in range(1, 16)])
    pl.semaphore_wait(sem, 22)
    tsib, sib = p.sibling()
    outs = []
    zs = []
    for c in (1, 3, 2):
        _, _, dev = p.zpeer(c)
        zs.append(send(x, xg.at[p.t], xs.at[c], xr.at[c], dev))
    for k in range(1, 8):
        t, dev = p.tp(k)
        outs.append(send(wp.at[t], wst.at[p.t], ws.at[k], wr, dev))
    outs.append(send(x, xg.at[p.t], xs.at[0], xr.at[0], sib))
    for k in range(1, 8):
        t, dev = p.tp(k)
        outs.append(send(pos, posg.at[p.t], ps.at[k], pr, dev))
    own = [
        local_copy(x, xg.at[p.t], ls.at[0]),
        local_copy(pos, posg.at[p.t], ls.at[1]),
        local_copy(wp.at[p.t], wst.at[p.t], ls.at[2]),
    ]
    own[2].wait()
    landed(wst.at[pl.ds(0, 7)], wr)
    me = p.g * 2 + p.f
    own.append(local_copy(wst, wg.at[me], ls.at[3]))
    for k in range(1, 16):
        _, dev = p.gf(k)
        outs.append(send(wst, wg.at[me], gs.at[k], gr, dev))
    fwd = []
    for c in (1, 3, 2):
        landed(xg.at[0], xr.at[c])
        z = lax.rem(p.z + 4 - c, 4)
        block = xg.at[z * 2 + p.core]
        fwd.append(send(block, block, fs.at[c], fr.at[c], sib))
    landed(posg.at[pl.ds(0, 7)], pr)
    landed(wg.at[pl.ds(0, 15)], gr)
    landed(xg.at[0], xr.at[0])
    for c in (1, 3, 2):
        landed(xg.at[0], fr.at[c])
    for c in zs + outs + fwd:
        c.wait_send()
    for c in (own[0], own[1], own[3]):
        c.wait()


def start(x, wp, pos):
    return pl.pallas_call(
        start_kernel,
        out_shape=(
            jax.ShapeDtypeStruct((8, 128, 1024), BF),
            jax.ShapeDtypeStruct((16, 8, 16, 128), BF),
            jax.ShapeDtypeStruct((8, 8, 128), F32),
        ),
        in_specs=[HBM] * 3,
        out_specs=(HBM,) * 3,
        scratch_shapes=[
            pltpu.VMEM((8, 16, 128), BF),
            DMA((4,)),
            DMA((4,)),
            DMA((4,)),
            DMA((4,)),
            DMA((8,)),
            DMA,
            DMA((8,)),
            DMA,
            DMA((16,)),
            DMA,
            DMA((4,)),
        ],
        compiler_params=pltpu.CompilerParams(collective_id=0, has_side_effects=True),
        name="start",
    )(x, wp, pos)


QB = 256


def forward_kernel(
    qp,
    kv,
    cot,
    eg,
    eu,
    ed,
    wop,
    attg,
    o,
    lse,
    kvall,
    cotr,
    egr,
    eur,
    edr,
    wog,
    att,
    acc,
    lsum,
    wst,
    ks,
    kr,
    as_,
    ar,
    cs,
    cr,
    es,
    er,
    fs,
    fr,
    ws,
    wr,
    gs,
    gr,
    ls,
):
    p = Place()
    tsib, sib = p.sibling()
    sem = greet(
        [p.chips(k)[1] for k in range(1, 32)]
        + [p.tp(k)[1] for k in range(1, 8)]
        + [p.gf(k)[1] for k in range(1, 16)]
    )
    pl.semaphore_wait(sem, 31 + 7 + 15)
    outs = []
    for k in range(1, 8):
        _, dev = p.cp(k)
        outs.append(send(kv, kvall.at[k], ks.at[k], kr.at[k], dev))
    own_kv = local_copy(kv, kvall.at[0], kr.at[0])
    for k in range(1, 8):
        _, dev = p.tp(k)
        outs.append(send(wop, wst.at[p.t], ws.at[k], wr, dev))
    own_wo = local_copy(wop, wst.at[p.t], ls.at[0])
    mine = p.core * 2 + p.f
    other = p.core * 2 + 1 - p.f
    own_e = []
    pieces = ((eg, egr), (eu, eur), (ed, edr))
    for i, (src, dst) in enumerate(pieces):
        outs.append(send(src, dst.at[mine], es.at[i], er.at[i], p.partner()))
        outs.append(send(src, dst.at[mine], es.at[3 + i], er.at[3 + i], sib))
        own_e.append(local_copy(src, dst.at[mine], ls.at[1 + i]))
    cots = chips_all(p, cot, cotr, cs, cr)

    acc[...] = jnp.zeros_like(acc)
    lsum[...] = jnp.zeros_like(lsum)

    def slot(k, _):
        landed(kvall.at[0], kr.at[k])
        kvb = kvall[k]

        def block(i, _):
            rows = pl.ds(pl.multiple_of(i * QB, QB), QB)
            s = dot(qp[rows, :], kvb, NT)
            e = jnp.exp2(s)
            part = e[:, 0:128]
            for j in range(1, 8):
                part = part + e[:, j * 128 : (j + 1) * 128]
            lsum[rows, :] += part
            acc[rows, :] += dot(e.astype(BF), kvb)
            return 0

        lax.fori_loop(0, 2048 // QB, block, 0)
        return 0

    lax.fori_loop(0, 2, slot, 0)
    own_wo.wait()
    landed(wst.at[pl.ds(0, 7)], wr)
    me = p.g * 2 + p.f
    own_wg = local_copy(wst, wog.at[me], ls.at[4])
    for k in range(1, 16):
        _, dev = p.gf(k)
        outs.append(send(wst, wog.at[me], gs.at[k], gr, dev))
    lax.fori_loop(2, 6, slot, 0)
    for i, (_, dst) in enumerate(pieces):
        landed(dst.at[0], er.at[i])
        outs.append(send(dst.at[other], dst.at[other], fs.at[i], fr.at[i], sib))
    lax.fori_loop(6, 8, slot, 0)

    lane = lax.broadcasted_iota(jnp.int32, (128, 128), 1)
    ones = jnp.ones((8, 128), F32)
    for t in range(8):
        parts = []
        for h in range(2):
            rows = pl.ds(h * 1024 + t * 128, 128)
            total = jnp.sum(lsum[rows, :], axis=1, keepdims=True)
            parts.append(acc[rows, :] / total)
        whole = jnp.where(lane < 64, pltpu.roll(parts[0], 64, 1), parts[1])
        o[pl.ds(t * 128, 128), :] = whole
        att[t] = whole.astype(BF)
    for k in range(1, 8):
        t, dev = p.tp(k)
        outs.append(send(att.at[t], attg.at[p.t], as_.at[k], ar, dev))
    own_att = local_copy(att.at[p.t], attg.at[p.t], ls.at[5])
    for h in range(2):
        rows = lax.dot_general(
            ones,
            lsum[pl.ds(h * 1024, 1024), :],
            NT,
            precision=lax.Precision.HIGHEST,
            preferred_element_type=F32,
        )
        lse[h] = jnp.log2(rows)

    landed(attg.at[pl.ds(0, 7)], ar)
    landed(wog.at[pl.ds(0, 15)], gr)
    for i, (_, dst) in enumerate(pieces):
        landed(dst.at[0], er.at[3 + i])
        landed(dst.at[0], fr.at[i])
    chips_done(cots, cotr, cr)
    for c in outs:
        c.wait_send()
    for c in own_e + [own_wg, own_att]:
        c.wait()


def forward(qp, kv, cot, eg, eu, ed, wop):
    return pl.pallas_call(
        forward_kernel,
        out_shape=(
            jax.ShapeDtypeStruct((8, 128, 128), BF),
            jax.ShapeDtypeStruct((1024, 128), F32),
            jax.ShapeDtypeStruct((2, 8, 1024), F32),
            jax.ShapeDtypeStruct((8, 1024, 128), BF),
            jax.ShapeDtypeStruct((32, 48, 1024), BF),
            jax.ShapeDtypeStruct((4, 1024, 128), BF),
            jax.ShapeDtypeStruct((4, 1024, 128), BF),
            jax.ShapeDtypeStruct((4, 128, 1024), BF),
            jax.ShapeDtypeStruct((16, 8, 80, 128), BF),
        ),
        in_specs=[VMEM, HBM, HBM, HBM, HBM, HBM, HBM],
        out_specs=(HBM, VMEM, VMEM, VMEM, HBM, HBM, HBM, HBM, HBM),
        scratch_shapes=[
            pltpu.VMEM((8, 128, 128), BF),
            pltpu.VMEM((2048, 128), F32),
            pltpu.VMEM((2048, 128), F32),
            pltpu.VMEM((8, 80, 128), BF),
            DMA((8,)),
            DMA((8,)),
            DMA((8,)),
            DMA,
            DMA((32,)),
            DMA,
            DMA((6,)),
            DMA((6,)),
            DMA((3,)),
            DMA((3,)),
            DMA((8,)),
            DMA,
            DMA((16,)),
            DMA,
            DMA((6,)),
        ],
        compiler_params=pltpu.CompilerParams(
            collective_id=1, has_side_effects=True, vmem_limit_bytes=48 * 2**20
        ),
        name="attention_forward",
    )(qp, kv, cot, eg, eu, ed, wop)


def rows_kernel(src, dst, ss, rs):
    p = Place()
    sem = greet([p.chips(k)[1] for k in range(1, 32)])
    pl.semaphore_wait(sem, 31)
    chips_done(chips_all(p, src, dst, ss, rs), dst, rs)


def rows_out(src, number, name):
    return pl.pallas_call(
        rows_kernel,
        out_shape=jax.ShapeDtypeStruct(src.shape, src.dtype),
        in_specs=[HBM],
        out_specs=HBM,
        scratch_shapes=[DMA((32,)), DMA],
        compiler_params=pltpu.CompilerParams(collective_id=number, has_side_effects=True),
        name=name,
    )(src)


KB = 256
GB = 512


def backward_kernel(
    qp,
    kvall,
    o,
    lse,
    gat,
    gb,
    ysend,
    dw,
    dqt,
    dkv,
    gbg,
    yret,
    dwr,
    gatr,
    dop,
    delta,
    acc,
    dks,
    dkr,
    as_,
    ar,
    bs,
    br,
    ys,
    yr,
    es,
    er,
    ss,
    sr,
    ls,
):
    p = Place()
    tsib, sib = p.sibling()
    sem = greet(
        [p.chips(k)[1] for k in range(1, 32)]
        + [p.tp(k)[1] for k in range(1, 8)]
        + [p.partner(), (p.g * 8 + tsib, 1 - p.f)]
    )
    pl.semaphore_wait(sem, 31 + 7 + 2)
    outs = []
    for k in range(1, 8):
        t, dev = p.tp(k)
        outs.append(send(gat.at[t], gatr.at[p.t], as_.at[k], ar, dev))
    own = [local_copy(gat.at[p.t], gatr.at[p.t], ls.at[0])]
    own[0].wait()
    landed(gatr.at[pl.ds(0, 7)], ar)
    for k in range(1, 8):
        _, dev = p.tp(k)
        outs.append(send(gb, gbg.at[p.t], bs.at[k], br, dev))
    own_gb = local_copy(gb, gbg.at[p.t], ls.at[1])
    mine = p.core * 2 + p.f
    owners = (
        (p.core * 2 + 1 - p.f, p.partner()),
        ((1 - p.core) * 2 + p.f, sib),
        ((1 - p.core) * 2 + 1 - p.f, (p.g * 8 + tsib, 1 - p.f)),
    )
    for i, (q, dev) in enumerate(owners):
        outs.append(send(dw.at[q], dwr.at[1 + i], es.at[i], er.at[i], dev))
    own_dw = local_copy(dw.at[mine], dwr.at[0], ls.at[2])
    yrows = chips_all(p, ysend, yret, ys, yr)

    lane = lax.broadcasted_iota(jnp.int32, (128, 128), 1)
    ones = jnp.ones((8, 128), F32)
    for t in range(8):
        both = gatr[t].astype(F32)
        rows = pl.ds(t * 128, 128)
        first = jnp.where(lane < 64, 0.0, pltpu.roll(both, 64, 1))
        second = jnp.where(lane < 64, 0.0, both)
        dop[rows, :] = first.astype(BF)
        dop[pl.ds(1024 + t * 128, 128), :] = second.astype(BF)
        prod = both * o[rows, :]
        for h in range(2):
            part = jnp.where((lane < 64) == (h == 0), prod, 0.0)
            delta[h, :, rows] = lax.dot_general(
                ones, part, NT, precision=lax.Precision.HIGHEST, preferred_element_type=F32
            )
    dqt[...] = jnp.zeros_like(dqt)

    def slot(s, carry):
        def keys(j, _):
            krows = pl.ds(pl.multiple_of(j * KB, KB), KB)
            kvb = kvall[s, krows, :]
            kt = kvb.T[:64, :]
            total = jnp.zeros((KB, 128), F32)
            for i in range(2048 // GB):
                rows = pl.ds(i * GB, GB)
                h, cols = i * GB // 1024, pl.ds(i * GB % 1024, GB)
                q = qp[rows, :]
                d = dop[rows, :]
                w = jnp.exp2(dot(kvb, q, NT) - lse[h, 0:1, cols])
                ds = (w * (dot(kvb, d, NT) - delta[h, 0:1, cols])).astype(BF)
                total = total + dot(w.astype(BF), d) + dot(ds, q)
                dqt[:, rows] += dot(kt, ds)
            acc[krows, :] = total
            return 0

        lax.fori_loop(0, 1024 // KB, keys, 0)

    for k in (7, 6, 5, 4, 3, 2, 1):
        slot(k, 0)
        dks[k] = acc[...].astype(BF)
        _, dev = p.cp(k, back=True)
        outs.append(send(dks.at[k], dkr.at[k], ss.at[k], sr.at[k], dev))
    slot(0, 0)
    whole = acc[...]
    for k in range(1, 8):
        landed(dkr.at[0], sr.at[k])
        whole = whole + dkr[k].astype(F32)
    dkv[...] = whole

    landed(gbg.at[pl.ds(0, 7)], br)
    for i in range(3):
        landed(dwr.at[0], er.at[i])
    chips_done(yrows, yret, yr)
    for c in outs:
        c.wait_send()
    own_gb.wait()
    own_dw.wait()


def backward(qp, kvall, o, lse, gat, gb, ysend, dw):
    return pl.pallas_call(
        backward_kernel,
        out_shape=(
            jax.ShapeDtypeStruct((64, 2048), F32),
            jax.ShapeDtypeStruct((1024, 128), F32),
            jax.ShapeDtypeStruct((8, 128, 1024), BF),
            jax.ShapeDtypeStruct((32, 48, 1024), BF),
            jax.ShapeDtypeStruct(dw.shape, BF),
        ),
        in_specs=[VMEM, VMEM, VMEM, VMEM, HBM, HBM, HBM, HBM],
        out_specs=(VMEM, VMEM, HBM, HBM, HBM),
        scratch_shapes=[
            pltpu.VMEM((8, 128, 128), BF),
            pltpu.VMEM((2048, 128), BF),
            pltpu.VMEM((2, 8, 1024), F32),
            pltpu.VMEM((1024, 128), F32),
            pltpu.VMEM((8, 1024, 128), BF),
            pltpu.VMEM((8, 1024, 128), BF),
            DMA((8,)),
            DMA,
            DMA((8,)),
            DMA,
            DMA((32,)),
            DMA,
            DMA((3,)),
            DMA((3,)),
            DMA((8,)),
            DMA((8,)),
            DMA((3,)),
        ],
        compiler_params=pltpu.CompilerParams(
            collective_id=4, has_side_effects=True, vmem_limit_bytes=56 * 2**20
        ),
        name="attention_backward",
    )(qp, kvall, o, lse, gat, gb, ysend, dw)


def final_kernel(
    dx,
    dwm,
    dwo,
    dxs,
    d2r,
    dwor,
    sibr,
    zsend,
    zr,
    dwr,
    d2s,
    d2l,
    ss,
    sr,
    zs,
    zrs,
    ws,
    wrs,
    ts,
    trs,
    os_,
    ors,
    ls,
):
    p = Place()
    tsib, sib = p.sibling()
    sem = greet([p.tp(k)[1] for k in range(1, 8)] + [p.gf(k)[1] for k in range(1, 16)])
    self_in = p.g == p.t
    for q in range(8):
        for f in range(2):
            to = (q * 8 + p.g, f)

            @pl.when(jnp.logical_not(jnp.logical_and(self_in, jnp.logical_and(q == p.g, f == p.f))))
            def _():
                pl.semaphore_signal(sem, inc=1, device_id=to, device_id_type=MESH)

    pl.semaphore_wait(sem, 7 + 15 + 16 - jnp.where(self_in, 1, 0))
    outs = []
    for c in (1, 2, 3, 0):
        z = lax.rem(p.z + c, 4)
        outs.append(send(dx.at[1 - p.core, z], sibr.at[z], ss.at[c], sr.at[c], sib))
    me = p.g * 2 + p.f
    for k in range(1, 16):
        r, dev = p.gf(k)
        outs.append(send(dwm.at[r], dwr.at[me], ws.at[k], wrs, dev))
    own_dw = local_copy(dwm.at[me], dwr.at[me], ls.at[0])
    for q in range(8):
        for f in range(2):
            to = (p.t * 8 + q, f)
            is_self = jnp.logical_and(self_in, jnp.logical_and(q == p.t, f == p.f))
            src, dst = dwo.at[q * 2 + f], dwor.at[p.g * 2 + p.f]

            @pl.when(jnp.logical_not(is_self))
            def _():
                send(src, dst, os_.at[q * 2 + f], ors.at[p.g * 2 + p.f], to)

            @pl.when(is_self)
            def _():
                local_copy(src, dst, ls.at[1])

    for c in (1, 3, 2):
        z, _, dev = p.zpeer(c)
        landed(sibr.at[0], sr.at[c])
        zsend[c] = (dx[p.core, z].astype(F32) + sibr[z].astype(F32)).astype(BF)
        outs.append(send(zsend.at[c], zr.at[c], zs.at[c], zrs.at[c], dev))
    landed(sibr.at[0], sr.at[0])
    whole = dx[p.core, p.z].astype(F32) + sibr[p.z].astype(F32)

    own_dw.wait()
    landed(dwr.at[pl.ds(0, 15)], wrs)
    total = dwr[0].astype(F32)
    for r in range(1, 16):
        total = total + dwr[r].astype(F32)
    for t in range(8):
        d2s[t, 0:8, :] = total[t * 8 : (t + 1) * 8, :]
        d2s[t, 8:16, :] = total[64:72, :]
    for k in range(1, 8):
        t, dev = p.tp(k)
        outs.append(send(d2s.at[t], d2l.at[p.t], ts.at[k], trs, dev))
    own_d2 = local_copy(d2s.at[p.t], d2l.at[p.t], ls.at[2])
    for c in (1, 3, 2):
        landed(zr.at[0], zrs.at[c])
        whole = whole + zr[c].astype(F32)
    dxs[...] = whole
    for q in range(8):
        for f in range(2):
            is_self = jnp.logical_and(self_in, jnp.logical_and(q == p.t, f == p.f))
            src, dst = dwo.at[q * 2 + f], dwor.at[p.g * 2 + p.f]

            @pl.when(jnp.logical_not(is_self))
            def _():
                landed(src, os_.at[q * 2 + f])

            @pl.when(is_self)
            def _():
                landed(dst, ls.at[1])

            from_self = jnp.logical_and(self_in, jnp.logical_and(q == p.g, f == p.f))

            @pl.when(jnp.logical_not(from_self))
            def _():
                landed(dwor.at[0], ors.at[q * 2 + f])

    own_d2.wait()
    landed(d2l.at[pl.ds(0, 7)], trs)
    d2r[...] = d2l[...]
    for c in outs:
        c.wait_send()


def final(dx, dwm, dwo):
    return pl.pallas_call(
        final_kernel,
        out_shape=(
            jax.ShapeDtypeStruct((128, 1024), F32),
            jax.ShapeDtypeStruct((8, 16, 384), F32),
            jax.ShapeDtypeStruct((16, 8, 1024), F32),
        ),
        in_specs=[VMEM, HBM, HBM],
        out_specs=(VMEM, VMEM, HBM),
        scratch_shapes=[
            pltpu.VMEM((4, 128, 1024), BF),
            pltpu.VMEM((4, 128, 1024), BF),
            pltpu.VMEM((4, 128, 1024), BF),
            pltpu.VMEM((16, 80, 384), BF),
            pltpu.VMEM((8, 16, 384), F32),
            pltpu.VMEM((8, 16, 384), F32),
            DMA((4,)),
            DMA((4,)),
            DMA((4,)),
            DMA((4,)),
            DMA((16,)),
            DMA,
            DMA((8,)),
            DMA,
            DMA((16,)),
            DMA((16,)),
            DMA((3,)),
        ],
        compiler_params=pltpu.CompilerParams(
            collective_id=5, has_side_effects=True, vmem_limit_bytes=32 * 2**20
        ),
        name="last_sums",
    )(dx, dwm, dwo)


def norm_stats(v):
    factor = lax.rsqrt(jnp.mean(v * v, axis=-1, keepdims=True) + EPS)
    return v * factor, factor


def norm_back(grad_normed, normed, factor):
    return factor * (grad_normed - normed * jnp.mean(grad_normed * normed, axis=-1, keepdims=True))


def rotate(v, cosine, sine):
    first, second = jnp.split(v, 2, axis=-1)
    return jnp.concatenate(
        [first * cosine - second * sine, second * cosine + first * sine], axis=-1
    )


def local(
    layer_input,
    positions,
    routes,
    attn_gain,
    w_query,
    w_key,
    w_value,
    query_gain,
    key_gain,
    w_output,
    ffn_gain,
    w_router,
    w_gate,
    w_up,
    w_down,
    cotangent,
):
    x = layer_input[0]
    cot = cotangent[0]
    expert = lax.div(lax.axis_index("ctx"), 2)

    wq = w_query.reshape(8, 8, 128).transpose(1, 0, 2)
    wk = w_key.reshape(8, 8, 64).transpose(1, 0, 2)
    wv = w_value.reshape(8, 8, 64).transpose(1, 0, 2)
    wp = jnp.concatenate([wq, jnp.concatenate([wk, wv], axis=2)], axis=1)
    pos = jnp.broadcast_to(positions.astype(F32), (8, 128))
    xg, wg, posg = start(x, wp, pos)

    experts = jnp.arange(32, dtype=jnp.int32)
    chosen = routes[0][:, :, None] == experts[None, None, :]
    hits = jnp.sum(chosen.astype(F32), axis=1)
    earlier = dot(jnp.tril(jnp.ones((128, 128), BF), -1), hits.astype(BF))
    place = jnp.where(hits > 0, earlier, -1.0)
    token_slots = (
        (place[:, :, None] == jnp.arange(48, dtype=F32)[None, None, :])
        .astype(BF)
        .reshape(128, 32 * 48)
    )
    cot_out = dot(token_slots, cot, TN).astype(BF).reshape(32, 48, 1024)

    xf = xg.reshape(1024, 1024).astype(F32)
    normed_a, factor_a = norm_stats(xf)
    normed_in = (normed_a * attn_gain).astype(BF)
    wqkv = (
        wg.reshape(8, 2, 8, 2, 8, 128).transpose(0, 2, 1, 4, 3, 5).reshape(1024, 256)
    )
    raw = dot(normed_in, wqkv)
    steps = jnp.arange(32, dtype=F32) * (2.0 / 64)
    inverse = jnp.power(50000.0, -steps)
    angles = posg[:, 0, :].reshape(1024, 1) * inverse
    cosine, sine = jnp.cos(angles), jnp.sin(angles)
    normed_q, factor_q = norm_stats(raw[:, :128].reshape(1024, 2, 64))
    normed_k, factor_k = norm_stats(raw[:, 128:192])
    scale = 0.125 * LOG2E
    queries = (rotate(normed_q * query_gain, cosine[:, None], sine[:, None]) * scale).astype(BF)
    keys = rotate(normed_k * key_gain, cosine, sine).astype(BF)
    values = raw[:, 192:].astype(BF)
    kv = jnp.concatenate([keys, values], axis=1)
    qp = jnp.pad(queries.transpose(1, 0, 2), ((0, 0), (0, 0), (0, 64))).reshape(2048, 128)

    wop = jnp.concatenate(
        [w_output.reshape(64, 128), jnp.pad(w_router, ((0, 8), (0, 96)))], axis=0
    )
    attg, o, lse, kvall, cot_rows, egr, eur, edr, wog = forward(
        qp, kv, cot_out, w_gate[0], w_up[0], w_down[0], wop
    )

    wog = wog.reshape(8, 2, 8, 80, 128).transpose(0, 2, 1, 3, 4)
    wo = wog[:, :, :, :64].reshape(1024, 1024)
    wr = wog[:, :, :, 64:72, :32].reshape(1024, 32)
    attended = attg.transpose(1, 0, 2).reshape(128, 1024)
    residual = x.astype(F32) + dot(attended, wo)
    normed_m, factor_m = norm_stats(residual)
    normed_mid = (normed_m * ffn_gain).astype(BF)
    outgoing = dot(token_slots, normed_mid, TN).astype(BF).reshape(32, 48, 1024)
    rows = rows_out(outgoing, 2, "rows_out").reshape(1536, 1024)

    grads = cot_rows.reshape(1536, 1024)
    gate_w = egr.transpose(1, 0, 2).reshape(1024, 512)
    up_w = eur.transpose(1, 0, 2).reshape(1024, 512)
    down_w = edr.reshape(512, 1024)
    grad_hidden0 = dot(grads, down_w, NT)
    gate_pre = dot(rows, gate_w)
    up_pre = dot(rows, up_w)
    logits = dot(rows, wr)
    expo = jnp.exp(logits - jnp.max(logits, axis=1, keepdims=True))
    probs = expo / jnp.sum(expo, axis=1, keepdims=True)
    here = (experts == expert).astype(F32)[None, :]
    gate = jnp.sum(probs * here, axis=1, keepdims=True)
    sig = jax.nn.sigmoid(gate_pre)
    activated = gate_pre * sig
    hidden = activated * up_pre
    grad_gate_w = jnp.sum(hidden * grad_hidden0, axis=1, keepdims=True)
    gated_hidden = (gate * hidden).astype(BF)
    grad_hidden = gate * grad_hidden0
    grad_gate_pre = (grad_hidden * up_pre * sig * (1.0 + gate_pre * (1.0 - sig))).astype(BF)
    grad_up_pre = (grad_hidden * activated).astype(BF)
    grad_logits = (grad_gate_w * gate * (here - probs)).astype(BF)
    grad_in = (
        dot(grad_gate_pre, gate_w, NT) + dot(grad_up_pre, up_w, NT) + dot(grad_logits, wr, NT)
    ).astype(BF)
    back = rows_out(grad_in.reshape(32, 48, 1024), 3, "rows_back").reshape(1536, 1024)
    mixed = dot(gated_hidden, down_w).astype(BF).reshape(32, 48, 1024)
    grad_gate = dot(rows, grad_gate_pre, TN).astype(BF).reshape(1024, 4, 128).transpose(1, 0, 2)
    grad_up = dot(rows, grad_up_pre, TN).astype(BF).reshape(1024, 4, 128).transpose(1, 0, 2)
    grad_down = dot(gated_hidden, grads, TN).astype(BF).reshape(4, 1024, 128)
    dw = jnp.stack([grad_gate, grad_up, grad_down], axis=1)
    grad_router = dot(rows, grad_logits, TN)

    grad_out = cot.astype(F32)
    grad_mid = dot(token_slots, back)
    grad_ffn = jnp.sum(grad_mid * normed_m, axis=0)
    grad_residual = grad_out + norm_back(grad_mid * ffn_gain, normed_m, factor_m)
    grad_branch = grad_residual.astype(BF)
    grad_attended = dot(grad_branch, wo, NT).astype(BF)
    gat = grad_attended.reshape(128, 8, 128).transpose(1, 0, 2)
    dqt, dkv, gbg, yret, dwr = backward(qp, kvall, o, lse, gat, grad_branch, mixed, dw)

    layer_output = residual + dot(token_slots, yret.reshape(1536, 1024))
    dws = jnp.sum(dwr.astype(F32), axis=0)

    dq = dqt.reshape(64, 2, 1024).transpose(2, 1, 0) * 0.125
    dk = dkv[:, :64] * LN2
    dqn = rotate(dq, cosine[:, None], -sine[:, None])
    dkn = rotate(dk, cosine, -sine)
    query_gain_part = jnp.sum(dqn * normed_q, axis=(0, 1))
    key_gain_part = jnp.sum(dkn * normed_k, axis=0)
    dq_raw = norm_back(dqn * query_gain, normed_q, factor_q).reshape(1024, 128)
    dk_raw = norm_back(dkn * key_gain, normed_k, factor_k)
    draw = jnp.concatenate([dq_raw, dk_raw, dkv[:, 64:]], axis=1).astype(BF)
    dwqkv = dot(normed_in, draw, TN)
    dx = dot(draw, wqkv, NT)
    attn_part = jnp.sum(dx * normed_a, axis=0)
    att_t = o.astype(BF)
    dwo = dot(att_t, gbg.reshape(1024, 1024), TN).reshape(16, 8, 1024)

    misc = jnp.concatenate(
        [grad_router, grad_ffn[:, None], attn_part[:, None], jnp.zeros((1024, 94), F32)], axis=1
    )
    both = jnp.concatenate([dwqkv, misc], axis=1).astype(BF)
    both = both.reshape(8, 8, 2, 8, 384).transpose(0, 2, 1, 3, 4).reshape(16, 64, 384)
    gains = jnp.concatenate([query_gain_part, key_gain_part, jnp.zeros((256,), F32)])
    gains = jnp.broadcast_to(gains.astype(BF), (16, 16, 384))
    dwm = jnp.concatenate([both, gains], axis=1)
    dxp = dx.astype(BF).reshape(4, 2, 128, 1024).transpose(1, 0, 2, 3)
    dxs, d2, dwor = final(dxp, dwm, dwo)

    normed_own, factor_own = norm_stats(x.astype(F32))
    grad_input = grad_residual + norm_back(dxs * attn_gain, normed_own, factor_own)
    own = d2[:, :8].transpose(1, 0, 2)
    sums = jnp.sum(own[:, :, 256:], axis=1)
    gain_sums = jnp.sum(d2[:, 8, :128], axis=0)
    return (
        layer_output.astype(BF)[None],
        grad_input[None],
        sums[:, 33],
        own[:, :, :128].reshape(8, 1024),
        own[:, :, 128:192].reshape(8, 512),
        own[:, :, 192:256].reshape(8, 512),
        gain_sums[:64],
        gain_sums[64:],
        jnp.sum(dwor, axis=0),
        sums[:, 32],
        sums[:, :32],
        dws[0][None],
        dws[1][None],
        dws[2].reshape(1, 128, 1024),
    )


def solution(mesh):
    rows = P(("ctx", "fsdp"), None)
    vector = P(("ctx", "fsdp"))
    tokens = P("fsdp", "ctx", None)
    return jax.shard_map(
        local,
        mesh=mesh,
        in_specs=(
            tokens,
            P("fsdp", "ctx"),
            tokens,
            P(),
            rows,
            rows,
            rows,
            P(),
            P(),
            rows,
            P(),
            rows,
            P("ctx", None, "fsdp"),
            P("ctx", None, "fsdp"),
            P("ctx", "fsdp", None),
            tokens,
        ),
        out_specs=(
            tokens,
            tokens,
            vector,
            rows,
            rows,
            rows,
            P(),
            P(),
            rows,
            vector,
            rows,
            P("ctx", None, "fsdp"),
            P("ctx", None, "fsdp"),
            P("ctx", "fsdp", None),
        ),
        check_vma=False,
    )
```

```python
import jax
import jax.numpy as jnp
from jax import lax
from jax.experimental import pallas as pl
from jax.experimental.pallas import tpu as pltpu
from jax.sharding import PartitionSpec as P

EPS = 1e-06
LOG2E = 1.4426950408889634
LN2 = 0.6931471805599453
MESH = pl.DeviceIdType.MESH
BF = jnp.bfloat16
F32 = jnp.float32
NN = (((1,), (0,)), ((), ()))
NT = (((1,), (1,)), ((), ()))
TN = (((0,), (0,)), ((), ()))
HBM = pl.BlockSpec(memory_space=pl.ANY)
VMEM = pl.BlockSpec(memory_space=pltpu.VMEM)
DMA = pltpu.SemaphoreType.DMA
MEMBERS = ((0, 0), (1, 0), (0, 1), (0, 3), (1, 1), (1, 3), (0, 2), (1, 2))
CHIPS = tuple(((i + j // 4) % 2, (i + j) % 4, i) for j in range(8) for i in range(4))


def dot(left, right, dims=NN):
    return lax.dot_general(left, right, dims, preferred_element_type=F32)


def dot_exact(left, right, dims=NN):
    return lax.dot_general(
        left, right, dims, precision=lax.Precision.HIGHEST, preferred_element_type=F32
    )


class Place:
    def __init__(self):
        ctx = lax.axis_index("ctx")
        self.f = lax.axis_index("fsdp")
        self.t = lax.rem(ctx, 8)
        self.g = lax.div(ctx, 8)
        self.core = lax.rem(ctx, 2)
        self.z = lax.rem(lax.div(ctx, 2), 4)
        self.y = lax.rem(self.g, 4)
        self.xl = lax.div(self.g, 4)
        self.chip = lax.div(ctx, 2)

    def tp(self, k):
        t = lax.rem(self.t + k, 8)
        return t, (self.g * 8 + t, self.f)

    def cp(self, a, b):
        g = lax.rem(self.xl + a, 2) * 4 + lax.rem(self.y + b + 4, 4)
        return (g * 8 + self.t, self.f)

    def gf(self, k):
        r = lax.rem(self.g * 2 + self.f + k, 16)
        return r, (lax.div(r, 2) * 8 + self.t, lax.rem(r, 2))

    def chips(self, s, sign=1):
        a, b, c = CHIPS[s]
        xl = lax.rem(self.xl + a, 2)
        y = lax.rem(self.y + sign * b + 4, 4)
        z = lax.rem(self.z + sign * c + 4, 4)
        e = (xl * 4 + y) * 4 + z
        return e, (e * 2 + self.core, self.f)

    def zpeer(self, c):
        z = lax.rem(self.z + c + 4, 4)
        t = z * 2 + self.core
        return z, t, (self.g * 8 + t, self.f)

    def sibling(self):
        t = self.z * 2 + 1 - self.core
        return t, (self.g * 8 + t, self.f)

    def partner(self):
        return (self.g * 8 + self.t, 1 - self.f)

    def all_tp(self):
        return [self.tp(k)[1] for k in range(1, 8)]

    def all_gf(self):
        return [self.gf(k)[1] for k in range(1, 16)]

    def all_chips(self):
        return [self.chips(s)[1] for s in range(1, 32)]


def greet(devices):
    sem = pltpu.get_barrier_semaphore()
    for d in devices:
        pl.semaphore_signal(sem, inc=1, device_id=d, device_id_type=MESH)
    return sem


class Copies:
    def __init__(self, sems):
        self.sems, self.count, self.begun = sems, 0, []

    def next(self):
        self.count += 1
        return self.sems.at[self.count - 1]

    def to(self, device, src, dst, recv):
        copy = pltpu.make_async_remote_copy(
            src_ref=src,
            dst_ref=dst,
            send_sem=self.next(),
            recv_sem=recv,
            device_id=device,
            device_id_type=MESH,
        )
        copy.start()
        self.begun.append(copy.wait_send)

    def own(self, src, dst):
        copy = pltpu.make_async_copy(src, dst, self.next())
        copy.start()
        self.begun.append(copy.wait)

    def here(self, src, dst):
        copy = pltpu.make_async_copy(src, dst, self.next())
        copy.start()
        return copy

    def done(self):
        for wait in self.begun:
            wait()


def landed(ref, sem):
    pltpu.make_async_copy(ref, ref, sem).wait()


def params(number, mib):
    return pltpu.CompilerParams(
        collective_id=number, has_side_effects=True, vmem_limit_bytes=mib * 2**20
    )


def start_kernel(
    x,
    wp,
    wop,
    pos,
    routes,
    cot,
    xg,
    wg,
    wog,
    posg,
    slots_t,
    slots,
    cota,
    wst,
    cots,
    ss,
    xr,
    fr,
    pr,
    wr,
    gr,
    orr,
    cr,
):
    p = Place()
    _, sib = p.sibling()
    flat = [s for s in range(32) if CHIPS[s][2] == 0]
    sem = greet(p.all_tp() + p.all_gf() + [p.chips(s)[1] for s in flat[1:]])
    pl.semaphore_wait(sem, 7 + 15 + 7)
    me = p.g * 2 + p.f
    c = Copies(ss)
    for k in range(1, 8):
        t, dev = p.tp(k)
        c.to(dev, wp.at[t], wst.at[p.t], wr)
    for k in (1, 3, 2):
        c.to(p.zpeer(k)[2], x, xg.at[p.t], xr.at[k])
    c.to(sib, x, xg.at[p.t], xr.at[0])
    for k in range(1, 8):
        c.to(p.tp(k)[1], pos, posg.at[p.t], pr)
    first = c.here(wp.at[p.t], wst.at[p.t])
    c.own(x, xg.at[p.t])
    c.own(pos, posg.at[p.t])
    first.wait()
    landed(wst.at[pl.ds(0, 7)], wr)
    c.own(wst, wg.at[me])
    for k in range(1, 16):
        c.to(p.gf(k)[1], wst, wg.at[me], gr)
    c.own(wop, wog.at[me])
    for k in range(1, 16):
        c.to(p.gf(k)[1], wop, wog.at[me], orr)

    number = lax.broadcasted_iota(jnp.int32, (32, 128), 0)
    hits = jnp.zeros((32, 128), F32)
    for k in range(8):
        hits = hits + jnp.where(routes[k : k + 1, :] == number, 1.0, 0.0)
    row = lax.broadcasted_iota(jnp.int32, (128, 128), 0)
    col = lax.broadcasted_iota(jnp.int32, (128, 128), 1)
    before = jnp.where(row < col, 1.0, 0.0).astype(BF)
    place = jnp.where(hits > 0, dot(hits.astype(BF), before), -1.0)
    within = lax.broadcasted_iota(jnp.int32, (48, 128), 0).astype(F32)
    for e in range(32):
        block = jnp.where(place[e : e + 1, :] == within, 1.0, 0.0)
        slots_t[e * 48 : (e + 1) * 48, :] = block.astype(BF)
    for j in range(12):
        cols = slice(j * 128, (j + 1) * 128)
        slots[:, cols] = slots_t[cols, :].astype(F32).T.astype(BF)
    for j, s in enumerate(flat):
        e, dev = p.chips(s)
        mine = slots_t[pl.ds(pl.multiple_of(e * 48, 16), 48), :]
        cots[j] = dot(mine, cot[...]).astype(BF)
        if j:
            c.to(dev, cots.at[j], cota.at[j], cr)
        else:
            c.own(cots.at[0], cota.at[0])

    for k in (1, 3, 2):
        landed(xg.at[0], xr.at[k])
        block = xg.at[p.zpeer(-k)[1]]
        c.to(sib, block, block, fr.at[k])
    landed(posg.at[pl.ds(0, 7)], pr)
    landed(wg.at[pl.ds(0, 15)], gr)
    landed(wog.at[pl.ds(0, 15)], orr)
    landed(xg.at[0], xr.at[0])
    for k in (1, 3, 2):
        landed(xg.at[0], fr.at[k])
    landed(cota.at[pl.ds(0, 7)], cr)
    c.done()


def start(x, wp, wop, pos, routes, cot):
    return pl.pallas_call(
        start_kernel,
        out_shape=(
            jax.ShapeDtypeStruct((8, 128, 1024), BF),
            jax.ShapeDtypeStruct((16, 8, 16, 128), BF),
            jax.ShapeDtypeStruct((16, 80, 128), BF),
            jax.ShapeDtypeStruct((8, 8, 128), F32),
            jax.ShapeDtypeStruct((1536, 128), BF),
            jax.ShapeDtypeStruct((128, 1536), BF),
            jax.ShapeDtypeStruct((8, 48, 1024), BF),
        ),
        in_specs=[HBM] * 4 + [VMEM] * 2,
        out_specs=(HBM,) * 4 + (VMEM, VMEM, HBM),
        scratch_shapes=[
            pltpu.VMEM((8, 16, 128), BF),
            pltpu.VMEM((8, 48, 1024), BF),
            DMA((72,)),
            DMA((4,)),
            DMA((4,)),
            DMA,
            DMA,
            DMA,
            DMA,
            DMA,
        ],
        compiler_params=params(0, 24),
        name="start",
    )(x, wp, wop, pos, routes, cot)


QB = 256
UNROLL = 4


def forward_kernel(
    qp,
    kv,
    slots_t,
    cot,
    eg,
    eu,
    ed,
    wob,
    x,
    gain,
    o,
    att_t,
    lse,
    kvall,
    cotb,
    egr,
    eur,
    edr,
    wo,
    residual,
    outgoing,
    acc,
    lsum,
    cots,
    attg,
    ss,
    kr,
    ar,
    cr,
    er,
    pr,
    fr,
    wr,
    wfr,
):
    p = Place()
    _, sib = p.sibling()
    sem = greet(p.all_chips() + p.all_tp() + [p.partner()])
    pl.semaphore_wait(sem, 31 + 7 + 1)
    c = Copies(ss)
    c.to(p.cp(1, 0), kv, kvall.at[1], kr.at[1])
    for n in (2, 3, 6):
        c.to(p.cp(*MEMBERS[n]), kv, kvall.at[n], kr.at[n])
    own_kv = c.here(kv, kvall.at[0])
    for k in (1, 3, 2):
        c.to(p.zpeer(k)[2], wob, wo.at[:, p.t], wr.at[k])
    c.to(sib, wob, wo.at[:, p.t], wr.at[0])
    own_wo = c.here(wob, wo.at[:, p.t])
    mine = p.core * 2 + p.f
    other = p.core * 2 + 1 - p.f
    pieces = ((eg, egr), (eu, eur), (ed, edr))
    for i, (src, dst) in enumerate(pieces):
        c.to(p.partner(), src, dst.at[mine], pr.at[i])
        c.to(sib, src, dst.at[mine], er.at[i])
        c.own(src, dst.at[mine])
    tall = [s for s in range(32) if CHIPS[s][2] != 0]

    def cot_rows(lo, hi):
        for j in range(lo, hi):
            e, dev = p.chips(tall[j])
            rows = slots_t[pl.ds(pl.multiple_of(e * 48, 16), 48), :]
            cots[j] = dot(rows, cot[...]).astype(BF)
            c.to(dev, cots.at[j], cotb.at[j], cr)

    acc[...] = jnp.zeros_like(acc)
    lsum[...] = jnp.zeros_like(lsum)
    own_kv.wait()

    def work(n):
        kvb = kvall[n]

        def block(i, _):
            for u in range(UNROLL):
                rows = pl.ds(pl.multiple_of((i * UNROLL + u) * QB, QB), QB)
                e = jnp.exp2(dot(qp[rows, :], kvb, NT))
                part = e[:, 0:128]
                for j in range(1, 8):
                    part = part + e[:, j * 128 : (j + 1) * 128]
                lsum[rows, :] += part
                acc[rows, :] += dot(e.astype(BF), kvb)
            return 0

        lax.fori_loop(0, 2048 // QB // UNROLL, block, 0)

    def arrived(n, _):
        landed(kvall.at[0], kr.at[n])
        work(n)
        return 0

    work(0)
    landed(kvall.at[0], kr.at[1])
    for n, m in ((4, 2), (5, 3), (7, 6)):
        c.to(p.cp(*MEMBERS[m]), kvall.at[1], kvall.at[n], kr.at[n])
    cot_rows(0, 8)
    work(1)
    cot_rows(8, 16)
    lax.fori_loop(2, 4, arrived, 0)
    cot_rows(16, 24)
    for k in (1, 3, 2):
        landed(wob, wr.at[k])
        block = wo.at[:, p.zpeer(-k)[1]]
        c.to(sib, block, block, wfr.at[k])
    lax.fori_loop(4, 8, arrived, 0)

    lane = lax.broadcasted_iota(jnp.int32, (128, 128), 1)
    for t in range(8):
        parts = []
        for h in range(2):
            rows = pl.ds(h * 1024 + t * 128, 128)
            total = jnp.sum(lsum[rows, :], axis=1, keepdims=True)
            parts.append(acc[rows, :] / total)
        whole = jnp.where(lane < 64, pltpu.roll(parts[0], 64, 1), parts[1])
        o[pl.ds(t * 128, 128), :] = whole
        att_t[pl.ds(t * 128, 128), :] = whole.astype(BF)
    for k in range(1, 8):
        t, dev = p.tp(k)
        block = att_t.at[pl.ds(pl.multiple_of(t * 128, 128), 128)]
        c.to(dev, block, attg.at[p.t], ar)
    own_att = c.here(att_t.at[pl.ds(pl.multiple_of(p.t * 128, 128), 128)], attg.at[p.t])
    ones = jnp.ones((8, 128), F32)
    for h in range(2):
        lse[h] = jnp.log2(dot_exact(ones, lsum[pl.ds(h * 1024, 1024), :], NT))
    for i, (_, dst) in enumerate(pieces):
        landed(dst.at[0], pr.at[i])
        c.to(sib, dst.at[other], dst.at[other], fr.at[i])
    own_wo.wait()
    landed(wob, wr.at[0])
    for k in (1, 3, 2):
        landed(wob, wfr.at[k])
    own_att.wait()
    landed(attg.at[pl.ds(0, 7)], ar)

    att = jnp.concatenate([attg[t] for t in range(8)], axis=1)
    square = jnp.zeros((128, 1), F32)
    for j in range(4):
        cols = slice(j * 256, (j + 1) * 256)
        weights = wo[:, :, :, cols].reshape(1024, 256)
        value = x[:, cols].astype(F32) + dot(att, weights)
        residual[:, cols] = value
        square = square + jnp.sum(value * value, axis=1, keepdims=True)
    factor = lax.rsqrt(square * (1.0 / 1024) + EPS)
    normed = (residual[...] * factor * gain[...]).astype(BF)
    for j in range(4):
        rows = dot(slots_t[j * 384 : (j + 1) * 384, :], normed).astype(BF)
        outgoing[j * 8 : (j + 1) * 8] = rows.reshape(8, 48, 1024)

    for i, (_, dst) in enumerate(pieces):
        landed(dst.at[0], er.at[i])
        landed(dst.at[0], fr.at[i])
    landed(cotb, cr)
    c.done()


def forward(qp, kv, slots_t, cot, eg, eu, ed, wob, x, gain):
    return pl.pallas_call(
        forward_kernel,
        out_shape=(
            jax.ShapeDtypeStruct((1024, 128), F32),
            jax.ShapeDtypeStruct((1024, 128), BF),
            jax.ShapeDtypeStruct((2, 8, 1024), F32),
            jax.ShapeDtypeStruct((8, 1024, 128), BF),
            jax.ShapeDtypeStruct((24, 48, 1024), BF),
            jax.ShapeDtypeStruct((4, 1024, 128), BF),
            jax.ShapeDtypeStruct((4, 1024, 128), BF),
            jax.ShapeDtypeStruct((4, 128, 1024), BF),
            jax.ShapeDtypeStruct((8, 8, 16, 1152), BF),
            jax.ShapeDtypeStruct((128, 1024), F32),
            jax.ShapeDtypeStruct((32, 48, 1024), BF),
        ),
        in_specs=[VMEM, HBM, VMEM, VMEM, HBM, HBM, HBM, HBM, VMEM, VMEM],
        out_specs=(VMEM,) * 4 + (HBM,) * 4 + (VMEM,) * 3,
        scratch_shapes=[
            pltpu.VMEM((2048, 128), F32),
            pltpu.VMEM((2048, 128), F32),
            pltpu.VMEM((24, 48, 1024), BF),
            pltpu.VMEM((8, 128, 128), BF),
            DMA((64,)),
            DMA((8,)),
            DMA,
            DMA,
            DMA((3,)),
            DMA((3,)),
            DMA((3,)),
            DMA((4,)),
            DMA((4,)),
        ],
        compiler_params=params(1, 48),
        name="attention_forward",
    )(qp, kv, slots_t, cot, eg, eu, ed, wob, x, gain)


def expert_kernel(
    outgoing,
    cota,
    cotb,
    egr,
    eur,
    edr,
    wo,
    slots,
    residual,
    cot,
    gain,
    mixed,
    dwg,
    dwu,
    dwd,
    dwr,
    grad_residual,
    branch,
    gat,
    grad_ffn,
    rows,
    grads,
    wg,
    wu,
    wd,
    gh,
    gp,
    up,
    hid,
    gl,
    gin,
    back,
    sg,
    su,
    sd,
    rg,
    ru,
    rd,
    ss,
    rr,
    br,
    wr,
):
    p = Place()
    _, sib = p.sibling()
    sem = greet(p.all_chips() + [sib])
    pl.semaphore_wait(sem, 31 + 1)
    c = Copies(ss)
    for s in range(1, 32):
        e, dev = p.chips(s)
        c.to(dev, outgoing.at[e], rows.at[s], rr.at[s // 4])
    local = [c.here(outgoing.at[p.chip], rows.at[0])]
    for q in range(4):
        half = p.core if q < 2 else 1 - p.core
        src = half * 2 + q % 2
        cols = pl.ds(q * 128, 128)
        local.append(c.here(edr.at[src], wd.at[cols, :]))
        local.append(c.here(egr.at[src], wg.at[:, cols]))
        local.append(c.here(eur.at[src], wu.at[:, cols]))
    for j in range(8):
        local.append(c.here(cota.at[j], grads.at[4 * j]))
        local.append(c.here(cotb.at[pl.ds(3 * j, 3)], grads.at[pl.ds(4 * j + 1, 3)]))
    for copy in local:
        copy.wait()

    def hidden_grads(j, _):
        block = grads[pl.ds(j * 4, 4)].reshape(192, 1024)
        gh[pl.ds(pl.multiple_of(j * 192, 64), 192), :] = dot(block, wd[...], NT)
        return 0

    lax.fori_loop(0, 8, hidden_grads, 0)

    lane = lax.broadcasted_iota(jnp.int32, (192, 128), 1)
    here = jnp.where(lane == p.chip, 1.0, 0.0)
    router = wo[:, :, :, 1024:].reshape(1024, 128)

    for j in range(8):
        landed(rows.at[pl.ds(0, 4 if j else 3)], rr.at[j])
        block = rows[4 * j : 4 * j + 4].reshape(192, 1024)
        span = pl.ds(j * 192, 192)
        gate_pre = dot(block, wg[...])
        up_pre = dot(block, wu[...])
        logits = jnp.where(lane < 32, dot(block, router), -1e30)
        expo = jnp.exp(logits - jnp.max(logits, axis=1, keepdims=True))
        probs = expo / jnp.sum(expo, axis=1, keepdims=True)
        gate = jnp.sum(probs * here, axis=1, keepdims=True)
        sig = jax.nn.sigmoid(gate_pre)
        act = gate_pre * sig
        hidden = act * up_pre
        grad_hidden = gh[span, :]
        weight = jnp.sum(hidden * grad_hidden, axis=1, keepdims=True) * gate
        grad_hidden = grad_hidden * gate
        grad_gate = (grad_hidden * up_pre * sig * (1.0 + gate_pre * (1.0 - sig))).astype(BF)
        grad_up = (grad_hidden * act).astype(BF)
        grad_logits = (weight * (here - probs)).astype(BF)
        hid[span, :] = (hidden * gate).astype(BF)
        gp[span, :] = grad_gate
        up[span, :] = grad_up
        gl[span, :] = grad_logits
        total = dot(grad_gate, wg[...], NT) + dot(grad_up, wu[...], NT)
        total = total + dot(grad_logits, router, NT)
        gin[4 * j : 4 * j + 4] = total.astype(BF).reshape(4, 48, 1024)
        for s in range(4 * j, 4 * j + 4):
            if s:
                c.to(p.chips(s, -1)[1], gin.at[s], back.at[p.chip], br)
            else:
                c.own(gin.at[0], back.at[p.chip])

    for m in range(4):
        cols = slice(m * 256, (m + 1) * 256)
        left = rows[:, :, cols].reshape(1536, 256)
        for src, own, sends in ((gp, dwg, sg), (up, dwu, su)):
            value = dot(left, src[...], TN).astype(BF)
            for q in range(2):
                own[q, cols, :] = value[:, q * 128 : (q + 1) * 128]
                sends[q, cols, :] = value[:, (2 + q) * 128 : (3 + q) * 128]
        dwr[cols, :] = dot(left, gl[...], TN)
    for m in range(4):
        cols = slice(m * 256, (m + 1) * 256)
        right = grads[:, :, cols].reshape(1536, 256)
        value = dot(hid[...], right, TN).astype(BF)
        dwd[:, :, cols] = value[:256].reshape(2, 128, 256)
        sd[:, :, cols] = value[256:].reshape(2, 128, 256)
    for i, (src, dst) in enumerate(((sg, rg), (su, ru), (sd, rd))):
        c.to(sib, src, dst, wr.at[i])

    def outputs(j, _):
        block = hid[pl.ds(pl.multiple_of(j * 192, 64), 192), :]
        mixed[pl.ds(j * 4, 4)] = dot(block, wd[...]).astype(BF).reshape(4, 48, 1024)
        return 0

    lax.fori_loop(0, 8, outputs, 0)
    for i, (got, own) in enumerate(((rg, dwg), (ru, dwu), (rd, dwd))):
        landed(got, wr.at[i])
        own[...] = (own[...].astype(F32) + got[...].astype(F32)).astype(BF)

    landed(back.at[pl.ds(0, 31)], br)
    c.done()
    res = residual[...]
    factor = lax.rsqrt(jnp.mean(res * res, axis=1, keepdims=True) + EPS)
    normed = res * factor
    for j in range(4):
        cols = slice(j * 256, (j + 1) * 256)
        grad_residual[:, cols] = dot(slots[...], back[:, :, cols].reshape(1536, 256))
    grad_mid = grad_residual[...]
    part = jnp.sum(grad_mid * normed, axis=0, keepdims=True)
    grad_ffn[...] = jnp.broadcast_to(part, (8, 1024))
    g = grad_mid * gain[...]
    g = factor * (g - normed * jnp.mean(g * normed, axis=1, keepdims=True))
    g = cot[...].astype(F32) + g
    grad_residual[...] = g
    low = g.astype(BF)
    branch[...] = low
    for t in range(8):
        weights = wo[t][:, :, :1024].reshape(128, 1024)
        gat[t] = dot(low, weights, NT).astype(BF)


def expert_rows(outgoing, cota, cotb, egr, eur, edr, wo, slots, residual, cot, gain):
    shape = jax.ShapeDtypeStruct
    return pl.pallas_call(
        expert_kernel,
        out_shape=(
            shape((32, 48, 1024), BF),
            shape((2, 1024, 128), BF),
            shape((2, 1024, 128), BF),
            shape((2, 128, 1024), BF),
            shape((1024, 128), F32),
            shape((128, 1024), F32),
            shape((128, 1024), BF),
            shape((8, 128, 128), BF),
            shape((8, 1024), F32),
        ),
        in_specs=[HBM] * 6 + [VMEM] * 5,
        out_specs=(VMEM,) * 9,
        scratch_shapes=[
            pltpu.VMEM((32, 48, 1024), BF),
            pltpu.VMEM((32, 48, 1024), BF),
            pltpu.VMEM((1024, 512), BF),
            pltpu.VMEM((1024, 512), BF),
            pltpu.VMEM((512, 1024), BF),
            pltpu.VMEM((1536, 512), F32),
            pltpu.VMEM((1536, 512), BF),
            pltpu.VMEM((1536, 512), BF),
            pltpu.VMEM((1536, 512), BF),
            pltpu.VMEM((1536, 128), BF),
            pltpu.VMEM((32, 48, 1024), BF),
            pltpu.VMEM((32, 48, 1024), BF),
            pltpu.VMEM((2, 1024, 128), BF),
            pltpu.VMEM((2, 1024, 128), BF),
            pltpu.VMEM((2, 128, 1024), BF),
            pltpu.VMEM((2, 1024, 128), BF),
            pltpu.VMEM((2, 1024, 128), BF),
            pltpu.VMEM((2, 128, 1024), BF),
            DMA((96,)),
            DMA((8,)),
            DMA,
            DMA((3,)),
        ],
        compiler_params=params(2, 58),
        name="experts",
    )(outgoing, cota, cotb, egr, eur, edr, wo, slots, residual, cot, gain)


KB = 256
GB = 1024


def backward_kernel(
    qp,
    kvall,
    o,
    lse,
    att_t,
    gat,
    branch,
    mixed,
    dwg,
    dwu,
    dwd,
    dqt,
    dkv,
    yret,
    rwg,
    rwu,
    rwd,
    dwor,
    gatr,
    dop,
    delta,
    acc,
    bg,
    dwo,
    dks,
    dkr,
    ss,
    ar,
    bs,
    fs,
    yr,
    er,
    sr,
    os_,
    ors,
):
    p = Place()
    _, sib = p.sibling()
    sem = greet(p.all_chips() + p.all_tp() + [p.partner()])
    inside = p.g == p.t
    owners = []
    for q in range(8):
        for f in range(2):
            to_self = jnp.logical_and(inside, jnp.logical_and(q == p.t, f == p.f))
            owners.append((q, f, to_self))

            @pl.when(jnp.logical_not(to_self))
            def _(q=q, f=f):
                pl.semaphore_signal(sem, inc=1, device_id=(q * 8 + p.g, f), device_id_type=MESH)

    pl.semaphore_wait(sem, 31 + 7 + 1 + 16 - jnp.where(inside, 1, 0))
    c = Copies(ss)
    for k in range(1, 8):
        t, dev = p.tp(k)
        c.to(dev, gat.at[t], gatr.at[p.t], ar)
    own = c.here(gat.at[p.t], gatr.at[p.t])
    for k in (1, 3, 2):
        c.to(p.zpeer(k)[2], branch, bg.at[p.t], bs.at[k])
    c.to(sib, branch, bg.at[p.t], bs.at[0])
    own_bg = c.here(branch, bg.at[p.t])
    for i, (src, dst) in enumerate(((dwg, rwg), (dwu, rwu), (dwd, rwd))):
        c.to(p.partner(), src.at[1 - p.f], dst, er.at[i])
    for s in range(1, 32):
        c.to(p.chips(s, -1)[1], mixed.at[s], yret.at[p.chip], yr)
    c.own(mixed.at[0], yret.at[p.chip])
    own.wait()
    landed(gatr.at[pl.ds(0, 7)], ar)

    lane = lax.broadcasted_iota(jnp.int32, (128, 128), 1)
    ones = jnp.ones((8, 128), F32)
    for t in range(8):
        both = gatr[t].astype(F32)
        rows = pl.ds(t * 128, 128)
        dop[rows, :] = jnp.where(lane < 64, 0.0, pltpu.roll(both, 64, 1)).astype(BF)
        dop[pl.ds(1024 + t * 128, 128), :] = jnp.where(lane < 64, 0.0, both).astype(BF)
        prod = both * o[rows, :]
        for h in range(2):
            part = jnp.where((lane < 64) == (h == 0), prod, 0.0)
            delta[h, :, rows] = dot_exact(ones, part, NT)
    dqt[...] = jnp.zeros_like(dqt)

    def work(n):
        def keys(j, _):
            krows = pl.ds(pl.multiple_of(j * KB, KB), KB)
            kvb = kvall[n, krows, :]
            kt = kvb.T[:64, :]
            total = jnp.zeros((KB, 128), F32)
            for i in range(2048 // GB):
                rows = pl.ds(i * GB, GB)
                h, cols = i * GB // 1024, pl.ds(i * GB % 1024, GB)
                q = qp[rows, :]
                d = dop[rows, :]
                w = jnp.exp2(dot(kvb, q, NT) - lse[h, 0:1, cols])
                ds = (w * (dot(kvb, d, NT) - delta[h, 0:1, cols])).astype(BF)
                total = total + dot(w.astype(BF), d) + dot(ds, q)
                dqt[:, rows] += dot(kt, ds)
            acc[krows, :] = total
            return 0

        lax.fori_loop(0, 1024 // KB, keys, 0)

    def part(n):
        a, b = MEMBERS[n]
        work(n)
        dks[n] = acc[...].astype(BF)
        c.to(p.cp(0, -b), dks.at[n], dkr.at[n], sr.at[n])

    for n in (7, 4, 5):
        part(n)
    work(1)
    dks[1] = acc[...].astype(BF)
    for k in (1, 3, 2):
        landed(branch, bs.at[k])
        block = bg.at[p.zpeer(-k)[1]]
        c.to(sib, block, block, fs.at[k])
    part(6)
    part(2)
    own_bg.wait()
    landed(branch, bs.at[0])
    for k in (1, 3, 2):
        landed(branch, fs.at[k])
    for j in range(4):
        cols = slice(j * 256, (j + 1) * 256)
        total = jnp.zeros((128, 256), F32)
        for t in range(8):
            total = total + dot(att_t[t * 128 : (t + 1) * 128, :], bg[t, :, cols], TN)
        dwo[:, :, cols] = total.reshape(16, 8, 256)
    for i, (q, f, to_self) in enumerate(owners):
        src, dst = dwo.at[i], dwor.at[p.g * 2 + p.f]

        @pl.when(jnp.logical_not(to_self))
        def _(q=q, f=f, i=i, src=src, dst=dst):
            pltpu.make_async_remote_copy(
                src_ref=src,
                dst_ref=dst,
                send_sem=os_.at[i],
                recv_sem=ors.at[p.g * 2 + p.f],
                device_id=(p.t * 8 + q, f),
                device_id_type=MESH,
            ).start()

        @pl.when(to_self)
        def _(src=src, dst=dst):
            pltpu.make_async_copy(src, dst, os_.at[16]).start()

    part(3)
    whole = dks[1].astype(F32)
    for n in (7, 4, 5):
        landed(dkr.at[0], sr.at[n])
        whole = whole + dkr[n].astype(F32)
    dks[0] = whole.astype(BF)
    c.to(p.cp(1, 0), dks.at[0], dkr.at[1], sr.at[1])
    work(0)
    whole = acc[...]
    for n in (6, 2, 3, 1):
        landed(dkr.at[0], sr.at[n])
        whole = whole + dkr[n].astype(F32)
    dkv[...] = whole

    for i, dst in enumerate((rwg, rwu, rwd)):
        landed(dst, er.at[i])
    for i, (q, f, to_self) in enumerate(owners):

        @pl.when(jnp.logical_not(to_self))
        def _(i=i):
            landed(dwo.at[i], os_.at[i])

        @pl.when(to_self)
        def _(i=i):
            landed(dwo.at[i], os_.at[16])

        from_self = jnp.logical_and(inside, jnp.logical_and(q == p.g, f == p.f))

        @pl.when(jnp.logical_not(from_self))
        def _(i=i):
            landed(dwor.at[0], ors.at[i])

    landed(yret.at[pl.ds(0, 31)], yr)
    c.done()


def backward(qp, kvall, o, lse, att_t, gat, branch, mixed, dwg, dwu, dwd):
    shape = jax.ShapeDtypeStruct
    return pl.pallas_call(
        backward_kernel,
        out_shape=(
            shape((64, 2048), F32),
            shape((1024, 128), F32),
            shape((32, 48, 1024), BF),
            shape((1024, 128), BF),
            shape((1024, 128), BF),
            shape((128, 1024), BF),
            shape((16, 8, 1024), F32),
        ),
        in_specs=[VMEM] * 5 + [HBM] * 6,
        out_specs=(VMEM, VMEM, HBM, HBM, HBM, HBM, HBM),
        scratch_shapes=[
            pltpu.VMEM((8, 128, 128), BF),
            pltpu.VMEM((2048, 128), BF),
            pltpu.VMEM((2, 8, 1024), F32),
            pltpu.VMEM((1024, 128), F32),
            pltpu.VMEM((8, 128, 1024), BF),
            pltpu.VMEM((16, 8, 1024), F32),
            pltpu.VMEM((8, 1024, 128), BF),
            pltpu.VMEM((8, 1024, 128), BF),
            DMA((64,)),
            DMA,
            DMA((4,)),
            DMA((4,)),
            DMA,
            DMA((3,)),
            DMA((8,)),
            DMA((17,)),
            DMA((16,)),
        ],
        compiler_params=params(3, 56),
        name="attention_backward",
    )(qp, kvall, o, lse, att_t, gat, branch, mixed, dwg, dwu, dwd)


def final_kernel(
    dx,
    dwm,
    dxs,
    d2r,
    sibr,
    zsend,
    zr,
    dwr,
    d2s,
    d2l,
    ss,
    sr,
    zrs,
    wrs,
    trs,
):
    p = Place()
    _, sib = p.sibling()
    sem = greet(p.all_tp() + p.all_gf())
    pl.semaphore_wait(sem, 7 + 15)
    c = Copies(ss)
    for k in (1, 2, 3, 0):
        z = lax.rem(p.z + k, 4)
        c.to(sib, dx.at[1 - p.core, z], sibr.at[z], sr.at[k])
    me = p.g * 2 + p.f
    for k in range(1, 16):
        r, dev = p.gf(k)
        c.to(dev, dwm.at[r], dwr.at[me], wrs)
    own_dw = c.here(dwm.at[me], dwr.at[me])

    for k in (1, 3, 2):
        z, _, dev = p.zpeer(k)
        landed(sibr.at[0], sr.at[k])
        zsend[k] = (dx[p.core, z].astype(F32) + sibr[z].astype(F32)).astype(BF)
        c.to(dev, zsend.at[k], zr.at[k], zrs.at[k])
    landed(sibr.at[0], sr.at[0])
    whole = dx[p.core, p.z].astype(F32) + sibr[p.z].astype(F32)

    own_dw.wait()
    landed(dwr.at[pl.ds(0, 15)], wrs)
    total = dwr[0].astype(F32)
    for r in range(1, 16):
        total = total + dwr[r].astype(F32)
    for t in range(8):
        d2s[t, 0:8, :] = total[t * 8 : (t + 1) * 8, :]
        d2s[t, 8:16, :] = total[64:72, :]
    for k in range(1, 8):
        t, dev = p.tp(k)
        c.to(dev, d2s.at[t], d2l.at[p.t], trs)
    own_d2 = c.here(d2s.at[p.t], d2l.at[p.t])
    for k in (1, 3, 2):
        landed(zr.at[0], zrs.at[k])
        whole = whole + zr[k].astype(F32)
    dxs[...] = whole
    own_d2.wait()
    landed(d2l.at[pl.ds(0, 7)], trs)
    d2r[...] = d2l[...]
    c.done()


def final(dx, dwm):
    return pl.pallas_call(
        final_kernel,
        out_shape=(
            jax.ShapeDtypeStruct((128, 1024), F32),
            jax.ShapeDtypeStruct((8, 16, 384), F32),
        ),
        in_specs=[VMEM, HBM],
        out_specs=(VMEM, VMEM),
        scratch_shapes=[
            pltpu.VMEM((4, 128, 1024), BF),
            pltpu.VMEM((4, 128, 1024), BF),
            pltpu.VMEM((4, 128, 1024), BF),
            pltpu.VMEM((16, 80, 384), BF),
            pltpu.VMEM((8, 16, 384), F32),
            pltpu.VMEM((8, 16, 384), F32),
            DMA((32,)),
            DMA((4,)),
            DMA((4,)),
            DMA,
            DMA,
        ],
        compiler_params=params(4, 32),
        name="last_sums",
    )(dx, dwm)


def norm_stats(v):
    factor = lax.rsqrt(jnp.mean(v * v, axis=-1, keepdims=True) + EPS)
    return v * factor, factor


def norm_back(grad_normed, normed, factor):
    return factor * (grad_normed - normed * jnp.mean(grad_normed * normed, axis=-1, keepdims=True))


def rotate(v, cosine, sine):
    first, second = jnp.split(v, 2, axis=-1)
    return jnp.concatenate(
        [first * cosine - second * sine, second * cosine + first * sine], axis=-1
    )


def local(
    layer_input,
    positions,
    routes,
    attn_gain,
    w_query,
    w_key,
    w_value,
    query_gain,
    key_gain,
    w_output,
    ffn_gain,
    w_router,
    w_gate,
    w_up,
    w_down,
    cotangent,
):
    x = layer_input[0]
    cot = cotangent[0]
    gain_m = ffn_gain.reshape(1, 1024)

    wq = w_query.reshape(8, 8, 128).transpose(1, 0, 2)
    wk = w_key.reshape(8, 8, 64).transpose(1, 0, 2)
    wv = w_value.reshape(8, 8, 64).transpose(1, 0, 2)
    wp = jnp.concatenate([wq, jnp.concatenate([wk, wv], axis=2)], axis=1)
    wop = jnp.concatenate(
        [w_output.reshape(64, 128), jnp.pad(w_router, ((0, 8), (0, 96)))], axis=0
    )
    pos = jnp.broadcast_to(positions.astype(F32), (8, 128))
    xg, wg, wog, posg, slots_t, slots, cota = start(x, wp, wop, pos, routes[0].T, cot)

    xf = xg.reshape(1024, 1024).astype(F32)
    normed_a, factor_a = norm_stats(xf)
    normed_in = (normed_a * attn_gain).astype(BF)
    wqkv = wg.reshape(8, 2, 8, 2, 8, 128).transpose(0, 2, 1, 4, 3, 5).reshape(1024, 256)
    raw = dot(normed_in, wqkv)
    steps = jnp.arange(32, dtype=F32) * (2.0 / 64)
    inverse = jnp.power(50000.0, -steps)
    angles = posg[:, 0, :].reshape(1024, 1) * inverse
    cosine, sine = jnp.cos(angles), jnp.sin(angles)
    normed_q, factor_q = norm_stats(raw[:, :128].reshape(1024, 2, 64))
    normed_k, factor_k = norm_stats(raw[:, 128:192])
    scale = 0.125 * LOG2E
    queries = (rotate(normed_q * query_gain, cosine[:, None], sine[:, None]) * scale).astype(BF)
    keys = rotate(normed_k * key_gain, cosine, sine).astype(BF)
    values = raw[:, 192:].astype(BF)
    kv = jnp.concatenate([keys, values], axis=1)
    qp = jnp.pad(queries.transpose(1, 0, 2), ((0, 0), (0, 0), (0, 64))).reshape(2048, 128)

    wob = jnp.concatenate(
        [
            wog[:, :64].reshape(8, 16, 1024),
            jnp.concatenate([wog[0::2, 64:72], wog[1::2, 64:72]], axis=1),
        ],
        axis=2,
    )
    (o, att_t, lse, kvall, cotb, egr, eur, edr, wo, residual, outgoing) = forward(
        qp, kv, slots_t, cot, w_gate[0], w_up[0], w_down[0], wob, x, gain_m
    )
    (mixed, dwg, dwu, dwd, dwr, grad_residual, branch, gat, grad_ffn) = expert_rows(
        outgoing, cota, cotb, egr, eur, edr, wo, slots, residual, cot, gain_m
    )
    dqt, dkv, yret, rwg, rwu, rwd, dwor = backward(
        qp, kvall, o, lse, att_t, gat, branch, mixed, dwg, dwu, dwd
    )

    layer_output = residual + dot(slots, yret.reshape(1536, 1024))
    f = lax.axis_index("fsdp")

    def owned(mine, got):
        return lax.dynamic_index_in_dim(mine, f, keepdims=True).astype(F32) + got.astype(F32)

    dq = dqt.reshape(64, 2, 1024).transpose(2, 1, 0) * 0.125
    dk = dkv[:, :64] * LN2
    dqn = rotate(dq, cosine[:, None], -sine[:, None])
    dkn = rotate(dk, cosine, -sine)
    query_gain_part = jnp.sum(dqn * normed_q, axis=(0, 1))
    key_gain_part = jnp.sum(dkn * normed_k, axis=0)
    dq_raw = norm_back(dqn * query_gain, normed_q, factor_q).reshape(1024, 128)
    dk_raw = norm_back(dkn * key_gain, normed_k, factor_k)
    draw = jnp.concatenate([dq_raw, dk_raw, dkv[:, 64:]], axis=1).astype(BF)
    dwqkv = dot(normed_in, draw, TN)
    dx = dot(draw, wqkv, NT)
    attn_part = jnp.sum(dx * normed_a, axis=0)

    misc = jnp.concatenate(
        [dwr[:, :32], grad_ffn[0][:, None], attn_part[:, None], jnp.zeros((1024, 94), F32)],
        axis=1,
    )
    both = jnp.concatenate([dwqkv, misc], axis=1).astype(BF)
    both = both.reshape(8, 8, 2, 8, 384).transpose(0, 2, 1, 3, 4).reshape(16, 64, 384)
    gains = jnp.concatenate([query_gain_part, key_gain_part, jnp.zeros((256,), F32)])
    gains = jnp.broadcast_to(gains.astype(BF), (16, 16, 384))
    dwm = jnp.concatenate([both, gains], axis=1)
    dxp = dx.astype(BF).reshape(4, 2, 128, 1024).transpose(1, 0, 2, 3)
    dxs, d2 = final(dxp, dwm)

    normed_own, factor_own = norm_stats(x.astype(F32))
    grad_input = grad_residual + norm_back(dxs * attn_gain, normed_own, factor_own)
    own = d2[:, :8].transpose(1, 0, 2)
    sums = jnp.sum(own[:, :, 256:], axis=1)
    gain_sums = jnp.sum(d2[:, 8, :128], axis=0)
    return (
        layer_output.astype(BF)[None],
        grad_input[None],
        sums[:, 33],
        own[:, :, :128].reshape(8, 1024),
        own[:, :, 128:192].reshape(8, 512),
        own[:, :, 192:256].reshape(8, 512),
        gain_sums[:64],
        gain_sums[64:],
        jnp.sum(dwor, axis=0),
        sums[:, 32],
        sums[:, :32],
        owned(dwg, rwg),
        owned(dwu, rwu),
        owned(dwd, rwd),
    )


def solution(mesh):
    rows = P(("ctx", "fsdp"), None)
    vector = P(("ctx", "fsdp"))
    tokens = P("fsdp", "ctx", None)
    return jax.shard_map(
        local,
        mesh=mesh,
        in_specs=(
            tokens,
            P("fsdp", "ctx"),
            tokens,
            P(),
            rows,
            rows,
            rows,
            P(),
            P(),
            rows,
            P(),
            rows,
            P("ctx", None, "fsdp"),
            P("ctx", None, "fsdp"),
            P("ctx", "fsdp", None),
            tokens,
        ),
        out_specs=(
            tokens,
            tokens,
            vector,
            rows,
            rows,
            rows,
            P(),
            P(),
            rows,
            vector,
            rows,
            P("ctx", None, "fsdp"),
            P("ctx", None, "fsdp"),
            P("ctx", "fsdp", None),
        ),
        check_vma=False,
    )
```

```python
import jax
import jax.numpy as jnp
import numpy as np
from jax import lax
from jax.experimental import pallas as pl
from jax.experimental.pallas import tpu as pltpu
from jax.sharding import PartitionSpec as P

EPS = 1e-06
LOG2E = 1.4426950408889634
LN2 = 0.6931471805599453
MESH = pl.DeviceIdType.MESH
VMEM_MIB = 62
BF = jnp.bfloat16
F32 = jnp.float32
NN = (((1,), (0,)), ((), ()))
NT = (((1,), (1,)), ((), ()))
TN = (((0,), (0,)), ((), ()))
HBM = pl.BlockSpec(memory_space=pltpu.HBM)
VMEM = pl.BlockSpec(memory_space=pltpu.VMEM)
DMA = pltpu.SemaphoreType.DMA
MEMBERS = ((0, 0), (1, 0), (0, 1), (0, 3), (1, 1), (1, 3), (0, 2), (1, 2))
CHIPS = tuple(((i + j // 4) % 2, (i + j) % 4, i) for j in range(8) for i in range(4))


def dot(left, right, dims=NN):
    return lax.dot_general(left, right, dims, preferred_element_type=F32)


def dot_exact(left, right, dims=NN):
    return lax.dot_general(
        left, right, dims, precision=lax.Precision.HIGHEST, preferred_element_type=F32
    )


FLAT = [s for s in range(32) if CHIPS[s][2] == 0]
TALL = [s for s in range(32) if CHIPS[s][2] != 0]
STRAIGHT = [s for s in TALL if CHIPS[s][1] == 0]
SLANTED = [s for s in TALL if CHIPS[s][1] != 0]
ROWS_BACK = sorted(range(1, 32), key=lambda s: (1 - CHIPS[s][0], s))


class Place:
    def __init__(self):
        ctx = lax.axis_index("ctx")
        self.f = lax.axis_index("fsdp")
        self.t = lax.rem(ctx, 8)
        self.g = lax.div(ctx, 8)
        self.core = lax.rem(ctx, 2)
        self.z = lax.rem(lax.div(ctx, 2), 4)
        self.y = lax.rem(self.g, 4)
        self.xl = lax.div(self.g, 4)
        self.chip = lax.div(ctx, 2)

    def tp(self, k):
        t = lax.rem(self.t + k, 8)
        return t, (self.g * 8 + t, self.f)

    def cp(self, a, b):
        g = lax.rem(self.xl + a, 2) * 4 + lax.rem(self.y + b + 4, 4)
        return (g * 8 + self.t, self.f)

    def gf(self, k):
        r = lax.rem(self.g * 2 + self.f + k, 16)
        return r, (lax.div(r, 2) * 8 + self.t, lax.rem(r, 2))

    def chips(self, s, sign=1):
        a, b, c = CHIPS[s]
        xl = lax.rem(self.xl + a, 2)
        y = lax.rem(self.y + sign * b + 4, 4)
        z = lax.rem(self.z + sign * c + 4, 4)
        e = (xl * 4 + y) * 4 + z
        return e, (e * 2 + self.core, self.f)

    def zpeer(self, c):
        z = lax.rem(self.z + c + 4, 4)
        t = z * 2 + self.core
        return z, t, (self.g * 8 + t, self.f)

    def sibling(self):
        t = self.z * 2 + 1 - self.core
        return t, (self.g * 8 + t, self.f)

    def partner(self):
        return (self.g * 8 + self.t, 1 - self.f)

    def all_tp(self):
        return [self.tp(k)[1] for k in range(1, 8)]

    def all_gf(self):
        return [self.gf(k)[1] for k in range(1, 16)]

    def all_chips(self):
        return [self.chips(s)[1] for s in range(1, 32)]


def greet(devices):
    sem = pltpu.get_barrier_semaphore()
    for d in devices:
        pl.semaphore_signal(sem, inc=1, device_id=d, device_id_type=MESH)
    return sem


class Copies:
    def __init__(self, sems):
        self.sems, self.count, self.begun = sems, 0, []

    def next(self):
        self.count += 1
        return self.sems.at[self.count - 1]

    def to(self, device, src, dst, recv):
        copy = pltpu.make_async_remote_copy(
            src_ref=src,
            dst_ref=dst,
            send_sem=self.next(),
            recv_sem=recv,
            device_id=device,
            device_id_type=MESH,
        )
        copy.start()
        self.begun.append(copy.wait_send)

    def own(self, src, dst):
        copy = pltpu.make_async_copy(src, dst, self.next())
        copy.start()
        self.begun.append(copy.wait)

    def here(self, src, dst):
        copy = pltpu.make_async_copy(src, dst, self.next())
        copy.start()
        return copy

    def done(self):
        for wait in self.begun:
            wait()


def landed(ref, sem):
    pltpu.make_async_copy(ref, ref, sem).wait()


def params(number, mib):
    return pltpu.CompilerParams(
        collective_id=number, has_side_effects=True, vmem_limit_bytes=mib * 2**20
    )


def lanes(rows):
    return lax.broadcasted_iota(jnp.int32, (rows, 128), 1)


def swap(v):
    low = lax.rem(lanes(v.shape[0]), 64) < 32
    return jnp.where(low, pltpu.roll(v, 96, 1), pltpu.roll(v, 32, 1))


def head_mean(v):
    row = lax.broadcasted_iota(jnp.int32, (128, 128), 0)
    same = lax.div(row, 64) == lax.div(lanes(128), 64)
    return dot_exact(v, jnp.where(same, 1.0 / 64, 0.0))


def cos_sin(angle):
    k = jnp.floor(angle * 0.6366197723675814 + 0.5)
    r = angle - k * 1.5703125
    r = r - k * 4.837512969970703125e-4
    r = r - k * 7.54978995489188216e-8
    r2 = r * r
    s = r + r * r2 * (-1.6666654611e-1 + r2 * (8.3321608736e-3 + r2 * -1.9515295891e-4))
    c = 4.166664568298827e-2 + r2 * (-1.388731625493765e-3 + r2 * 2.443315711809948e-5)
    c = 1.0 - 0.5 * r2 + r2 * r2 * c
    q = k - 4.0 * jnp.floor(k * 0.25)
    odd = jnp.logical_or(q == 1.0, q == 3.0)
    cosine, sine = jnp.where(odd, s, c), jnp.where(odd, c, s)
    cosine = jnp.where(jnp.logical_or(q == 1.0, q == 2.0), -cosine, cosine)
    sine = jnp.where(q >= 2.0, -sine, sine)
    return cosine, sine


def column(row):
    at = lax.broadcasted_iota(jnp.int32, (128, 128), 0) == lanes(128)
    return jnp.sum(jnp.where(at, row, 0.0), axis=1, keepdims=True)


QB = 256
UNROLL = 4


def front_kernel(
    x,
    cot,
    routes,
    pos,
    wq,
    wk,
    wv,
    wo_own,
    wr_own,
    gain_a,
    gain_m,
    gain_q,
    gain_k,
    rates,
    eg,
    eu,
    ed,
    outgoing,
    residual,
    wo,
    slots,
    grads,
    ewg,
    ewu,
    ewd,
    o_out,
    att_out,
    lse_out,
    kv_out,
    qp_out,
    raw_out,
    wqkv_out,
    tabc_out,
    tabs_out,
    normed_out,
    normed_t_out,
    xv,
    cotv,
    routev,
    posv,
    wqv,
    wkv,
    wvv,
    wov,
    wrv,
    gav,
    gmv,
    gqv,
    gkv,
    ratev,
    wps,
    wops,
    posf,
    xg,
    wg,
    wog,
    wob,
    posg,
    wst,
    cots,
    normed,
    normed_t,
    slots_t,
    qp,
    kvall,
    raw,
    wqkv,
    tabc,
    tabs,
    acc,
    lsum,
    o,
    att_t,
    lse,
    attg,
    ss,
    xr,
    fr,
    pr,
    wr,
    gr,
    orr,
    cr,
    kr,
    ar,
    er,
    hr,
    efr,
    wor,
    wofr,
):
    p = Place()
    _, sib = p.sibling()
    me = p.g * 2 + p.f
    c = Copies(ss)
    small = (
        (wq, wqv),
        (wk, wkv),
        (wv, wvv),
        (wo_own, wov),
        (wr_own, wrv),
        (pos, posv),
        (routes, routev),
        (gain_q, gqv),
        (gain_k, gkv),
        (rates, ratev),
        (gain_a, gav),
        (gain_m, gmv),
    )
    loads = [c.here(src, dst) for src, dst in small]
    own_x = c.here(x, xg.at[p.t])
    load_cot = c.here(cot, cotv)
    load_x = c.here(x, xv)
    sem = greet(p.all_chips() + p.all_tp() + p.all_gf())
    for copy in loads:
        copy.wait()

    low8 = lanes(8) < 64
    for t in range(8):
        pair = slice(t // 2 * 128, t // 2 * 128 + 128)
        key, value = wkv[:, pair].astype(F32), wvv[:, pair].astype(F32)
        if t % 2:
            both = jnp.where(low8, pltpu.roll(key, 64, 1), value)
        else:
            both = jnp.where(low8, key, pltpu.roll(value, 64, 1))
        query = wqv[:, t * 128 : (t + 1) * 128].astype(F32)
        wps[t] = jnp.concatenate([query, both], axis=0).astype(BF)
    for i in range(4):
        pair = [wov[:, (2 * i + j) * 128 : (2 * i + j + 1) * 128].astype(F32) for j in range(2)]
        wops[i * 16 : (i + 1) * 16, :] = jnp.concatenate(pair, axis=0).astype(BF)
    router = jnp.concatenate([wrv[...].astype(F32), jnp.zeros((8, 96), F32)], axis=1)
    wops[64:80, :] = jnp.concatenate([router, jnp.zeros((8, 128), F32)], axis=0).astype(BF)
    posf[...] = jnp.broadcast_to(posv[...].astype(F32), (8, 128))
    own = [
        c.here(wps.at[p.t], wst.at[p.t]),
        c.here(posf, posg.at[p.t]),
        c.here(wops, wog.at[me]),
    ]
    pl.semaphore_wait(sem, 31 + 7 + 15)

    for k in range(1, 8):
        t, dev = p.tp(k)
        c.to(dev, wps.at[t], wst.at[p.t], wr)
    for k in (1, 3):
        c.to(p.zpeer(k)[2], x, xg.at[p.t], xr.at[k])
    c.to(sib, x, xg.at[p.t], xr.at[0])
    for k in range(1, 8):
        c.to(p.tp(k)[1], posf, posg.at[p.t], pr)
    for copy in own:
        copy.wait()

    number = lax.broadcasted_iota(jnp.int32, (32, 128), 0)
    hits = jnp.zeros((32, 128), F32)
    for k in range(8):
        hits = hits + jnp.where(routev[k : k + 1, :] == number, 1.0, 0.0)
    row = lax.broadcasted_iota(jnp.int32, (128, 128), 0)
    col = lanes(128)
    before = jnp.where(row < col, 1.0, 0.0).astype(BF)
    place = jnp.where(hits > 0, dot(hits.astype(BF), before), -1.0)
    within = lax.broadcasted_iota(jnp.int32, (48, 128), 0).astype(F32)
    for e in range(32):
        block = jnp.where(place[e : e + 1, :] == within, 1.0, 0.0)
        slots_t[e * 48 : (e + 1) * 48, :] = block.astype(BF)
    load_cot.wait()

    def cot_rows(which):
        for s in which:
            e, dev = p.chips(s)
            mine = slots_t[pl.ds(pl.multiple_of(e * 48, 16), 48), :]
            cots[s] = dot(mine, cotv[...]).astype(BF)
            if s:
                c.to(dev, cots.at[s], grads.at[s], cr)
            else:
                c.own(cots.at[s], grads.at[s])

    landed(wst.at[pl.ds(0, 7)], wr)
    own_wg = c.here(wst, wg.at[me])
    for k in range(1, 16):
        c.to(p.gf(k)[1], wst, wg.at[me], gr)
    for k in range(1, 16):
        c.to(p.gf(k)[1], wops, wog.at[me], orr)
    at_own = pl.ds(pl.multiple_of(p.f * 128, 128), 128)
    at_sib = pl.ds(pl.multiple_of(256 + p.f * 128, 128), 128)
    from_partner = pl.ds(pl.multiple_of((1 - p.f) * 128, 128), 128)
    at_sib_partner = pl.ds(pl.multiple_of(256 + (1 - p.f) * 128, 128), 128)

    def part(ref, i, span):
        return ref.at[span, :] if i == 2 else ref.at[:, span]

    weights = ((eg, ewg), (eu, ewu), (ed, ewd))
    for i, (src, dst) in enumerate(weights):
        c.to(sib, src, part(dst, i, at_sib), er.at[i])
        c.own(src, part(dst, i, at_own))
    cot_rows(FLAT)
    for j in range(12):
        cols = slice(j * 128, (j + 1) * 128)
        slots[:, cols] = slots_t[cols, :].astype(F32).T.astype(BF)

    def pass_on(k, n):
        landed(xg.at[0], xr.at[k])
        t = p.zpeer(-k)[1]
        half = pl.ds(0 if k == 1 else 64, 64)
        c.to(p.zpeer(k)[2], xg.at[t, half], xg.at[t, half], xr.at[n])
        c.to(sib, xg.at[t], xg.at[t], fr.at[k])
        return t

    t1 = pass_on(1, 2)
    t3 = pass_on(3, 4)
    cot_rows(STRAIGHT)
    cot_rows(SLANTED[0:6])

    landed(posg.at[pl.ds(0, 7)], pr)
    signed = jnp.where(lax.rem(col, 64) < 32, -1.0, 1.0)
    for t in range(8):
        cosine, sine = cos_sin(column(posg[t, 0:1, :]) * ratev[...])
        tabc[t * 128 : (t + 1) * 128, :] = cosine
        tabs[t * 128 : (t + 1) * 128, :] = sine * signed

    own_wg.wait()
    landed(wg.at[pl.ds(0, 15)], gr)

    def columns(g, _):
        for t in range(8):
            one, two = wg[2 * g, t].astype(F32), wg[2 * g + 1, t].astype(F32)
            both = [jnp.concatenate([one[i : i + 8], two[i : i + 8]], axis=0) for i in (0, 8)]
            at = pl.ds(pl.multiple_of((g * 8 + t) * 16, 16), 16)
            wqkv[at, :] = jnp.concatenate(both, axis=1).astype(BF)
        return 0

    lax.fori_loop(0, 8, columns, 0)

    lane = lanes(128)
    head_q = jnp.concatenate([gqv[...], gqv[...]], axis=1)
    head_k = jnp.concatenate([gkv[...], jnp.ones((1, 64), F32)], axis=1)

    def project(t):
        rows = pl.ds(pl.multiple_of(t * 128, 128), 128)
        value = xg[t].astype(F32)
        factor = lax.rsqrt(jnp.mean(value * value, axis=1, keepdims=True) + EPS)
        value = (value * factor * gav[...]).astype(BF)
        normed[rows, :] = value
        normed_t[:, rows] = value.astype(F32).T.astype(BF)
        out = dot(value, wqkv[...])
        raw[rows, :] = out
        cosine, sine = tabc[rows, :], tabs[rows, :]
        q, k = out[:, :128], out[:, 128:]
        q = q * lax.rsqrt(head_mean(q * q) + EPS) * head_q
        q = ((q * cosine + swap(q) * sine) * (0.125 * LOG2E)).astype(BF).astype(F32)
        qp[rows, :] = jnp.where(lane < 64, q, 0.0).astype(BF)
        second = pl.ds(pl.multiple_of(1024 + t * 128, 128), 128)
        qp[second, :] = jnp.where(lane < 64, pltpu.roll(q, 64, 1), 0.0).astype(BF)
        n = k * lax.rsqrt(head_mean(k * k) + EPS) * head_k
        n = n * cosine + swap(n) * sine
        kvall[0, rows, :] = jnp.where(lane < 64, n, k).astype(BF)

    own_x.wait()
    project(p.t)
    t2 = p.zpeer(2)[1]
    landed(xg.at[0, pl.ds(0, 64)], xr.at[2])
    landed(xg.at[0, pl.ds(0, 64)], xr.at[4])
    c.to(sib, xg.at[t2], xg.at[t2], fr.at[2])
    project(t1)
    project(t3)
    landed(xg.at[0], xr.at[0])
    project(p.sibling()[0])
    project(t2)
    for k in (1, 3, 2):
        landed(xg.at[0], fr.at[k])
        project(lax.rem(p.z + 4 - k, 4) * 2 + 1 - p.core)

    def kv_to(a, b, src, n, span=None, recv=None):
        src, dst = kvall.at[src], kvall.at[n]
        if span is not None:
            src, dst = src.at[span], dst.at[span]
        c.to(p.cp(a, b), src, dst, kr.at[n if recv is None else recv])

    kv_to(1, 0, 0, 1)
    kv_to(0, 1, 0, 2)
    kv_to(0, 3, 0, 3)
    kept = (
        (qp, qp_out),
        (raw, raw_out),
        (wqkv, wqkv_out),
        (tabc, tabc_out),
        (tabs, tabs_out),
        (normed, normed_out),
        (normed_t, normed_t_out),
    )
    for src, dst in kept:
        c.own(src, dst)

    acc[...] = jnp.zeros_like(acc)
    lsum[...] = jnp.zeros_like(lsum)

    def work(n, _):
        kvb = kvall[n]

        def block(i, _):
            for u in range(UNROLL):
                rows = pl.ds(pl.multiple_of((i * UNROLL + u) * QB, QB), QB)
                e = jnp.exp2(dot(qp[rows, :], kvb, NT))
                total = e[:, 0:128]
                for j in range(1, 8):
                    total = total + e[:, j * 128 : (j + 1) * 128]
                lsum[rows, :] += total
                acc[rows, :] += dot(e.astype(BF), kvb)
            return 0

        lax.fori_loop(0, 2048 // QB // UNROLL, block, 0)
        return 0

    first, second = pl.ds(0, 512), pl.ds(512, 512)
    work(0, 0)
    landed(kvall.at[0], kr.at[1])
    kv_to(0, 1, 1, 4)
    kv_to(0, 3, 1, 5)
    for i, (src, dst) in enumerate(weights):
        c.to(p.partner(), src, part(dst, i, at_own), hr.at[i])

    landed(wog.at[pl.ds(0, 15)], orr)

    def output_rows(g, _):
        one, two = wog[2 * g].astype(F32), wog[2 * g + 1].astype(F32)
        for i in range(9):
            both = [one[i * 8 : i * 8 + 8], two[i * 8 : i * 8 + 8]]
            wob[g, :, i * 128 : (i + 1) * 128] = jnp.concatenate(both, axis=0).astype(BF)
        return 0

    lax.fori_loop(0, 8, output_rows, 0)
    for k in (1, 3, 2):
        c.to(p.zpeer(k)[2], wob, wo.at[:, p.t], wor.at[k])
    c.to(sib, wob, wo.at[:, p.t], wor.at[0])
    own_wo = c.here(wob, wo.at[:, p.t])

    work(1, 0)
    landed(kvall.at[0], kr.at[2])
    kv_to(0, 1, 2, 6, first)
    landed(kvall.at[0], kr.at[3])
    kv_to(0, 3, 3, 6, second, 8)
    lax.fori_loop(2, 4, work, 0)
    landed(kvall.at[0], kr.at[4])
    kv_to(0, 1, 4, 7, first)
    landed(kvall.at[0], kr.at[5])
    kv_to(0, 3, 5, 7, second, 9)
    cot_rows(SLANTED[6:10])
    lax.fori_loop(4, 6, work, 0)
    for i, (_, dst) in enumerate(weights):
        piece = part(dst, i, from_partner)
        landed(piece, hr.at[i])
        c.to(sib, piece, part(dst, i, at_sib_partner), efr.at[i])
    for k in (1, 3, 2):
        landed(wob, wor.at[k])
        block = wo.at[:, p.zpeer(-k)[1]]
        c.to(sib, block, block, wofr.at[k])
    half = kvall.at[0, first]
    for n in (6, 8, 7, 9):
        landed(half, kr.at[n])
    lax.fori_loop(6, 8, work, 0)

    for t in range(8):
        parts = []
        for h in range(2):
            rows = pl.ds(h * 1024 + t * 128, 128)
            total = jnp.sum(lsum[rows, :], axis=1, keepdims=True)
            parts.append(acc[rows, :] / total)
        whole = jnp.where(lane < 64, pltpu.roll(parts[0], 64, 1), parts[1])
        o[pl.ds(t * 128, 128), :] = whole
        att_t[pl.ds(t * 128, 128), :] = whole.astype(BF)
    for k in range(1, 8):
        t, dev = p.tp(k)
        block = att_t.at[pl.ds(pl.multiple_of(t * 128, 128), 128)]
        c.to(dev, block, attg.at[p.t], ar)
    own_att = c.here(att_t.at[pl.ds(pl.multiple_of(p.t * 128, 128), 128)], attg.at[p.t])
    cot_rows(SLANTED[10:18])
    ones = jnp.ones((8, 128), F32)
    for h in range(2):
        lse[h] = jnp.log2(dot_exact(ones, lsum[pl.ds(h * 1024, 1024), :], NT))
    for src, dst in ((o, o_out), (att_t, att_out), (lse, lse_out), (kvall, kv_out)):
        c.own(src, dst)
    own_wo.wait()
    landed(wob, wor.at[0])
    for k in (1, 3, 2):
        landed(wob, wofr.at[k])
    load_x.wait()
    own_att.wait()
    landed(attg.at[pl.ds(0, 7)], ar)

    att = jnp.concatenate([attg[t] for t in range(8)], axis=1)
    square = jnp.zeros((128, 1), F32)
    for j in range(4):
        cols = slice(j * 256, (j + 1) * 256)
        value = xv[:, cols].astype(F32) + dot(att, wo[:, :, :, cols].reshape(1024, 256))
        residual[:, cols] = value
        square = square + jnp.sum(value * value, axis=1, keepdims=True)
    factor = lax.rsqrt(square * (1.0 / 1024) + EPS)
    value = (residual[...] * factor * gmv[...]).astype(BF)
    for j in range(4):
        rows = dot(slots_t[j * 384 : (j + 1) * 384, :], value).astype(BF)
        outgoing[j * 8 : (j + 1) * 8] = rows.reshape(8, 48, 1024)

    for i, (_, dst) in enumerate(weights):
        landed(part(dst, i, at_sib), er.at[i])
        landed(part(dst, i, at_sib), efr.at[i])
    landed(grads.at[pl.ds(0, 31)], cr)
    c.done()


def front(*operands):
    shape = jax.ShapeDtypeStruct
    v = pltpu.VMEM
    return pl.pallas_call(
        front_kernel,
        out_shape=(
            shape((32, 48, 1024), BF),
            shape((128, 1024), F32),
            shape((8, 8, 16, 1152), BF),
            shape((128, 1536), BF),
            shape((32, 48, 1024), BF),
            shape((1024, 512), BF),
            shape((1024, 512), BF),
            shape((512, 1024), BF),
            shape((1024, 128), F32),
            shape((1024, 128), BF),
            shape((2, 8, 1024), F32),
            shape((8, 1024, 128), BF),
            shape((2048, 128), BF),
            shape((1024, 256), F32),
            shape((1024, 256), BF),
            shape((1024, 128), F32),
            shape((1024, 128), F32),
            shape((1024, 1024), BF),
            shape((1024, 1024), BF),
        ),
        in_specs=[HBM] * 17,
        out_specs=(VMEM,) * 4 + (HBM,) * 15,
        scratch_shapes=[
            v((128, 1024), BF),
            v((128, 1024), BF),
            v((8, 128), jnp.int32),
            v((1, 128), jnp.int32),
            v((8, 1024), BF),
            v((8, 512), BF),
            v((8, 512), BF),
            v((8, 1024), BF),
            v((8, 32), BF),
            v((1, 1024), F32),
            v((1, 1024), F32),
            v((1, 64), F32),
            v((1, 64), F32),
            v((1, 128), F32),
            v((8, 16, 128), BF),
            v((80, 128), BF),
            v((8, 128), F32),
            v((8, 128, 1024), BF),
            v((16, 8, 16, 128), BF),
            v((16, 80, 128), BF),
            v((8, 16, 1152), BF),
            v((8, 8, 128), F32),
            v((8, 16, 128), BF),
            v((32, 48, 1024), BF),
            v((1024, 1024), BF),
            v((1024, 1024), BF),
            v((1536, 128), BF),
            v((2048, 128), BF),
            v((8, 1024, 128), BF),
            v((1024, 256), F32),
            v((1024, 256), BF),
            v((1024, 128), F32),
            v((1024, 128), F32),
            v((2048, 128), F32),
            v((2048, 128), F32),
            v((1024, 128), F32),
            v((1024, 128), BF),
            v((2, 8, 1024), F32),
            v((8, 128, 128), BF),
            DMA((176,)),
            DMA((5,)),
            DMA((4,)),
            DMA,
            DMA,
            DMA,
            DMA,
            DMA,
            DMA((10,)),
            DMA,
            DMA((3,)),
            DMA((3,)),
            DMA((3,)),
            DMA((4,)),
            DMA((4,)),
        ],
        compiler_params=params(0, VMEM_MIB),
        name="front",
    )(*operands)


def expert_kernel(
    outgoing,
    residual,
    wo,
    slots,
    grads_in,
    ewg,
    ewu,
    ewd,
    cot_in,
    gain_in,
    branch,
    gat,
    grad_residual_out,
    grad_ffn_out,
    mixed_out,
    dwg_out,
    dwu_out,
    dwd_out,
    dwr_out,
    residual_out,
    slots_out,
    cot,
    gain,
    mixed,
    dwg,
    dwu,
    dwd,
    dwr,
    grad_residual,
    grad_ffn,
    rows,
    grads,
    wg,
    wu,
    wd,
    gh,
    gp,
    up,
    hid,
    gl,
    gin,
    back,
    sg,
    su,
    sd,
    rg,
    ru,
    rd,
    ss,
    rr,
    br,
    wr,
):
    p = Place()
    _, sib = p.sibling()
    sem = greet(p.all_chips() + [sib])
    c = Copies(ss)
    own_rows = c.here(outgoing.at[p.chip], rows.at[0])
    local = [c.here(grads_in, grads), c.here(ewd, wd), c.here(ewg, wg), c.here(ewu, wu)]
    load_cot, load_gain = c.here(cot_in, cot), c.here(gain_in, gain)
    c.own(residual, residual_out)
    c.own(slots, slots_out)
    pl.semaphore_wait(sem, 31 + 1)
    for s in range(1, 32):
        e, dev = p.chips(s)
        c.to(dev, outgoing.at[e], rows.at[s], rr.at[s // 4])
    own_rows.wait()
    for copy in local:
        copy.wait()

    def hidden_grads(j, _):
        block = grads[pl.ds(j * 4, 4)].reshape(192, 1024)
        gh[pl.ds(pl.multiple_of(j * 192, 64), 192), :] = dot(block, wd[...], NT)
        return 0

    lax.fori_loop(0, 8, hidden_grads, 0)

    lane = lax.broadcasted_iota(jnp.int32, (192, 128), 1)
    here = jnp.where(lane == p.chip, 1.0, 0.0)
    router = wo[:, :, :, 1024:].reshape(1024, 128)

    for j in range(8):
        landed(rows.at[pl.ds(0, 4 if j else 3)], rr.at[j])
        block = rows[4 * j : 4 * j + 4].reshape(192, 1024)
        span = pl.ds(j * 192, 192)
        gate_pre = dot(block, wg[...])
        up_pre = dot(block, wu[...])
        logits = jnp.where(lane < 32, dot(block, router), -1e30)
        expo = jnp.exp(logits - jnp.max(logits, axis=1, keepdims=True))
        probs = expo / jnp.sum(expo, axis=1, keepdims=True)
        gate = jnp.sum(probs * here, axis=1, keepdims=True)
        sig = jax.nn.sigmoid(gate_pre)
        act = gate_pre * sig
        hidden = act * up_pre
        grad_hidden = gh[span, :]
        weight = jnp.sum(hidden * grad_hidden, axis=1, keepdims=True) * gate
        grad_hidden = grad_hidden * gate
        grad_gate = (grad_hidden * up_pre * sig * (1.0 + gate_pre * (1.0 - sig))).astype(BF)
        grad_up = (grad_hidden * act).astype(BF)
        grad_logits = (weight * (here - probs)).astype(BF)
        hid[span, :] = (hidden * gate).astype(BF)
        gp[span, :] = grad_gate
        up[span, :] = grad_up
        gl[span, :] = grad_logits
        total = dot(grad_gate, wg[...], NT) + dot(grad_up, wu[...], NT)
        total = total + dot(grad_logits, router, NT)
        gin[4 * j : 4 * j + 4] = total.astype(BF).reshape(4, 48, 1024)
        for s in range(4 * j, 4 * j + 4):
            if s:
                c.to(p.chips(s, -1)[1], gin.at[s], back.at[p.chip], br)
            else:
                own_back = c.here(gin.at[0], back.at[p.chip])

    for m in range(4):
        cols = slice(m * 256, (m + 1) * 256)
        left = rows[:, :, cols].reshape(1536, 256)
        for src, own, sends in ((gp, dwg, sg), (up, dwu, su)):
            value = dot(left, src[...], TN).astype(BF)
            for q in range(2):
                own[q, cols, :] = value[:, q * 128 : (q + 1) * 128]
                sends[q, cols, :] = value[:, (2 + q) * 128 : (3 + q) * 128]
        dwr[cols, :] = dot(left, gl[...], TN)
    for m in range(4):
        cols = slice(m * 256, (m + 1) * 256)
        right = grads[:, :, cols].reshape(1536, 256)
        value = dot(hid[...], right, TN).astype(BF)
        dwd[:, :, cols] = value[:256].reshape(2, 128, 256)
        sd[:, :, cols] = value[256:].reshape(2, 128, 256)
    for i, (src, dst) in enumerate(((sg, rg), (su, ru), (sd, rd))):
        c.to(sib, src, dst, wr.at[i])

    def outputs(j, _):
        block = hid[pl.ds(pl.multiple_of(j * 192, 64), 192), :]
        mixed[pl.ds(j * 4, 4)] = dot(block, wd[...]).astype(BF).reshape(4, 48, 1024)
        return 0

    lax.fori_loop(0, 8, outputs, 0)
    c.own(mixed, mixed_out)
    c.own(dwr, dwr_out)
    for i, (got, own) in enumerate(((rg, dwg), (ru, dwu), (rd, dwd))):
        landed(got, wr.at[i])
        own[...] = (own[...].astype(F32) + got[...].astype(F32)).astype(BF)
    for src, dst in ((dwg, dwg_out), (dwu, dwu_out), (dwd, dwd_out)):
        c.own(src, dst)
    load_cot.wait()
    load_gain.wait()

    landed(back.at[pl.ds(0, 31)], br)
    own_back.wait()
    res = residual[...]
    factor = lax.rsqrt(jnp.mean(res * res, axis=1, keepdims=True) + EPS)
    normed = res * factor
    for j in range(4):
        cols = slice(j * 256, (j + 1) * 256)
        grad_residual[:, cols] = dot(slots[...], back[:, :, cols].reshape(1536, 256))
    grad_mid = grad_residual[...]
    part = jnp.sum(grad_mid * normed, axis=0, keepdims=True)
    grad_ffn[...] = jnp.broadcast_to(part, (8, 1024))
    g = grad_mid * gain[...]
    g = factor * (g - normed * jnp.mean(g * normed, axis=1, keepdims=True))
    g = cot[...].astype(F32) + g
    grad_residual[...] = g
    low = g.astype(BF)
    branch[...] = low
    for t in range(8):
        weights = wo[t][:, :, :1024].reshape(128, 1024)
        gat[t] = dot(low, weights, NT).astype(BF)
    c.own(grad_residual, grad_residual_out)
    c.own(grad_ffn, grad_ffn_out)
    c.done()


def expert_rows(*operands):
    shape = jax.ShapeDtypeStruct
    v = pltpu.VMEM
    return pl.pallas_call(
        expert_kernel,
        out_shape=(
            shape((128, 1024), BF),
            shape((8, 128, 128), BF),
            shape((128, 1024), F32),
            shape((8, 1024), F32),
            shape((32, 48, 1024), BF),
            shape((2, 1024, 128), BF),
            shape((2, 1024, 128), BF),
            shape((2, 128, 1024), BF),
            shape((1024, 128), F32),
            shape((128, 1024), F32),
            shape((128, 1536), BF),
        ),
        in_specs=[VMEM] * 4 + [HBM] * 6,
        out_specs=(VMEM,) * 2 + (HBM,) * 9,
        scratch_shapes=[
            v((128, 1024), BF),
            v((1, 1024), F32),
            v((32, 48, 1024), BF),
            v((2, 1024, 128), BF),
            v((2, 1024, 128), BF),
            v((2, 128, 1024), BF),
            v((1024, 128), F32),
            v((128, 1024), F32),
            v((8, 1024), F32),
            v((32, 48, 1024), BF),
            v((32, 48, 1024), BF),
            v((1024, 512), BF),
            v((1024, 512), BF),
            v((512, 1024), BF),
            v((1536, 512), F32),
            v((1536, 512), BF),
            v((1536, 512), BF),
            v((1536, 512), BF),
            v((1536, 128), BF),
            v((32, 48, 1024), BF),
            v((32, 48, 1024), BF),
            v((2, 1024, 128), BF),
            v((2, 1024, 128), BF),
            v((2, 128, 1024), BF),
            v((2, 1024, 128), BF),
            v((2, 1024, 128), BF),
            v((2, 128, 1024), BF),
            DMA((96,)),
            DMA((8,)),
            DMA,
            DMA((3,)),
        ],
        compiler_params=params(1, VMEM_MIB),
        name="experts",
    )(*operands)


KB = 256
GB = 1024


def back_kernel(
    branch,
    gat,
    grad_residual_in,
    grad_ffn_in,
    mixed,
    dwg,
    dwu,
    dwd,
    dwr_in,
    residual_in,
    slots_in,
    o_in,
    att_in,
    lse_in,
    kv_in,
    qp_in,
    raw_in,
    wqkv_in,
    tabc_in,
    tabs_in,
    normed_in,
    normed_t_in,
    x_in,
    gain_a,
    gain_q,
    gain_k,
    layer_output,
    wide,
    narrow,
    grad_residual,
    grad_ffn,
    dwr,
    residual,
    slots,
    o,
    att_t,
    lse,
    kvall,
    qp,
    raw,
    wqkv,
    tabc,
    tabs,
    normed,
    normed_t,
    xv,
    gav,
    gqv,
    gkv,
    own_g,
    own_u,
    own_d,
    rwg,
    rwu,
    rwd,
    yret,
    dqt,
    dwor,
    gatr,
    dop,
    delta,
    acc,
    bg,
    dwo,
    dwos,
    dwol,
    dks,
    dkr,
    draw,
    dx,
    dwm,
    part,
    sibr,
    zsend,
    zr,
    dwin,
    d2s,
    d2l,
    ss,
    ar,
    bs,
    fs,
    yr,
    er,
    sr,
    os_,
    ors,
    dsr,
    zrs,
    wrs,
    trs,
):
    p = Place()
    _, sib = p.sibling()
    c = Copies(ss)
    first = [
        c.here(src, dst)
        for src, dst in ((o_in, o), (lse_in, lse), (qp_in, qp), (kv_in, kvall), (att_in, att_t))
    ]
    own_gat = c.here(gat.at[p.t], gatr.at[p.t])
    own_bg = c.here(branch, bg.at[p.t])
    sem = greet(p.all_chips() + p.all_tp() + p.all_gf())
    mirror = p.t * 8 + p.g
    at_home = p.g == p.t

    @pl.when(jnp.logical_not(at_home))
    def _():
        pl.semaphore_signal(sem, inc=1, device_id=(mirror, p.f), device_id_type=MESH)

    pl.semaphore_wait(sem, 31 + 7 + 15 + jnp.where(at_home, 0, 1))
    for k in range(1, 8):
        t, dev = p.tp(k)
        c.to(dev, gat.at[t], gatr.at[p.t], ar)
    own_gat.wait()
    for copy in first:
        copy.wait()
    landed(gatr.at[pl.ds(0, 7)], ar)
    for k in (1, 3, 2):
        c.to(p.zpeer(k)[2], branch, bg.at[p.t], bs.at[k])
    c.to(sib, branch, bg.at[p.t], bs.at[0])
    own_mixed = c.here(mixed.at[0], yret.at[p.chip])
    out_g, out_u, out_d = narrow.at[0:1024], narrow.at[1024:2048], wide.at[128:256]
    owned = ((dwg, own_g, rwg, out_g), (dwu, own_u, rwu, out_u), (dwd, own_d, rwd, out_d))
    owned_copies = []
    for i, (src, mine, got, _) in enumerate(owned):
        c.to(p.partner(), src.at[1 - p.f], got, er.at[i])
        owned_copies.append(c.here(src.at[p.f], mine))

    def outputs(which):
        for s in which:
            c.to(p.chips(s, -1)[1], mixed.at[s], yret.at[p.chip], yr)

    outputs(ROWS_BACK[0:6])
    later = (
        (raw_in, raw),
        (wqkv_in, wqkv),
        (tabc_in, tabc),
        (tabs_in, tabs),
        (normed_in, normed),
        (normed_t_in, normed_t),
        (grad_residual_in, grad_residual),
        (grad_ffn_in, grad_ffn),
        (dwr_in, dwr),
        (residual_in, residual),
        (slots_in, slots),
        (x_in, xv),
        (gain_a, gav),
        (gain_q, gqv),
        (gain_k, gkv),
    )
    later = [c.here(src, dst) for src, dst in later]

    lane = lanes(128)
    ones = jnp.ones((8, 128), F32)
    for t in range(8):
        both = gatr[t].astype(F32)
        rows = pl.ds(t * 128, 128)
        dop[rows, :] = jnp.where(lane < 64, 0.0, pltpu.roll(both, 64, 1)).astype(BF)
        dop[pl.ds(1024 + t * 128, 128), :] = jnp.where(lane < 64, 0.0, both).astype(BF)
        prod = both * o[rows, :]
        for h in range(2):
            value = jnp.where((lane < 64) == (h == 0), prod, 0.0)
            delta[h, :, rows] = dot_exact(ones, value, NT)
    dqt[...] = jnp.zeros_like(dqt)

    def work(n):
        def keys(j, _):
            krows = pl.ds(pl.multiple_of(j * KB, KB), KB)
            kvb = kvall[n, krows, :]
            kt = kvb.T[:64, :]
            total = jnp.zeros((KB, 128), F32)
            for i in range(2048 // GB):
                rows = pl.ds(i * GB, GB)
                h, cols = i * GB // 1024, pl.ds(i * GB % 1024, GB)
                q = qp[rows, :]
                d = dop[rows, :]
                w = jnp.exp2(dot(kvb, q, NT) - lse[h, 0:1, cols])
                ds = (w * (dot(kvb, d, NT) - delta[h, 0:1, cols])).astype(BF)
                total = total + dot(w.astype(BF), d) + dot(ds, q)
                dqt[h * 64 : (h + 1) * 64, cols] += dot(kt, ds)
            acc[krows, :] = total
            return 0

        lax.fori_loop(0, 1024 // KB, keys, 0)

    def chunk(n):
        a, b = MEMBERS[n]
        work(n)
        dks[n] = acc[...].astype(BF)
        c.to(p.cp(0, -b), dks.at[n], dkr.at[n], sr.at[n])

    chunk(7)
    outputs(ROWS_BACK[6:10])
    chunk(4)
    outputs(ROWS_BACK[10:14])
    chunk(5)
    for k in (1, 3, 2):
        landed(branch, bs.at[k])
        block = bg.at[p.zpeer(-k)[1]]
        c.to(sib, block, block, fs.at[k])
    outputs(ROWS_BACK[14:18])
    chunk(6)
    outputs(ROWS_BACK[18:22])
    chunk(2)
    outputs(ROWS_BACK[22:26])
    own_bg.wait()
    landed(branch, bs.at[0])
    for k in (1, 3, 2):
        landed(branch, fs.at[k])
    for j in range(4):
        cols = slice(j * 256, (j + 1) * 256)
        total = jnp.zeros((128, 256), F32)
        for t in range(8):
            total = total + dot(att_t[t * 128 : (t + 1) * 128, :], bg[t, :, cols], TN)
        for r in range(16):
            block = total[r * 8 : (r + 1) * 8, :]
            both = [block[:, :128], block[:, 128:]]
            dwo[r, j * 16 : (j + 1) * 16, :] = jnp.concatenate(both, axis=0).astype(BF)
    me = p.g * 2 + p.f
    for k in range(1, 16):
        r, dev = p.gf(k)
        c.to(dev, dwo.at[r], dwor.at[me], ors)
    own_dwo = c.here(dwo.at[me], dwor.at[me])

    chunk(3)
    outputs(ROWS_BACK[26:31])
    work(1)
    whole = acc[...]
    for n in (7, 4, 5):
        landed(dkr.at[0], sr.at[n])
        whole = whole + dkr[n].astype(F32)
    dks[0] = whole.astype(BF)
    c.to(p.cp(1, 0), dks.at[0], dkr.at[1], sr.at[1])
    work(0)

    for copy in later:
        copy.wait()
    head_gains = (
        jnp.concatenate([gqv[...], gqv[...]], axis=1),
        jnp.concatenate([gkv[...], jnp.ones((1, 64), F32)], axis=1),
    )

    def through(i, rows, grad):
        cosine, sine = tabc[rows, :], tabs[rows, :]
        value = raw[rows, i * 128 : (i + 1) * 128]
        grad = grad * cosine - swap(grad) * sine
        factor = lax.rsqrt(head_mean(value * value) + EPS)
        value = value * factor
        total = jnp.sum(grad * value, axis=0, keepdims=True)
        grad = grad * head_gains[i]
        return total, factor * (grad - value * head_mean(grad * value))

    gains_q = jnp.zeros((1, 128), F32)
    for t in range(8):
        rows = slice(t * 128, (t + 1) * 128)
        total, value = through(0, rows, dqt[:, rows].T * 0.125)
        gains_q = gains_q + total
        draw[rows, 0:128] = value.astype(BF)
    for n in (6, 2, 3, 1):
        landed(dkr.at[0], sr.at[n])
    gains_k = jnp.zeros((1, 128), F32)
    for t in range(8):
        rows = slice(t * 128, (t + 1) * 128)
        whole = acc[rows, :]
        for n in (6, 2, 3, 1):
            whole = whole + dkr[n, rows, :].astype(F32)
        total, value = through(1, rows, whole * LN2)
        gains_k = gains_k + total
        draw[rows, 128:256] = jnp.where(lane < 64, value, whole).astype(BF)
    part[...] = jnp.zeros_like(part)

    def input_grad(core, z):
        rows = pl.ds(pl.multiple_of((z * 2 + core) * 128, 128), 128)
        left = draw[rows, :]
        for j in range(4):
            cols = slice(j * 256, (j + 1) * 256)
            value = dot(left, wqkv[cols, :], NT)
            prod = value * normed[rows, cols].astype(F32)
            part[1:2, cols] += jnp.sum(prod, axis=0, keepdims=True)
            dx[core, z, :, cols] = value.astype(BF)

    for k in (1, 3, 2, 0):
        z = lax.rem(p.z + k, 4)
        input_grad(1 - p.core, z)
        c.to(sib, dx.at[1 - p.core, z], sibr.at[z], dsr.at[k])
    for k in (1, 3, 2):
        z, _, dev = p.zpeer(k)
        input_grad(p.core, z)
        landed(sibr.at[0], dsr.at[k])
        zsend[k] = (dx[p.core, z].astype(F32) + sibr[z].astype(F32)).astype(BF)
        c.to(dev, zsend.at[k], zr.at[k], zrs.at[k])
    input_grad(p.core, p.z)

    part[1:2, :] = part[1:2, :] / gav[...]
    part[0:1, :] = grad_ffn[0:1, :]
    eight = lax.broadcasted_iota(jnp.int32, (8, 128), 0)
    pick = jnp.where(lanes(8) == 32 + eight, 1.0, 0.0)
    pick = jnp.where(eight < 2, pick, 0.0)
    gains = jnp.concatenate(
        [gains_q, jnp.where(lanes(1) < 64, gains_k, 0.0), jnp.zeros((1, 128), F32)], axis=1
    )
    gains = jnp.broadcast_to(gains, (16, 384)).astype(BF)
    me = p.g * 2 + p.f
    for j in range(8):
        g = lax.rem(p.g + j, 8)
        rows = pl.ds(pl.multiple_of(g * 128, 128), 128)
        value = dot(normed_t[rows, :], draw[...])
        misc = dwr[rows, :] + dot_exact(part[:, rows], pick, TN)
        value = jnp.concatenate([value, misc], axis=1)
        for f in range(2):
            mine = [value[(2 * t + f) * 8 : (2 * t + f) * 8 + 8, :] for t in range(8)]
            dwm[g * 2 + f, 0:64, :] = jnp.concatenate(mine, axis=0).astype(BF)
            dwm[g * 2 + f, 64:80, :] = gains
        if j:
            for f in range(2):
                c.to((g * 8 + p.t, f), dwm.at[g * 2 + f], dwin.at[me], wrs)
        else:
            c.to(p.partner(), dwm.at[g * 2 + 1 - p.f], dwin.at[me], wrs)
            own_dw = c.here(dwm.at[me], dwin.at[me])

    landed(sibr.at[0], dsr.at[0])
    whole = dx[p.core, p.z].astype(F32) + sibr[p.z].astype(F32)
    for i, (_, mine, got, out) in enumerate(owned):
        owned_copies[i].wait()
        landed(got, er.at[i])
        out[...] = mine[...].astype(F32) + got[...].astype(F32)
    own_dwo.wait()
    landed(dwor.at[pl.ds(0, 15)], ors)
    total = dwor[0].astype(F32)
    for r in range(1, 16):
        total = total + dwor[r].astype(F32)
    for i in range(8):
        dwos[:, i * 128 : (i + 1) * 128] = total[i * 8 : (i + 1) * 8, :]

    @pl.when(jnp.logical_not(at_home))
    def _():
        pltpu.make_async_remote_copy(
            src_ref=dwos,
            dst_ref=dwol,
            send_sem=os_.at[0],
            recv_sem=os_.at[1],
            device_id=(mirror, p.f),
            device_id_type=MESH,
        ).start()

    @pl.when(at_home)
    def _():
        pltpu.make_async_copy(dwos, dwol, os_.at[2]).start()

    own_dw.wait()
    landed(dwin.at[pl.ds(0, 15)], wrs)
    total = dwin[0].astype(F32)
    for r in range(1, 16):
        total = total + dwin[r].astype(F32)
    for t in range(8):
        d2s[t, 0:8, :] = total[t * 8 : (t + 1) * 8, :]
        d2s[t, 8:16, :] = total[64:72, :]
    for k in range(1, 8):
        t, dev = p.tp(k)
        c.to(dev, d2s.at[t], d2l.at[p.t], trs)
    own_d2 = c.here(d2s.at[p.t], d2l.at[p.t])

    for k in (1, 3, 2):
        landed(zr.at[0], zrs.at[k])
        whole = whole + zr[k].astype(F32)
    xf = xv[...].astype(F32)
    factor = lax.rsqrt(jnp.mean(xf * xf, axis=1, keepdims=True) + EPS)
    n = xf * factor
    g = whole * gav[...]
    g = factor * (g - n * jnp.mean(g * n, axis=1, keepdims=True))
    wide[0:128, :] = grad_residual[...] + g
    own_mixed.wait()
    landed(yret.at[pl.ds(0, 31)], yr)
    for j in range(4):
        cols = slice(j * 256, (j + 1) * 256)
        value = residual[:, cols] + dot(slots[...], yret[:, :, cols].reshape(1536, 256))
        layer_output[:, cols] = value.astype(BF)

    @pl.when(jnp.logical_not(at_home))
    def _():
        landed(dwos, os_.at[0])
        landed(dwol, os_.at[1])

    @pl.when(at_home)
    def _():
        landed(dwol, os_.at[2])

    wide[264:272, :] = dwol[...]
    own_d2.wait()
    landed(d2l.at[pl.ds(0, 7)], trs)
    low8 = lanes(8) < 64
    misc = jnp.zeros((8, 128), F32)
    totals = [jnp.zeros((8, 128), F32)] * 2
    for t in range(8):
        wide[256:264, t * 128 : (t + 1) * 128] = d2l[t, 0:8, 0:128]
        misc = misc + d2l[t, 0:8, 256:384]
        totals = [totals[i] + d2l[t, 8:16, i * 128 : (i + 1) * 128] for i in range(2)]
    for i in range(4):
        one, two = d2l[2 * i, 0:8, 128:256], d2l[2 * i + 1, 0:8, 128:256]
        cols = slice(i * 128, (i + 1) * 128)
        wide[272:280, cols] = jnp.where(low8, one, pltpu.roll(two, 64, 1))
        cols = slice(512 + i * 128, 512 + (i + 1) * 128)
        wide[272:280, cols] = jnp.where(low8, pltpu.roll(one, 64, 1), two)
    narrow[2048:2056, :] = misc
    heads = totals[0] + pltpu.roll(totals[0], 64, 1)
    narrow[2056:2064, :] = jnp.where(eight == 0, heads, totals[1])
    c.done()


def back(*operands):
    shape = jax.ShapeDtypeStruct
    v = pltpu.VMEM
    return pl.pallas_call(
        back_kernel,
        out_shape=(
            shape((128, 1024), BF),
            shape((280, 1024), F32),
            shape((2064, 128), F32),
        ),
        in_specs=[VMEM] * 2 + [HBM] * 24,
        out_specs=(VMEM,) * 3,
        scratch_shapes=[
            v((128, 1024), F32),
            v((8, 1024), F32),
            v((1024, 128), F32),
            v((128, 1024), F32),
            v((128, 1536), BF),
            v((1024, 128), F32),
            v((1024, 128), BF),
            v((2, 8, 1024), F32),
            v((8, 1024, 128), BF),
            v((2048, 128), BF),
            v((1024, 256), F32),
            v((1024, 256), BF),
            v((1024, 128), F32),
            v((1024, 128), F32),
            v((1024, 1024), BF),
            v((1024, 1024), BF),
            v((128, 1024), BF),
            v((1, 1024), F32),
            v((1, 64), F32),
            v((1, 64), F32),
            v((1024, 128), BF),
            v((1024, 128), BF),
            v((128, 1024), BF),
            v((1024, 128), BF),
            v((1024, 128), BF),
            v((128, 1024), BF),
            v((32, 48, 1024), BF),
            v((128, 1024), F32),
            v((16, 64, 128), BF),
            v((8, 128, 128), BF),
            v((2048, 128), BF),
            v((2, 8, 1024), F32),
            v((1024, 128), F32),
            v((8, 128, 1024), BF),
            v((16, 64, 128), BF),
            v((8, 1024), F32),
            v((8, 1024), F32),
            v((8, 1024, 128), BF),
            v((8, 1024, 128), BF),
            v((1024, 256), BF),
            v((2, 4, 128, 1024), BF),
            v((16, 80, 384), BF),
            v((8, 1024), F32),
            v((4, 128, 1024), BF),
            v((4, 128, 1024), BF),
            v((4, 128, 1024), BF),
            v((16, 80, 384), BF),
            v((8, 16, 384), F32),
            v((8, 16, 384), F32),
            DMA((128,)),
            DMA,
            DMA((4,)),
            DMA((4,)),
            DMA,
            DMA((3,)),
            DMA((8,)),
            DMA((3,)),
            DMA,
            DMA((4,)),
            DMA((4,)),
            DMA,
            DMA,
        ],
        compiler_params=params(2, VMEM_MIB),
        name="back",
    )(*operands)


RATES = np.power(50000.0, -(np.arange(128) % 32) / 32.0).astype(np.float32).reshape(1, 128)


def local(
    layer_input,
    positions,
    routes,
    attn_gain,
    w_query,
    w_key,
    w_value,
    query_gain,
    key_gain,
    w_output,
    ffn_gain,
    w_router,
    w_gate,
    w_up,
    w_down,
    cotangent,
):
    x = layer_input[0]
    cot = cotangent[0]
    gain_a = attn_gain.reshape(1, 1024)
    gain_m = ffn_gain.reshape(1, 1024)
    gain_q = query_gain.reshape(1, 64)
    gain_k = key_gain.reshape(1, 64)
    (outgoing, residual, wo, slots, grads, ewg, ewu, ewd, *kept) = front(
        x,
        cot,
        routes[0].T,
        positions,
        w_query,
        w_key,
        w_value,
        w_output,
        w_router,
        gain_a,
        gain_m,
        gain_q,
        gain_k,
        jnp.asarray(RATES),
        w_gate[0],
        w_up[0],
        w_down[0],
    )
    passed = expert_rows(outgoing, residual, wo, slots, grads, ewg, ewu, ewd, cot, gain_m)
    layer_output, wide, narrow = back(*passed, *kept, x, gain_a, gain_q, gain_k)
    return (
        layer_output[None],
        wide[None, 0:128],
        narrow[2048:2056, 33],
        wide[256:264],
        wide[272:280, :512],
        wide[272:280, 512:],
        narrow[2056, :64],
        narrow[2057, :64],
        wide[264:272],
        narrow[2048:2056, 32],
        narrow[2048:2056, :32],
        narrow[None, 0:1024],
        narrow[None, 1024:2048],
        wide[None, 128:256],
    )


def solution(mesh):
    rows = P(("ctx", "fsdp"), None)
    vector = P(("ctx", "fsdp"))
    tokens = P("fsdp", "ctx", None)
    return jax.shard_map(
        local,
        mesh=mesh,
        in_specs=(
            tokens,
            P("fsdp", "ctx"),
            tokens,
            P(),
            rows,
            rows,
            rows,
            P(),
            P(),
            rows,
            P(),
            rows,
            P("ctx", None, "fsdp"),
            P("ctx", None, "fsdp"),
            P("ctx", "fsdp", None),
            tokens,
        ),
        out_specs=(
            tokens,
            tokens,
            vector,
            rows,
            rows,
            rows,
            P(),
            P(),
            rows,
            vector,
            rows,
            P("ctx", None, "fsdp"),
            P("ctx", None, "fsdp"),
            P("ctx", "fsdp", None),
        ),
        check_vma=False,
    )
```

```python
import functools

import jax
import jax.numpy as jnp
import numpy as np
from jax import lax
from jax.experimental import pallas as pl
from jax.experimental.pallas import tpu as pltpu
from jax.sharding import PartitionSpec as P

EPS = 1e-06
LOG2E = 1.4426950408889634
LN2 = 0.6931471805599453
MESH = pl.DeviceIdType.MESH
VMEM_MIB = 62
BF = jnp.bfloat16
F32 = jnp.float32
NN = (((1,), (0,)), ((), ()))
NT = (((1,), (1,)), ((), ()))
TN = (((0,), (0,)), ((), ()))
HBM = pl.BlockSpec(memory_space=pltpu.HBM)
VMEM = pl.BlockSpec(memory_space=pltpu.VMEM)
DMA = pltpu.SemaphoreType.DMA
MEMBERS = ((0, 0), (0, 1), (0, 3), (1, 0), (0, 2), (1, 1), (1, 3), (1, 2))
PLANE = ((0, 0), (2, 2), (1, 1), (3, 3), (1, 3), (3, 1), (0, 1), (2, 3))
PLANE = PLANE + ((0, 3), (2, 1), (1, 0), (3, 2), (3, 0), (1, 2), (0, 2), (2, 0))
CHIPS = tuple((a, b, c) for b, c in PLANE for a in range(2))
ALONG_Z = [m for m in range(1, 16) if PLANE[m][0] == 0]
ALONG_Y = [m for m in range(1, 16) if PLANE[m][1] == 0]
ALONG_BOTH = [m for m in range(1, 16) if PLANE[m][0] and PLANE[m][1]]
LATER = ALONG_BOTH + ALONG_Y


def dot(left, right, dims=NN):
    return lax.dot_general(left, right, dims, preferred_element_type=F32)


def dot_exact(left, right, dims=NN):
    return lax.dot_general(
        left, right, dims, precision=lax.Precision.HIGHEST, preferred_element_type=F32
    )


class Place:
    def __init__(self):
        ctx = lax.axis_index("ctx")
        self.f = lax.axis_index("fsdp")
        self.t = lax.rem(ctx, 8)
        self.g = lax.div(ctx, 8)
        self.core = lax.rem(ctx, 2)
        self.z = lax.rem(lax.div(ctx, 2), 4)
        self.y = lax.rem(self.g, 4)
        self.xl = lax.div(self.g, 4)
        self.chip = lax.div(ctx, 2)

    def tp(self, k):
        t = lax.rem(self.t + k, 8)
        return t, (self.g * 8 + t, self.f)

    def cp(self, a, b):
        g = lax.rem(self.xl + a, 2) * 4 + lax.rem(self.y + b + 4, 4)
        return (g * 8 + self.t, self.f)

    def gf(self, k):
        r = lax.rem(self.g * 2 + self.f + k, 16)
        return r, (lax.div(r, 2) * 8 + self.t, lax.rem(r, 2))

    def chips(self, s, sign=1):
        a, b, c = CHIPS[s]
        xl = lax.rem(self.xl + a, 2)
        y = lax.rem(self.y + sign * b + 4, 4)
        z = lax.rem(self.z + sign * c + 4, 4)
        e = (xl * 4 + y) * 4 + z
        return e, (e * 2 + self.core, self.f)

    def plane(self, m, sign=1):
        b, c = PLANE[m]
        i = lax.rem(self.y + sign * b + 4, 4) * 4 + lax.rem(self.z + sign * c + 4, 4)
        e = self.xl * 16 + i
        return i, (e * 2 + self.core, self.f)

    def zpeer(self, c):
        z = lax.rem(self.z + c + 4, 4)
        t = z * 2 + self.core
        return z, t, (self.g * 8 + t, self.f)

    def sibling(self):
        t = self.z * 2 + 1 - self.core
        return t, (self.g * 8 + t, self.f)

    def partner(self):
        return (self.g * 8 + self.t, 1 - self.f)

    def all_tp(self):
        return [self.tp(k)[1] for k in range(1, 8)]

    def all_gf(self):
        return [self.gf(k)[1] for k in range(1, 16)]

    def all_chips(self):
        return [self.chips(s)[1] for s in range(1, 32)]


def greet(devices):
    sem = pltpu.get_barrier_semaphore()
    for d in devices:
        pl.semaphore_signal(sem, inc=1, device_id=d, device_id_type=MESH)
    return sem


class Copies:
    def __init__(self, sems):
        self.sems, self.count, self.begun = sems, 0, []

    def next(self):
        self.count += 1
        return self.sems.at[self.count - 1]

    def to(self, device, src, dst, recv):
        copy = pltpu.make_async_remote_copy(
            src_ref=src,
            dst_ref=dst,
            send_sem=self.next(),
            recv_sem=recv,
            device_id=device,
            device_id_type=MESH,
        )
        copy.start()
        self.begun.append(copy.wait_send)

    def own(self, src, dst):
        copy = pltpu.make_async_copy(src, dst, self.next())
        copy.start()
        self.begun.append(copy.wait)

    def here(self, src, dst):
        copy = pltpu.make_async_copy(src, dst, self.next())
        copy.start()
        return copy

    def done(self):
        for wait in self.begun:
            wait()


def landed(ref, sem):
    pltpu.make_async_copy(ref, ref, sem).wait()


def params(number, mib):
    return pltpu.CompilerParams(
        collective_id=number, has_side_effects=True, vmem_limit_bytes=mib * 2**20
    )


def lanes(rows):
    return lax.broadcasted_iota(jnp.int32, (rows, 128), 1)


def swap(v):
    low = lax.rem(lanes(v.shape[0]), 64) < 32
    return jnp.where(low, pltpu.roll(v, 96, 1), pltpu.roll(v, 32, 1))


def head_mean(v):
    row = lax.broadcasted_iota(jnp.int32, (128, 128), 0)
    same = lax.div(row, 64) == lax.div(lanes(128), 64)
    return dot_exact(v, jnp.where(same, 1.0 / 64, 0.0))


def cos_sin(angle):
    k = jnp.floor(angle * 0.6366197723675814 + 0.5)
    r = angle - k * 1.5703125
    r = r - k * 4.837512969970703125e-4
    r = r - k * 7.54978995489188216e-8
    r2 = r * r
    s = r + r * r2 * (-1.6666654611e-1 + r2 * (8.3321608736e-3 + r2 * -1.9515295891e-4))
    c = 4.166664568298827e-2 + r2 * (-1.388731625493765e-3 + r2 * 2.443315711809948e-5)
    c = 1.0 - 0.5 * r2 + r2 * r2 * c
    q = k - 4.0 * jnp.floor(k * 0.25)
    odd = jnp.logical_or(q == 1.0, q == 3.0)
    cosine, sine = jnp.where(odd, s, c), jnp.where(odd, c, s)
    cosine = jnp.where(jnp.logical_or(q == 1.0, q == 2.0), -cosine, cosine)
    sine = jnp.where(q >= 2.0, -sine, sine)
    return cosine, sine


def column(row):
    at = lax.broadcasted_iota(jnp.int32, (128, 128), 0) == lanes(128)
    return jnp.sum(jnp.where(at, row, 0.0), axis=1, keepdims=True)


QB = 256
UNROLL = 4


def front_kernel(
    x,
    cot,
    routes,
    pos,
    wq,
    wk,
    wv,
    wo_own,
    wr_own,
    gain_a,
    gain_m,
    gain_q,
    gain_k,
    rates,
    eg,
    eu,
    ed,
    outgoing,
    residual,
    wo,
    slots,
    grads,
    ewg,
    ewu,
    ewd,
    o_out,
    att_out,
    lse_out,
    kv_out,
    qp_out,
    raw_out,
    wqkv_out,
    tabc_out,
    tabs_out,
    normed_out,
    normed_t_out,
    near_out,
    xv,
    cotv,
    routev,
    posv,
    wqv,
    wkv,
    wvv,
    wov,
    wrv,
    gav,
    gmv,
    gqv,
    gkv,
    ratev,
    wps,
    wops,
    posf,
    xg,
    wg,
    wog,
    wob,
    posg,
    wst,
    cots,
    normed,
    normed_t,
    slots_t,
    slots_p,
    near,
    place_p,
    routep,
    cotp,
    qp,
    kvall,
    raw,
    wqkv,
    tabc,
    tabs,
    acc,
    lsum,
    o,
    att_t,
    lse,
    attg,
    ss,
    xr,
    fr,
    pr,
    wr,
    gr,
    orr,
    cr,
    kr,
    ar,
    er,
    hr,
    efr,
    wor,
    wofr,
    xpr,
):
    p = Place()
    _, sib = p.sibling()
    me = p.g * 2 + p.f
    c = Copies(ss)
    small = (
        (wq, wqv),
        (wk, wkv),
        (wv, wvv),
        (wo_own, wov),
        (wr_own, wrv),
        (pos, posv),
        (routes, routev),
        (gain_q, gqv),
        (gain_k, gkv),
        (rates, ratev),
        (gain_a, gav),
        (gain_m, gmv),
    )
    loads = [c.here(src, dst) for src, dst in small]
    own_x = c.here(x, xg.at[p.t])
    load_cot = c.here(cot, cotv)
    load_x = c.here(x, xv)
    sem = greet(p.all_chips() + p.all_tp() + p.all_gf())
    for copy in loads:
        copy.wait()

    low8 = lanes(8) < 64
    for t in range(8):
        pair = slice(t // 2 * 128, t // 2 * 128 + 128)
        key, value = wkv[:, pair].astype(F32), wvv[:, pair].astype(F32)
        if t % 2:
            both = jnp.where(low8, pltpu.roll(key, 64, 1), value)
        else:
            both = jnp.where(low8, key, pltpu.roll(value, 64, 1))
        query = wqv[:, t * 128 : (t + 1) * 128].astype(F32)
        wps[t] = jnp.concatenate([query, both], axis=0).astype(BF)
    for i in range(4):
        pair = [wov[:, (2 * i + j) * 128 : (2 * i + j + 1) * 128].astype(F32) for j in range(2)]
        wops[i * 16 : (i + 1) * 16, :] = jnp.concatenate(pair, axis=0).astype(BF)
    router = jnp.concatenate([wrv[...].astype(F32), jnp.zeros((8, 96), F32)], axis=1)
    wops[64:80, :] = jnp.concatenate([router, jnp.zeros((8, 128), F32)], axis=0).astype(BF)
    posf[...] = jnp.broadcast_to(posv[...].astype(F32), (8, 128))
    own = [
        c.here(wps.at[p.t], wst.at[p.t]),
        c.here(posf, posg.at[p.t]),
        c.here(wops, wog.at[me]),
    ]
    pl.semaphore_wait(sem, 31 + 7 + 15)

    for k in range(1, 8):
        t, dev = p.tp(k)
        c.to(dev, wps.at[t], wst.at[p.t], wr)
    for k in (1, 3):
        c.to(p.zpeer(k)[2], x, xg.at[p.t], xr.at[k])
    c.to(sib, x, xg.at[p.t], xr.at[0])
    c.to(p.cp(1, 0), routev, routep, xpr.at[0])
    c.to(p.cp(1, 0), cot, cotp, xpr.at[1])
    for k in range(1, 8):
        c.to(p.tp(k)[1], posf, posg.at[p.t], pr)
    for copy in own:
        copy.wait()

    row = lax.broadcasted_iota(jnp.int32, (128, 128), 0)
    col = lanes(128)

    def places(ref):
        number = lax.broadcasted_iota(jnp.int32, (32, 128), 0)
        hits = jnp.zeros((32, 128), F32)
        for k in range(8):
            hits = hits + jnp.where(ref[k : k + 1, :] == number, 1.0, 0.0)
        before = jnp.where(row < col, 1.0, 0.0).astype(BF)
        return jnp.where(hits > 0, dot(hits.astype(BF), before), -1.0)

    def slot_rows(place):
        within = lax.broadcasted_iota(jnp.int32, (48, 128), 0).astype(F32)
        return jnp.where(place == within, 1.0, 0.0).astype(BF)

    place = places(routev)
    for e in range(32):
        slots_t[e * 48 : (e + 1) * 48, :] = slot_rows(place[e : e + 1, :])
    load_cot.wait()

    def cot_rows(which):
        for m in which:
            i, dev = p.plane(m)
            for a, (ref, values) in enumerate(((slots_t, cotv), (slots_p, cotp))):
                first = i + p.xl * 16 if a == 0 else i
                mine = ref[pl.ds(pl.multiple_of(first * 48, 16), 48), :]
                cots[2 * m + a] = dot(mine, values[...]).astype(BF)
            pair = pl.ds(2 * m, 2)
            if m:
                c.to(dev, cots.at[pair], grads.at[pair], cr)
            else:
                c.own(cots.at[pair], grads.at[pair])

    landed(wst.at[pl.ds(0, 7)], wr)
    own_wg = c.here(wst, wg.at[me])
    for k in range(1, 16):
        c.to(p.gf(k)[1], wst, wg.at[me], gr)
    for k in range(1, 16):
        c.to(p.gf(k)[1], wops, wog.at[me], orr)
    at_own = pl.ds(pl.multiple_of(p.f * 128, 128), 128)
    at_sib = pl.ds(pl.multiple_of(256 + p.f * 128, 128), 128)
    from_partner = pl.ds(pl.multiple_of((1 - p.f) * 128, 128), 128)
    at_sib_partner = pl.ds(pl.multiple_of(256 + (1 - p.f) * 128, 128), 128)

    def part(ref, i, span):
        return ref.at[span, :] if i == 2 else ref.at[:, span]

    weights = ((eg, ewg), (eu, ewu), (ed, ewd))
    for i, (src, dst) in enumerate(weights):
        c.to(sib, src, part(dst, i, at_sib), er.at[i])
        c.own(src, part(dst, i, at_own))
    landed(routep, xpr.at[0])
    place_p[...] = places(routep)
    here = place_p[pl.ds(pl.multiple_of(p.xl * 16, 16), 16), :]
    for e in range(16):
        slots_p[e * 48 : (e + 1) * 48, :] = slot_rows(here[e : e + 1, :])
    for j in range(12):
        cols = slice(j * 128, (j + 1) * 128)
        slots[:, cols] = slots_t[cols, :].astype(F32).T.astype(BF)
    for j in range(6):
        cols = slice(j * 128, (j + 1) * 128)
        near[1, :, cols] = slots_p[cols, :].astype(F32).T.astype(BF)
    near[0] = slots[:, pl.ds(pl.multiple_of(p.xl * 768, 128), 768)]
    c.own(near, near_out)
    landed(cotp, xpr.at[1])

    def pass_on(k, n):
        landed(xg.at[0], xr.at[k])
        t = p.zpeer(-k)[1]
        half = pl.ds(0 if k == 1 else 64, 64)
        c.to(p.zpeer(k)[2], xg.at[t, half], xg.at[t, half], xr.at[n])
        c.to(sib, xg.at[t], xg.at[t], fr.at[k])
        return t

    t1 = pass_on(1, 2)
    t3 = pass_on(3, 4)
    cot_rows(ALONG_BOTH[0:4])
    c.to(p.partner(), eg, part(ewg, 0, at_own), hr.at[0])

    landed(posg.at[pl.ds(0, 7)], pr)
    signed = jnp.where(lax.rem(col, 64) < 32, -1.0, 1.0)
    for t in range(8):
        cosine, sine = cos_sin(column(posg[t, 0:1, :]) * ratev[...])
        tabc[t * 128 : (t + 1) * 128, :] = cosine
        tabs[t * 128 : (t + 1) * 128, :] = sine * signed

    own_wg.wait()
    landed(wg.at[pl.ds(0, 15)], gr)

    def columns(g, _):
        for t in range(8):
            one, two = wg[2 * g, t].astype(F32), wg[2 * g + 1, t].astype(F32)
            both = [jnp.concatenate([one[i : i + 8], two[i : i + 8]], axis=0) for i in (0, 8)]
            at = pl.ds(pl.multiple_of((g * 8 + t) * 16, 16), 16)
            wqkv[at, :] = jnp.concatenate(both, axis=1).astype(BF)
        return 0

    lax.fori_loop(0, 8, columns, 0)

    landed(wog.at[pl.ds(0, 15)], orr)

    def output_rows(g, _):
        one, two = wog[2 * g].astype(F32), wog[2 * g + 1].astype(F32)
        for i in range(9):
            both = [one[i * 8 : i * 8 + 8], two[i * 8 : i * 8 + 8]]
            wob[g, :, i * 128 : (i + 1) * 128] = jnp.concatenate(both, axis=0).astype(BF)
        return 0

    lax.fori_loop(0, 8, output_rows, 0)
    for k in (1, 3, 2):
        c.to(p.zpeer(k)[2], wob, wo.at[:, p.t], wor.at[k])
    c.to(sib, wob, wo.at[:, p.t], wor.at[0])
    own_wo = c.here(wob, wo.at[:, p.t])

    lane = lanes(128)
    head_q = jnp.concatenate([gqv[...], gqv[...]], axis=1)
    head_k = jnp.concatenate([gkv[...], jnp.ones((1, 64), F32)], axis=1)

    def project(t):
        rows = pl.ds(pl.multiple_of(t * 128, 128), 128)
        value = xg[t].astype(F32)
        factor = lax.rsqrt(jnp.mean(value * value, axis=1, keepdims=True) + EPS)
        value = (value * factor * gav[...]).astype(BF)
        normed[rows, :] = value
        normed_t[:, rows] = value.astype(F32).T.astype(BF)
        out = dot(value, wqkv[...])
        raw[rows, :] = out
        cosine, sine = tabc[rows, :], tabs[rows, :]
        q, k = out[:, :128], out[:, 128:]
        q = q * lax.rsqrt(head_mean(q * q) + EPS) * head_q
        q = ((q * cosine + swap(q) * sine) * (0.125 * LOG2E)).astype(BF).astype(F32)
        qp[rows, :] = jnp.where(lane < 64, q, 0.0).astype(BF)
        second = pl.ds(pl.multiple_of(1024 + t * 128, 128), 128)
        qp[second, :] = jnp.where(lane < 64, pltpu.roll(q, 64, 1), 0.0).astype(BF)
        n = k * lax.rsqrt(head_mean(k * k) + EPS) * head_k
        n = n * cosine + swap(n) * sine
        kvall[0, rows, :] = jnp.where(lane < 64, n, k).astype(BF)

    own_x.wait()
    project(p.t)
    t2 = p.zpeer(2)[1]
    landed(xg.at[0, pl.ds(0, 64)], xr.at[2])
    landed(xg.at[0, pl.ds(0, 64)], xr.at[4])
    c.to(sib, xg.at[t2], xg.at[t2], fr.at[2])
    project(t1)
    project(t3)
    landed(xg.at[0], xr.at[0])
    project(p.sibling()[0])
    project(t2)
    for k in (1, 3, 2):
        landed(xg.at[0], fr.at[k])
        project(lax.rem(p.z + 4 - k, 4) * 2 + 1 - p.core)

    def kv_to(a, b, src, n, span=None, recv=None):
        src, dst = kvall.at[src], kvall.at[n]
        if span is not None:
            src, dst = src.at[span], dst.at[span]
        c.to(p.cp(a, b), src, dst, kr.at[n if recv is None else recv])

    kv_to(0, 1, 0, 1)
    kv_to(0, 3, 0, 2)
    kv_to(1, 0, 0, 3)
    kept = (
        (qp, qp_out),
        (raw, raw_out),
        (wqkv, wqkv_out),
        (tabc, tabc_out),
        (tabs, tabs_out),
        (normed, normed_out),
        (normed_t, normed_t_out),
    )
    for src, dst in kept:
        c.own(src, dst)

    acc[...] = jnp.zeros_like(acc)
    lsum[...] = jnp.zeros_like(lsum)

    def work(n, _):
        kvb = kvall[n]

        def block(i, _):
            for u in range(UNROLL):
                rows = pl.ds(pl.multiple_of((i * UNROLL + u) * QB, QB), QB)
                e = jnp.exp2(dot(qp[rows, :], kvb, NT))
                total = e[:, 0:128]
                for j in range(1, 8):
                    total = total + e[:, j * 128 : (j + 1) * 128]
                lsum[rows, :] += total
                acc[rows, :] += dot(e.astype(BF), kvb)
            return 0

        lax.fori_loop(0, 2048 // QB // UNROLL, block, 0)
        return 0

    first, second = pl.ds(0, 512), pl.ds(512, 512)
    half = kvall.at[0, first]
    work(0, 0)
    landed(kvall.at[0], kr.at[1])
    kv_to(0, 1, 1, 4, first)
    kv_to(1, 0, 1, 5)
    landed(kvall.at[0], kr.at[2])
    kv_to(0, 3, 2, 4, second, 8)
    kv_to(1, 0, 2, 6)
    cot_rows([0] + ALONG_BOTH[4:9] + ALONG_Y)
    lax.fori_loop(1, 3, work, 0)
    landed(half, kr.at[4])
    landed(half, kr.at[8])
    kv_to(1, 0, 4, 7)
    for i, (src, dst) in enumerate(weights):
        if i:
            c.to(p.partner(), src, part(dst, i, at_own), hr.at[i])
    landed(kvall.at[0], kr.at[3])
    lax.fori_loop(3, 5, work, 0)
    for k in (1, 3, 2):
        landed(wob, wor.at[k])
        block = wo.at[:, p.zpeer(-k)[1]]
        c.to(sib, block, block, wofr.at[k])

    def arrived(n, _):
        landed(kvall.at[0], kr.at[n])
        return work(n, 0)

    lax.fori_loop(5, 8, arrived, 0)

    for t in range(8):
        parts = []
        for h in range(2):
            rows = pl.ds(h * 1024 + t * 128, 128)
            total = jnp.sum(lsum[rows, :], axis=1, keepdims=True)
            parts.append(acc[rows, :] / total)
        whole = jnp.where(lane < 64, pltpu.roll(parts[0], 64, 1), parts[1])
        o[pl.ds(t * 128, 128), :] = whole
        att_t[pl.ds(t * 128, 128), :] = whole.astype(BF)
    for k in range(1, 8):
        t, dev = p.tp(k)
        block = att_t.at[pl.ds(pl.multiple_of(t * 128, 128), 128)]
        c.to(dev, block, attg.at[p.t], ar)
    own_att = c.here(att_t.at[pl.ds(pl.multiple_of(p.t * 128, 128), 128)], attg.at[p.t])
    cot_rows(ALONG_Z)
    ones = jnp.ones((8, 128), F32)
    for h in range(2):
        lse[h] = jnp.log2(dot_exact(ones, lsum[pl.ds(h * 1024, 1024), :], NT))
    for src, dst in ((o, o_out), (att_t, att_out), (lse, lse_out), (kvall, kv_out)):
        c.own(src, dst)
    for i, (_, dst) in enumerate(weights):
        piece = part(dst, i, from_partner)
        landed(piece, hr.at[i])
        c.to(sib, piece, part(dst, i, at_sib_partner), efr.at[i])
    own_wo.wait()
    landed(wob, wor.at[0])
    for k in (1, 3, 2):
        landed(wob, wofr.at[k])
    load_x.wait()
    own_att.wait()
    landed(attg.at[pl.ds(0, 7)], ar)

    att = jnp.concatenate([attg[t] for t in range(8)], axis=1)
    square = jnp.zeros((128, 1), F32)
    for j in range(4):
        cols = slice(j * 256, (j + 1) * 256)
        value = xv[:, cols].astype(F32) + dot(att, wo[:, :, :, cols].reshape(1024, 256))
        residual[:, cols] = value
        square = square + jnp.sum(value * value, axis=1, keepdims=True)
    factor = lax.rsqrt(square * (1.0 / 1024) + EPS)
    value = (residual[...] * factor * gmv[...]).astype(BF)
    for j in range(4):
        rows = dot(slots_t[j * 384 : (j + 1) * 384, :], value).astype(BF)
        outgoing[j * 8 : (j + 1) * 8] = rows.reshape(8, 48, 1024)

    for i, (_, dst) in enumerate(weights):
        landed(part(dst, i, at_sib), er.at[i])
        landed(part(dst, i, at_sib), efr.at[i])
    landed(grads.at[pl.ds(0, 30)], cr)
    c.done()


def front(*operands):
    shape = jax.ShapeDtypeStruct
    v = pltpu.VMEM
    return pl.pallas_call(
        front_kernel,
        out_shape=(
            shape((32, 48, 1024), BF),
            shape((128, 1024), F32),
            shape((8, 8, 16, 1152), BF),
            shape((128, 1536), BF),
            shape((32, 48, 1024), BF),
            shape((1024, 512), BF),
            shape((1024, 512), BF),
            shape((512, 1024), BF),
            shape((1024, 128), F32),
            shape((1024, 128), BF),
            shape((2, 8, 1024), F32),
            shape((8, 1024, 128), BF),
            shape((2048, 128), BF),
            shape((1024, 256), F32),
            shape((1024, 256), BF),
            shape((1024, 128), F32),
            shape((1024, 128), F32),
            shape((1024, 1024), BF),
            shape((1024, 1024), BF),
            shape((2, 128, 768), BF),
        ),
        in_specs=[HBM] * 17,
        out_specs=(VMEM,) * 4 + (HBM,) * 16,
        scratch_shapes=[
            v((128, 1024), BF),
            v((128, 1024), BF),
            v((8, 128), jnp.int32),
            v((1, 128), jnp.int32),
            v((8, 1024), BF),
            v((8, 512), BF),
            v((8, 512), BF),
            v((8, 1024), BF),
            v((8, 32), BF),
            v((1, 1024), F32),
            v((1, 1024), F32),
            v((1, 64), F32),
            v((1, 64), F32),
            v((1, 128), F32),
            v((8, 16, 128), BF),
            v((80, 128), BF),
            v((8, 128), F32),
            v((8, 128, 1024), BF),
            v((16, 8, 16, 128), BF),
            v((16, 80, 128), BF),
            v((8, 16, 1152), BF),
            v((8, 8, 128), F32),
            v((8, 16, 128), BF),
            v((32, 48, 1024), BF),
            v((1024, 1024), BF),
            v((1024, 1024), BF),
            v((1536, 128), BF),
            v((768, 128), BF),
            v((2, 128, 768), BF),
            v((32, 128), F32),
            v((8, 128), jnp.int32),
            v((128, 1024), BF),
            v((2048, 128), BF),
            v((8, 1024, 128), BF),
            v((1024, 256), F32),
            v((1024, 256), BF),
            v((1024, 128), F32),
            v((1024, 128), F32),
            v((2048, 128), F32),
            v((2048, 128), F32),
            v((1024, 128), F32),
            v((1024, 128), BF),
            v((2, 8, 1024), F32),
            v((8, 128, 128), BF),
            DMA((176,)),
            DMA((5,)),
            DMA((4,)),
            DMA,
            DMA,
            DMA,
            DMA,
            DMA,
            DMA((10,)),
            DMA,
            DMA((3,)),
            DMA((3,)),
            DMA((3,)),
            DMA((4,)),
            DMA((4,)),
            DMA((2,)),
        ],
        compiler_params=params(0, VMEM_MIB),
        name="front",
    )(*operands)


def expert_kernel(
    outgoing,
    residual,
    wo,
    slots,
    grads_in,
    ewg,
    ewu,
    ewd,
    cot_in,
    gain_in,
    branch,
    gat,
    grad_residual_out,
    grad_ffn_out,
    mixed_out,
    dwg_out,
    dwu_out,
    dwd_out,
    dwr_out,
    residual_out,
    cot,
    gain,
    mixed,
    dwg,
    dwu,
    dwd,
    dwr,
    grad_residual,
    grad_ffn,
    rows,
    grads,
    wg,
    wu,
    wd,
    gh,
    gp,
    up,
    hid,
    gl,
    gin,
    back,
    sg,
    su,
    sd,
    rg,
    ru,
    rd,
    ss,
    rr,
    br,
    wr,
):
    p = Place()
    _, sib = p.sibling()
    sem = greet(p.all_chips() + [sib])
    c = Copies(ss)
    own_rows = c.here(outgoing.at[p.chip], rows.at[0])
    local = [c.here(grads_in, grads), c.here(ewd, wd), c.here(ewg, wg), c.here(ewu, wu)]
    load_cot, load_gain = c.here(cot_in, cot), c.here(gain_in, gain)
    c.own(residual, residual_out)
    pl.semaphore_wait(sem, 31 + 1)
    for s in range(1, 32):
        e, dev = p.chips(s)
        c.to(dev, outgoing.at[e], rows.at[s], rr.at[s // 4])
    own_rows.wait()
    for copy in local:
        copy.wait()

    def hidden_grads(j, _):
        block = grads[pl.ds(j * 4, 4)].reshape(192, 1024)
        gh[pl.ds(pl.multiple_of(j * 192, 64), 192), :] = dot(block, wd[...], NT)
        return 0

    lax.fori_loop(0, 8, hidden_grads, 0)

    lane = lax.broadcasted_iota(jnp.int32, (192, 128), 1)
    here = jnp.where(lane == p.chip, 1.0, 0.0)
    router = wo[:, :, :, 1024:].reshape(1024, 128)

    for j in range(8):
        landed(rows.at[pl.ds(0, 4 if j else 3)], rr.at[j])
        block = rows[4 * j : 4 * j + 4].reshape(192, 1024)
        span = pl.ds(j * 192, 192)
        gate_pre = dot(block, wg[...])
        up_pre = dot(block, wu[...])
        logits = jnp.where(lane < 32, dot(block, router), -1e30)
        expo = jnp.exp(logits - jnp.max(logits, axis=1, keepdims=True))
        probs = expo / jnp.sum(expo, axis=1, keepdims=True)
        gate = jnp.sum(probs * here, axis=1, keepdims=True)
        sig = jax.nn.sigmoid(gate_pre)
        act = gate_pre * sig
        hidden = act * up_pre
        grad_hidden = gh[span, :]
        weight = jnp.sum(hidden * grad_hidden, axis=1, keepdims=True) * gate
        grad_hidden = grad_hidden * gate
        grad_gate = (grad_hidden * up_pre * sig * (1.0 + gate_pre * (1.0 - sig))).astype(BF)
        grad_up = (grad_hidden * act).astype(BF)
        grad_logits = (weight * (here - probs)).astype(BF)
        hid[span, :] = (hidden * gate).astype(BF)
        gp[span, :] = grad_gate
        up[span, :] = grad_up
        gl[span, :] = grad_logits
        total = dot(grad_gate, wg[...], NT) + dot(grad_up, wu[...], NT)
        total = total + dot(grad_logits, router, NT)
        gin[4 * j : 4 * j + 4] = total.astype(BF).reshape(4, 48, 1024)
        for s in range(4 * j, 4 * j + 4):
            if s:
                c.to(p.chips(s, -1)[1], gin.at[s], back.at[p.chip], br)
            else:
                own_back = c.here(gin.at[0], back.at[p.chip])

    for m in range(4):
        cols = slice(m * 256, (m + 1) * 256)
        left = rows[:, :, cols].reshape(1536, 256)
        for src, own, sends in ((gp, dwg, sg), (up, dwu, su)):
            value = dot(left, src[...], TN).astype(BF)
            for q in range(2):
                own[q, cols, :] = value[:, q * 128 : (q + 1) * 128]
                sends[q, cols, :] = value[:, (2 + q) * 128 : (3 + q) * 128]
        dwr[cols, :] = dot(left, gl[...], TN)
    for m in range(4):
        cols = slice(m * 256, (m + 1) * 256)
        right = grads[:, :, cols].reshape(1536, 256)
        value = dot(hid[...], right, TN).astype(BF)
        dwd[:, :, cols] = value[:256].reshape(2, 128, 256)
        sd[:, :, cols] = value[256:].reshape(2, 128, 256)
    for i, (src, dst) in enumerate(((sg, rg), (su, ru), (sd, rd))):
        c.to(sib, src, dst, wr.at[i])

    def outputs(j, _):
        block = hid[pl.ds(pl.multiple_of(j * 192, 64), 192), :]
        mixed[pl.ds(j * 4, 4)] = dot(block, wd[...]).astype(BF).reshape(4, 48, 1024)
        return 0

    lax.fori_loop(0, 8, outputs, 0)
    c.own(mixed, mixed_out)
    c.own(dwr, dwr_out)
    for i, (got, own) in enumerate(((rg, dwg), (ru, dwu), (rd, dwd))):
        landed(got, wr.at[i])
        own[...] = (own[...].astype(F32) + got[...].astype(F32)).astype(BF)
    for src, dst in ((dwg, dwg_out), (dwu, dwu_out), (dwd, dwd_out)):
        c.own(src, dst)
    load_cot.wait()
    load_gain.wait()

    landed(back.at[pl.ds(0, 31)], br)
    own_back.wait()
    res = residual[...]
    factor = lax.rsqrt(jnp.mean(res * res, axis=1, keepdims=True) + EPS)
    normed = res * factor
    for j in range(4):
        cols = slice(j * 256, (j + 1) * 256)
        grad_residual[:, cols] = dot(slots[...], back[:, :, cols].reshape(1536, 256))
    grad_mid = grad_residual[...]
    part = jnp.sum(grad_mid * normed, axis=0, keepdims=True)
    grad_ffn[...] = jnp.broadcast_to(part, (8, 1024))
    g = grad_mid * gain[...]
    g = factor * (g - normed * jnp.mean(g * normed, axis=1, keepdims=True))
    g = cot[...].astype(F32) + g
    grad_residual[...] = g
    low = g.astype(BF)
    branch[...] = low
    for t in range(8):
        weights = wo[t][:, :, :1024].reshape(128, 1024)
        gat[t] = dot(low, weights, NT).astype(BF)
    c.own(grad_residual, grad_residual_out)
    c.own(grad_ffn, grad_ffn_out)
    c.done()


def expert_rows(*operands):
    shape = jax.ShapeDtypeStruct
    v = pltpu.VMEM
    return pl.pallas_call(
        expert_kernel,
        out_shape=(
            shape((128, 1024), BF),
            shape((8, 128, 128), BF),
            shape((128, 1024), F32),
            shape((8, 1024), F32),
            shape((32, 48, 1024), BF),
            shape((2, 1024, 128), BF),
            shape((2, 1024, 128), BF),
            shape((2, 128, 1024), BF),
            shape((1024, 128), F32),
            shape((128, 1024), F32),
        ),
        in_specs=[VMEM] * 4 + [HBM] * 6,
        out_specs=(VMEM,) * 2 + (HBM,) * 8,
        scratch_shapes=[
            v((128, 1024), BF),
            v((1, 1024), F32),
            v((32, 48, 1024), BF),
            v((2, 1024, 128), BF),
            v((2, 1024, 128), BF),
            v((2, 128, 1024), BF),
            v((1024, 128), F32),
            v((128, 1024), F32),
            v((8, 1024), F32),
            v((32, 48, 1024), BF),
            v((32, 48, 1024), BF),
            v((1024, 512), BF),
            v((1024, 512), BF),
            v((512, 1024), BF),
            v((1536, 512), F32),
            v((1536, 512), BF),
            v((1536, 512), BF),
            v((1536, 512), BF),
            v((1536, 128), BF),
            v((32, 48, 1024), BF),
            v((32, 48, 1024), BF),
            v((2, 1024, 128), BF),
            v((2, 1024, 128), BF),
            v((2, 128, 1024), BF),
            v((2, 1024, 128), BF),
            v((2, 1024, 128), BF),
            v((2, 128, 1024), BF),
            DMA((96,)),
            DMA((8,)),
            DMA,
            DMA((3,)),
        ],
        compiler_params=params(1, VMEM_MIB),
        name="experts",
    )(*operands)


KB = 256
GB = 1024


def back_kernel(
    branch,
    gat,
    grad_residual_in,
    grad_ffn_in,
    mixed,
    dwg,
    dwu,
    dwd,
    dwr_in,
    residual_in,
    o_in,
    att_in,
    lse_in,
    kv_in,
    qp_in,
    raw_in,
    wqkv_in,
    tabc_in,
    tabs_in,
    normed_in,
    normed_t_in,
    near_in,
    x_in,
    gain_a,
    gain_q,
    gain_k,
    layer_out,
    input_out,
    query_out,
    key_out,
    value_out,
    output_out,
    rows_out,
    misc_out,
    gate_out,
    up_out,
    down_out,
    layer_output,
    grad_input,
    grad_query,
    grad_key,
    grad_value,
    vectors,
    misc,
    out_g,
    out_u,
    out_d,
    grad_residual,
    grad_ffn,
    dwr,
    residual,
    near,
    ypart,
    ypeer,
    o,
    att_t,
    lse,
    kvall,
    qp,
    raw,
    wqkv,
    tabc,
    tabs,
    normed,
    normed_t,
    xv,
    gav,
    gqv,
    gkv,
    own_g,
    own_u,
    own_d,
    rwg,
    rwu,
    rwd,
    yret,
    dqt,
    earlyr,
    gatr,
    dop,
    delta,
    acc,
    bg,
    early,
    dwos,
    dwol,
    dks,
    dkr,
    draw,
    dx,
    dwm,
    part,
    sibr,
    zsend,
    zr,
    dwin,
    d2s,
    d2l,
    ss,
    ar,
    bs,
    fs,
    yr,
    er,
    sr,
    os_,
    ors,
    dsr,
    zrs,
    wrs,
    trs,
    ypr,
):
    p = Place()
    _, sib = p.sibling()
    c = Copies(ss)
    first = [
        c.here(src, dst)
        for src, dst in ((o_in, o), (lse_in, lse), (qp_in, qp), (kv_in, kvall), (att_in, att_t))
    ]
    own_gat = c.here(gat.at[p.t], gatr.at[p.t])
    own_bg = c.here(branch, bg.at[p.t])
    sem = greet(p.all_chips() + p.all_tp() + p.all_gf())
    mirror = p.t * 8 + p.g
    at_home = p.g == p.t

    @pl.when(jnp.logical_not(at_home))
    def _():
        pl.semaphore_signal(sem, inc=1, device_id=(mirror, p.f), device_id_type=MESH)

    pl.semaphore_wait(sem, 31 + 7 + 15 + jnp.where(at_home, 0, 1))
    for k in range(1, 8):
        t, dev = p.tp(k)
        c.to(dev, gat.at[t], gatr.at[p.t], ar)
    own_gat.wait()
    for copy in first:
        copy.wait()
    landed(gatr.at[pl.ds(0, 7)], ar)
    for k in (1, 3, 2):
        c.to(p.zpeer(k)[2], branch, bg.at[p.t], bs.at[k])
    c.to(sib, branch, bg.at[p.t], bs.at[0])
    here = p.y * 4 + p.z
    own_mixed = c.here(mixed.at[pl.ds(0, 2)], yret.at[here])
    owned = ((dwg, own_g, rwg, out_g), (dwu, own_u, rwu, out_u), (dwd, own_d, rwd, out_d))
    owned_copies = []
    for i, (src, mine, got, _) in enumerate(owned):
        c.to(p.partner(), src.at[1 - p.f], got, er.at[i])
        owned_copies.append(c.here(src.at[p.f], mine))

    def outputs(which):
        for m in which:
            c.to(p.plane(m, -1)[1], mixed.at[pl.ds(2 * m, 2)], yret.at[here], yr)

    outputs(ALONG_Z)
    later = (
        (raw_in, raw),
        (wqkv_in, wqkv),
        (tabc_in, tabc),
        (tabs_in, tabs),
        (normed_in, normed),
        (normed_t_in, normed_t),
        (grad_residual_in, grad_residual),
        (residual_in, residual),
        (near_in, near),
        (x_in, xv),
        (gain_a, gav),
        (gain_q, gqv),
        (gain_k, gkv),
    )
    soon = ((grad_ffn_in, grad_ffn), (dwr_in, dwr))
    soon = [c.here(src, dst) for src, dst in soon]
    later = [c.here(src, dst) for src, dst in later]

    lane = lanes(128)
    ones = jnp.ones((8, 128), F32)
    for t in range(8):
        both = gatr[t].astype(F32)
        rows = pl.ds(t * 128, 128)
        dop[rows, :] = jnp.where(lane < 64, 0.0, pltpu.roll(both, 64, 1)).astype(BF)
        dop[pl.ds(1024 + t * 128, 128), :] = jnp.where(lane < 64, 0.0, both).astype(BF)
        prod = both * o[rows, :]
        for h in range(2):
            value = jnp.where((lane < 64) == (h == 0), prod, 0.0)
            delta[h, :, rows] = dot_exact(ones, value, NT)
    dqt[...] = jnp.zeros_like(dqt)

    def work(n):
        def keys(j, _):
            krows = pl.ds(pl.multiple_of(j * KB, KB), KB)
            kvb = kvall[n, krows, :]
            kt = kvb.T[:64, :]
            total = jnp.zeros((KB, 128), F32)
            for i in range(2048 // GB):
                rows = pl.ds(i * GB, GB)
                h, cols = i * GB // 1024, pl.ds(i * GB % 1024, GB)
                q = qp[rows, :]
                d = dop[rows, :]
                w = jnp.exp2(dot(kvb, q, NT) - lse[h, 0:1, cols])
                ds = (w * (dot(kvb, d, NT) - delta[h, 0:1, cols])).astype(BF)
                total = total + dot(w.astype(BF), d) + dot(ds, q)
                dqt[h * 64 : (h + 1) * 64, cols] += dot(kt, ds)
            acc[krows, :] = total
            return 0

        lax.fori_loop(0, 1024 // KB, keys, 0)

    def chunk_x(n):
        work(n)
        dks[n] = acc[...].astype(BF)
        m = MEMBERS.index((0, MEMBERS[n][1]))
        c.to(p.cp(1, 0), dks.at[n], dkr.at[m], sr.at[m])

    def chunk_y(n):
        work(n)
        landed(dkr.at[0], sr.at[n])
        dks[n] = (acc[...] + dkr[n].astype(F32)).astype(BF)
        m = MEMBERS.index((1, MEMBERS[n][1]))
        c.to(p.cp(0, -MEMBERS[n][1]), dks.at[n], dkr.at[m], sr.at[m])

    chunk_x(5)
    outputs(LATER[0:2])
    chunk_x(6)
    outputs(LATER[2:4])
    chunk_x(7)
    for k in (1, 3, 2):
        landed(branch, bs.at[k])
        block = bg.at[p.zpeer(-k)[1]]
        c.to(sib, block, block, fs.at[k])
    outputs(LATER[4:6])
    chunk_x(3)
    outputs(LATER[6:8])
    chunk_y(4)
    outputs(LATER[8:10])
    own_bg.wait()
    landed(branch, bs.at[0])
    for k in (1, 3, 2):
        landed(branch, fs.at[k])
    for j in range(4):
        cols = slice(j * 256, (j + 1) * 256)
        total = jnp.zeros((128, 256), F32)
        for t in range(8):
            total = total + dot(att_t[t * 128 : (t + 1) * 128, :], bg[t, :, cols], TN)
        for r in range(16):
            block = total[r * 8 : (r + 1) * 8, :]
            both = [block[:, :128], block[:, 128:]]
            early[r, j * 16 : (j + 1) * 16, :] = jnp.concatenate(both, axis=0).astype(BF)
    for copy in soon:
        copy.wait()
    spot = lax.broadcasted_iota(jnp.int32, (128, 128), 0)
    same = jnp.logical_and(lax.div(spot, 16) == lax.div(lane, 8), lax.rem(spot, 8) == lax.rem(lane, 8))
    picks = [
        jnp.where(jnp.logical_and(same, lax.rem(lax.div(spot, 8), 2) == f), 1.0, 0.0)
        for f in range(2)
    ]
    sub16 = lax.broadcasted_iota(jnp.int32, (16, 128), 0)

    def rows_of(value, f):
        return jnp.concatenate(
            [value[(2 * t + f) * 8 : (2 * t + f) * 8 + 8, :] for t in range(8)], axis=0
        )

    for g in range(8):
        span = slice(g * 128, (g + 1) * 128)
        value = dwr[span, :]
        for f in range(2):
            early[g * 2 + f, 64:128, :] = rows_of(value, f).astype(BF)
            line = dot_exact(grad_ffn[0:1, span], picks[f])
            early[g * 2 + f, 128:144, :] = jnp.where(sub16 == 0, line, 0.0).astype(BF)
    me = p.g * 2 + p.f
    for k in range(1, 16):
        r, dev = p.gf(k)
        c.to(dev, early.at[r], earlyr.at[me], ors)
    own_early = c.here(early.at[me], earlyr.at[me])

    chunk_y(1)
    outputs(LATER[10:12])
    chunk_y(2)
    work(0)

    for copy in later:
        copy.wait()
    head_gains = (
        jnp.concatenate([gqv[...], gqv[...]], axis=1),
        jnp.concatenate([gkv[...], jnp.ones((1, 64), F32)], axis=1),
    )

    def through(i, rows, grad):
        cosine, sine = tabc[rows, :], tabs[rows, :]
        value = raw[rows, i * 128 : (i + 1) * 128]
        grad = grad * cosine - swap(grad) * sine
        factor = lax.rsqrt(head_mean(value * value) + EPS)
        value = value * factor
        total = jnp.sum(grad * value, axis=0, keepdims=True)
        grad = grad * head_gains[i]
        return total, factor * (grad - value * head_mean(grad * value))

    gains_q = jnp.zeros((1, 128), F32)
    for t in range(8):
        rows = slice(t * 128, (t + 1) * 128)
        total, value = through(0, rows, dqt[:, rows].T * 0.125)
        gains_q = gains_q + total
        draw[rows, 0:128] = value.astype(BF)
    for n in (0, 5, 7, 6):
        landed(dkr.at[0], sr.at[n])
    gains_k = jnp.zeros((1, 128), F32)
    for t in range(8):
        rows = slice(t * 128, (t + 1) * 128)
        whole = acc[rows, :]
        for n in (0, 5, 7, 6):
            whole = whole + dkr[n, rows, :].astype(F32)
        total, value = through(1, rows, whole * LN2)
        gains_k = gains_k + total
        draw[rows, 128:256] = jnp.where(lane < 64, value, whole).astype(BF)
    part[...] = jnp.zeros_like(part)

    def input_grad(core, z):
        rows = pl.ds(pl.multiple_of((z * 2 + core) * 128, 128), 128)
        left = draw[rows, :]
        for j in range(4):
            cols = slice(j * 256, (j + 1) * 256)
            value = dot(left, wqkv[cols, :], NT)
            prod = value * normed[rows, cols].astype(F32)
            part[0:1, cols] += jnp.sum(prod, axis=0, keepdims=True)
            dx[core, z, :, cols] = value.astype(BF)

    for k in (1, 3, 2, 0):
        z = lax.rem(p.z + k, 4)
        input_grad(1 - p.core, z)
        c.to(sib, dx.at[1 - p.core, z], sibr.at[z], dsr.at[k])
    for k in (1, 3, 2):
        z, _, dev = p.zpeer(k)
        input_grad(p.core, z)
        landed(sibr.at[0], dsr.at[k])
        zsend[k] = (dx[p.core, z].astype(F32) + sibr[z].astype(F32)).astype(BF)
        c.to(dev, zsend.at[k], zr.at[k], zrs.at[k])
    input_grad(p.core, p.z)

    part[0:1, :] = part[0:1, :] / gav[...]
    gains = jnp.concatenate([gains_q, jnp.where(lanes(1) < 64, gains_k, 0.0)], axis=1)
    wide16 = lax.broadcasted_iota(jnp.int32, (16, 256), 0)
    for j in range(8):
        g = lax.rem(p.g + j, 8)
        rows = pl.ds(pl.multiple_of(g * 128, 128), 128)
        value = dot(normed_t[rows, :], draw[...])
        for f in range(2):
            dwm[g * 2 + f, 0:64, :] = rows_of(value, f).astype(BF)
            line = dot_exact(part[0:1, rows], picks[f])
            line = jnp.concatenate([line, jnp.zeros((1, 128), F32)], axis=1)
            line = jnp.where(wide16 == 0, gains, jnp.where(wide16 == 1, line, 0.0))
            dwm[g * 2 + f, 64:80, :] = line.astype(BF)
        if j:
            for f in range(2):
                c.to((g * 8 + p.t, f), dwm.at[g * 2 + f], dwin.at[me], wrs)
        else:
            c.to(p.partner(), dwm.at[g * 2 + 1 - p.f], dwin.at[me], wrs)
            own_dw = c.here(dwm.at[me], dwin.at[me])

    own_mixed.wait()
    landed(yret.at[pl.ds(0, 15)], yr)
    for j in range(4):
        cols = slice(j * 256, (j + 1) * 256)
        ypart[:, cols] = dot(near[1], yret[:, 1, :, cols].reshape(768, 256)).astype(BF)
    c.to(p.cp(1, 0), ypart, ypeer, ypr)
    for j in range(4):
        cols = slice(j * 256, (j + 1) * 256)
        residual[:, cols] += dot(near[0], yret[:, 0, :, cols].reshape(768, 256))

    landed(sibr.at[0], dsr.at[0])
    whole = dx[p.core, p.z].astype(F32) + sibr[p.z].astype(F32)
    for i, (_, mine, got, out) in enumerate(owned):
        owned_copies[i].wait()
        landed(got, er.at[i])
        out[...] = mine[...].astype(F32) + got[...].astype(F32)
    for src, dst in ((out_g, gate_out), (out_u, up_out), (out_d, down_out)):
        c.own(src, dst)
    own_early.wait()
    landed(earlyr.at[pl.ds(0, 15)], ors)
    before = earlyr[0].astype(F32)
    for r in range(1, 16):
        before = before + earlyr[r].astype(F32)
    for i in range(8):
        dwos[:, i * 128 : (i + 1) * 128] = before[i * 8 : (i + 1) * 8, :]

    @pl.when(jnp.logical_not(at_home))
    def _():
        pltpu.make_async_remote_copy(
            src_ref=dwos,
            dst_ref=dwol,
            send_sem=os_.at[0],
            recv_sem=os_.at[1],
            device_id=(mirror, p.f),
            device_id_type=MESH,
        ).start()

    @pl.when(at_home)
    def _():
        pltpu.make_async_copy(dwos, dwol, os_.at[2]).start()

    own_dw.wait()
    landed(dwin.at[pl.ds(0, 15)], wrs)
    total = dwin[0].astype(F32)
    for r in range(1, 16):
        total = total + dwin[r].astype(F32)
    eight = lax.broadcasted_iota(jnp.int32, (8, 128), 0)
    for t in range(8):
        d2s[t, 0:8, :] = total[t * 8 : (t + 1) * 8, :]
        turn = (128 - 8 * t) % 128
        lines = [total[65:66, 0:128], before[128:129, :]]
        lines = [pltpu.roll(jnp.broadcast_to(v, (8, 128)), turn, 1) if turn else v for v in lines]
        lines = jnp.where(eight == 0, total[64:65, 0:128], jnp.where(eight == 2, lines[0], lines[1]))
        lines = jnp.where(eight == 1, total[64:65, 128:256], lines)
        d2s[t, 8:16, 0:128] = lines
        d2s[t, 8:16, 128:256] = before[64 + t * 8 : 72 + t * 8, :]
    for k in range(1, 8):
        t, dev = p.tp(k)
        c.to(dev, d2s.at[t], d2l.at[p.t], trs)
    own_d2 = c.here(d2s.at[p.t], d2l.at[p.t])

    for k in (1, 3, 2):
        landed(zr.at[0], zrs.at[k])
        whole = whole + zr[k].astype(F32)
    xf = xv[...].astype(F32)
    factor = lax.rsqrt(jnp.mean(xf * xf, axis=1, keepdims=True) + EPS)
    n = xf * factor
    g = whole * gav[...]
    g = factor * (g - n * jnp.mean(g * n, axis=1, keepdims=True))
    grad_input[...] = grad_residual[...] + g
    c.own(grad_input, input_out)
    landed(ypeer, ypr)
    layer_output[...] = (residual[...] + ypeer[...].astype(F32)).astype(BF)
    c.own(layer_output, layer_out)

    @pl.when(jnp.logical_not(at_home))
    def _():
        landed(dwos, os_.at[0])
        landed(dwol, os_.at[1])

    @pl.when(at_home)
    def _():
        landed(dwol, os_.at[2])

    c.own(dwol, output_out)
    own_d2.wait()
    landed(d2l.at[pl.ds(0, 7)], trs)
    low8 = lanes(8) < 64
    totals = [jnp.zeros((8, 128), F32)] * 2
    for t in range(8):
        grad_query[:, t * 128 : (t + 1) * 128] = d2l[t, 0:8, 0:128]
        totals = [totals[i] + d2l[t, 8:16, i * 128 : (i + 1) * 128] for i in range(2)]
    for i in range(4):
        one, two = d2l[2 * i, 0:8, 128:256], d2l[2 * i + 1, 0:8, 128:256]
        cols = slice(i * 128, (i + 1) * 128)
        grad_key[:, cols] = jnp.where(low8, one, pltpu.roll(two, 64, 1))
        grad_value[:, cols] = jnp.where(low8, pltpu.roll(one, 64, 1), two)
    both = totals[0] + pltpu.roll(totals[0], 64, 1)
    vectors[...] = jnp.where(eight == 0, both, totals[0])
    misc[...] = totals[1]
    last = (
        (grad_query, query_out),
        (grad_key, key_out),
        (grad_value, value_out),
        (vectors, rows_out),
        (misc, misc_out),
    )
    for src, dst in last:
        c.own(src, dst)
    c.done()


def back(*operands):
    shape = jax.ShapeDtypeStruct
    v = pltpu.VMEM
    return pl.pallas_call(
        back_kernel,
        out_shape=(
            shape((128, 1024), BF),
            shape((128, 1024), F32),
            shape((8, 1024), F32),
            shape((8, 512), F32),
            shape((8, 512), F32),
            shape((8, 1024), F32),
            shape((8, 128), F32),
            shape((8, 128), F32),
            shape((1024, 128), F32),
            shape((1024, 128), F32),
            shape((128, 1024), F32),
        ),
        in_specs=[VMEM] * 2 + [HBM] * 24,
        out_specs=(HBM,) * 11,
        scratch_shapes=[
            v((128, 1024), BF),
            v((128, 1024), F32),
            v((8, 1024), F32),
            v((8, 512), F32),
            v((8, 512), F32),
            v((8, 128), F32),
            v((8, 128), F32),
            v((1024, 128), F32),
            v((1024, 128), F32),
            v((128, 1024), F32),
            v((128, 1024), F32),
            v((8, 1024), F32),
            v((1024, 128), F32),
            v((128, 1024), F32),
            v((2, 128, 768), BF),
            v((128, 1024), BF),
            v((128, 1024), BF),
            v((1024, 128), F32),
            v((1024, 128), BF),
            v((2, 8, 1024), F32),
            v((8, 1024, 128), BF),
            v((2048, 128), BF),
            v((1024, 256), F32),
            v((1024, 256), BF),
            v((1024, 128), F32),
            v((1024, 128), F32),
            v((1024, 1024), BF),
            v((1024, 1024), BF),
            v((128, 1024), BF),
            v((1, 1024), F32),
            v((1, 64), F32),
            v((1, 64), F32),
            v((1024, 128), BF),
            v((1024, 128), BF),
            v((128, 1024), BF),
            v((1024, 128), BF),
            v((1024, 128), BF),
            v((128, 1024), BF),
            v((16, 2, 48, 1024), BF),
            v((128, 1024), F32),
            v((16, 144, 128), BF),
            v((8, 128, 128), BF),
            v((2048, 128), BF),
            v((2, 8, 1024), F32),
            v((1024, 128), F32),
            v((8, 128, 1024), BF),
            v((16, 144, 128), BF),
            v((8, 1024), F32),
            v((8, 1024), F32),
            v((8, 1024, 128), BF),
            v((8, 1024, 128), BF),
            v((1024, 256), BF),
            v((2, 4, 128, 1024), BF),
            v((16, 80, 256), BF),
            v((8, 1024), F32),
            v((4, 128, 1024), BF),
            v((4, 128, 1024), BF),
            v((4, 128, 1024), BF),
            v((16, 80, 256), BF),
            v((8, 16, 256), F32),
            v((8, 16, 256), F32),
            DMA((128,)),
            DMA,
            DMA((4,)),
            DMA((4,)),
            DMA,
            DMA((3,)),
            DMA((8,)),
            DMA((3,)),
            DMA,
            DMA((4,)),
            DMA((4,)),
            DMA,
            DMA,
            DMA,
        ],
        compiler_params=params(2, VMEM_MIB),
        name="back",
    )(*operands)


def outputs_kernel(count, *refs):
    ins, outs, held = refs[:count], refs[count : 2 * count], refs[2 * count : 3 * count]
    sems = refs[-1]
    loads = [pltpu.make_async_copy(ins[i], held[i], sems.at[0, i]) for i in range(count)]
    for copy in loads:
        copy.start()
    stores = [
        pltpu.make_async_copy(held[i], outs[i], sems.at[1, i]) for i in range(count - 1)
    ]
    for i in range(count - 1):
        loads[i].wait()
        stores[i].start()
    loads[-1].wait()
    outs[-1][...] = held[-1][:, :32]
    for copy in stores:
        copy.wait()


def to_outputs(*arrays):
    count = len(arrays)
    shapes = [jax.ShapeDtypeStruct(a.shape, a.dtype) for a in arrays[:-1]]
    shapes.append(jax.ShapeDtypeStruct((8, 32), F32))
    return pl.pallas_call(
        functools.partial(outputs_kernel, count),
        out_shape=tuple(shapes),
        in_specs=[HBM] * count,
        out_specs=(HBM,) * (count - 1) + (VMEM,),
        scratch_shapes=[pltpu.VMEM(a.shape, a.dtype) for a in arrays] + [DMA((2, count))],
        compiler_params=pltpu.CompilerParams(vmem_limit_bytes=VMEM_MIB * 2**20),
        name="outputs",
    )(*arrays)


RATES = np.power(50000.0, -(np.arange(128) % 32) / 32.0).astype(np.float32).reshape(1, 128)


def local(
    layer_input,
    positions,
    routes,
    attn_gain,
    w_query,
    w_key,
    w_value,
    query_gain,
    key_gain,
    w_output,
    ffn_gain,
    w_router,
    w_gate,
    w_up,
    w_down,
    cotangent,
):
    x = layer_input[0]
    cot = cotangent[0]
    gain_a = attn_gain.reshape(1, 1024)
    gain_m = ffn_gain.reshape(1, 1024)
    gain_q = query_gain.reshape(1, 64)
    gain_k = key_gain.reshape(1, 64)
    (outgoing, residual, wo, slots, grads, ewg, ewu, ewd, *kept) = front(
        x,
        cot,
        routes[0].T,
        positions,
        w_query,
        w_key,
        w_value,
        w_output,
        w_router,
        gain_a,
        gain_m,
        gain_q,
        gain_k,
        jnp.asarray(RATES),
        w_gate[0],
        w_up[0],
        w_down[0],
    )
    passed = expert_rows(outgoing, residual, wo, slots, grads, ewg, ewu, ewd, cot, gain_m)
    results = back(*passed, *kept, x, gain_a, gain_q, gain_k)
    vectors = results[6]
    (
        layer_output,
        grad_input,
        grad_query,
        grad_key,
        grad_value,
        grad_output,
        grad_gate,
        grad_up,
        grad_down,
        grad_router,
    ) = to_outputs(*results[:6], *results[8:], results[7])
    return (
        layer_output[None],
        grad_input[None],
        vectors[2, :8],
        grad_query,
        grad_key,
        grad_value,
        vectors[0, :64],
        vectors[1, :64],
        grad_output,
        vectors[3, :8],
        grad_router,
        grad_gate[None],
        grad_up[None],
        grad_down[None],
    )


def solution(mesh):
    rows = P(("ctx", "fsdp"), None)
    vector = P(("ctx", "fsdp"))
    tokens = P("fsdp", "ctx", None)
    return jax.shard_map(
        local,
        mesh=mesh,
        in_specs=(
            tokens,
            P("fsdp", "ctx"),
            tokens,
            P(),
            rows,
            rows,
            rows,
            P(),
            P(),
            rows,
            P(),
            rows,
            P("ctx", None, "fsdp"),
            P("ctx", None, "fsdp"),
            P("ctx", "fsdp", None),
            tokens,
        ),
        out_specs=(
            tokens,
            tokens,
            vector,
            rows,
            rows,
            rows,
            P(),
            P(),
            rows,
            vector,
            rows,
            P("ctx", None, "fsdp"),
            P("ctx", None, "fsdp"),
            P("ctx", "fsdp", None),
        ),
        check_vma=False,
    )
```

```python
import functools

import jax
import jax.numpy as jnp
import numpy as np
from jax import lax
from jax.experimental import pallas as pl
from jax.experimental.pallas import tpu as pltpu
from jax.sharding import PartitionSpec as P

EPS = 1e-06
LOG2E = 1.4426950408889634
LN2 = 0.6931471805599453
MESH = pl.DeviceIdType.MESH
VMEM_MIB = 62
BF = jnp.bfloat16
F32 = jnp.float32
NN = (((1,), (0,)), ((), ()))
NT = (((1,), (1,)), ((), ()))
TN = (((0,), (0,)), ((), ()))
HBM = pl.BlockSpec(memory_space=pltpu.HBM)
VMEM = pl.BlockSpec(memory_space=pltpu.VMEM)
DMA = pltpu.SemaphoreType.DMA
MEMBERS = ((0, 0), (0, 1), (0, 3), (1, 0), (0, 2), (1, 1), (1, 3), (1, 2))
PLANE = ((0, 0), (2, 2), (1, 1), (3, 3), (1, 3), (3, 1), (0, 1), (2, 3))
PLANE = PLANE + ((0, 3), (2, 1), (1, 0), (3, 2), (3, 0), (1, 2), (0, 2), (2, 0))
CHIPS = tuple((a, b, c) for b, c in PLANE for a in range(2))
ALONG_Z = [m for m in range(1, 16) if PLANE[m][0] == 0]
ALONG_Y = [m for m in range(1, 16) if PLANE[m][1] == 0]
ALONG_BOTH = [m for m in range(1, 16) if PLANE[m][0] and PLANE[m][1]]


def dot(left, right, dims=NN):
    return lax.dot_general(left, right, dims, preferred_element_type=F32)


def dot_exact(left, right, dims=NN):
    return lax.dot_general(
        left, right, dims, precision=lax.Precision.HIGHEST, preferred_element_type=F32
    )


class Place:
    def __init__(self):
        ctx = lax.axis_index("ctx")
        self.f = lax.axis_index("fsdp")
        self.t = lax.rem(ctx, 8)
        self.g = lax.div(ctx, 8)
        self.core = lax.rem(ctx, 2)
        self.z = lax.rem(lax.div(ctx, 2), 4)
        self.y = lax.rem(self.g, 4)
        self.xl = lax.div(self.g, 4)
        self.chip = lax.div(ctx, 2)

    def tp(self, k):
        t = lax.rem(self.t + k, 8)
        return t, (self.g * 8 + t, self.f)

    def cp(self, a, b):
        g = lax.rem(self.xl + a, 2) * 4 + lax.rem(self.y + b + 4, 4)
        return (g * 8 + self.t, self.f)

    def gf(self, k):
        r = lax.rem(self.g * 2 + self.f + k, 16)
        return r, (lax.div(r, 2) * 8 + self.t, lax.rem(r, 2))

    def chips(self, s, sign=1):
        a, b, c = CHIPS[s]
        xl = lax.rem(self.xl + a, 2)
        y = lax.rem(self.y + sign * b + 4, 4)
        z = lax.rem(self.z + sign * c + 4, 4)
        e = (xl * 4 + y) * 4 + z
        return e, (e * 2 + self.core, self.f)

    def plane(self, m, sign=1):
        b, c = PLANE[m]
        i = lax.rem(self.y + sign * b + 4, 4) * 4 + lax.rem(self.z + sign * c + 4, 4)
        e = self.xl * 16 + i
        return i, (e * 2 + self.core, self.f)

    def zpeer(self, c):
        z = lax.rem(self.z + c + 4, 4)
        t = z * 2 + self.core
        return z, t, (self.g * 8 + t, self.f)

    def sibling(self):
        t = self.z * 2 + 1 - self.core
        return t, (self.g * 8 + t, self.f)

    def partner(self):
        return (self.g * 8 + self.t, 1 - self.f)

    def all_tp(self):
        return [self.tp(k)[1] for k in range(1, 8)]

    def all_gf(self):
        return [self.gf(k)[1] for k in range(1, 16)]

    def all_chips(self):
        return [self.chips(s)[1] for s in range(1, 32)]


def greet(devices):
    sem = pltpu.get_barrier_semaphore()
    for d in devices:
        pl.semaphore_signal(sem, inc=1, device_id=d, device_id_type=MESH)
    return sem


class Copies:
    def __init__(self, sems):
        self.sems, self.count, self.begun = sems, 0, []

    def next(self):
        self.count += 1
        return self.sems.at[self.count - 1]

    def to(self, device, src, dst, recv):
        copy = pltpu.make_async_remote_copy(
            src_ref=src,
            dst_ref=dst,
            send_sem=self.next(),
            recv_sem=recv,
            device_id=device,
            device_id_type=MESH,
        )
        copy.start()
        self.begun.append(copy.wait_send)

    def own(self, src, dst):
        copy = pltpu.make_async_copy(src, dst, self.next())
        copy.start()
        self.begun.append(copy.wait)

    def here(self, src, dst):
        copy = pltpu.make_async_copy(src, dst, self.next())
        copy.start()
        return copy

    def done(self):
        for wait in self.begun:
            wait()


def landed(ref, sem):
    pltpu.make_async_copy(ref, ref, sem).wait()


def params(number, mib):
    return pltpu.CompilerParams(
        collective_id=number, has_side_effects=True, vmem_limit_bytes=mib * 2**20
    )


def lanes(rows):
    return lax.broadcasted_iota(jnp.int32, (rows, 128), 1)


def swap(v):
    low = lax.rem(lanes(v.shape[0]), 64) < 32
    return jnp.where(low, pltpu.roll(v, 96, 1), pltpu.roll(v, 32, 1))


def head_mean(v):
    row = lax.broadcasted_iota(jnp.int32, (128, 128), 0)
    same = lax.div(row, 64) == lax.div(lanes(128), 64)
    return dot_exact(v, jnp.where(same, 1.0 / 64, 0.0))


def cos_sin(angle):
    k = jnp.floor(angle * 0.6366197723675814 + 0.5)
    r = angle - k * 1.5703125
    r = r - k * 4.837512969970703125e-4
    r = r - k * 7.54978995489188216e-8
    r2 = r * r
    s = r + r * r2 * (-1.6666654611e-1 + r2 * (8.3321608736e-3 + r2 * -1.9515295891e-4))
    c = 4.166664568298827e-2 + r2 * (-1.388731625493765e-3 + r2 * 2.443315711809948e-5)
    c = 1.0 - 0.5 * r2 + r2 * r2 * c
    q = k - 4.0 * jnp.floor(k * 0.25)
    odd = jnp.logical_or(q == 1.0, q == 3.0)
    cosine, sine = jnp.where(odd, s, c), jnp.where(odd, c, s)
    cosine = jnp.where(jnp.logical_or(q == 1.0, q == 2.0), -cosine, cosine)
    sine = jnp.where(q >= 2.0, -sine, sine)
    return cosine, sine


def column(row):
    at = lax.broadcasted_iota(jnp.int32, (128, 128), 0) == lanes(128)
    return jnp.sum(jnp.where(at, row, 0.0), axis=1, keepdims=True)


QB = 256
UNROLL = 4


def front_kernel(
    x,
    cot,
    routes,
    pos,
    wq,
    wk,
    wv,
    wo_own,
    wr_own,
    gain_a,
    gain_m,
    gain_q,
    gain_k,
    rates,
    eg,
    eu,
    ed,
    outgoing,
    residual,
    wo,
    slots,
    grads,
    ewg,
    ewu,
    ewd,
    o_out,
    att_out,
    lse_out,
    kv_out,
    qp_out,
    raw_out,
    wqkv_out,
    tabc_out,
    tabs_out,
    normed_out,
    normed_t_out,
    near_out,
    xv,
    cotv,
    routev,
    posv,
    wqv,
    wkv,
    wvv,
    wov,
    wrv,
    gav,
    gmv,
    gqv,
    gkv,
    ratev,
    wps,
    wops,
    posf,
    xg,
    wg,
    wog,
    wob,
    posg,
    wst,
    cots,
    normed,
    normed_t,
    slots_t,
    slots_p,
    near,
    place_p,
    routep,
    cotp,
    qp,
    kvall,
    raw,
    wqkv,
    tabc,
    tabs,
    acc,
    lsum,
    o,
    att_t,
    lse,
    attg,
    ss,
    xr,
    fr,
    pr,
    wr,
    gr,
    orr,
    cr,
    kr,
    ar,
    er,
    hr,
    efr,
    wor,
    wofr,
    xpr,
):
    p = Place()
    _, sib = p.sibling()
    me = p.g * 2 + p.f
    c = Copies(ss)
    small = (
        (wq, wqv),
        (wk, wkv),
        (wv, wvv),
        (wo_own, wov),
        (wr_own, wrv),
        (pos, posv),
        (routes, routev),
        (gain_q, gqv),
        (gain_k, gkv),
        (rates, ratev),
        (gain_a, gav),
        (gain_m, gmv),
    )
    loads = [c.here(src, dst) for src, dst in small]
    own_x = c.here(x, xg.at[p.t])
    load_cot = c.here(cot, cotv)
    load_x = c.here(x, xv)
    sem = greet(p.all_chips() + p.all_tp() + p.all_gf())
    for copy in loads:
        copy.wait()

    low8 = lanes(8) < 64
    for t in range(8):
        pair = slice(t // 2 * 128, t // 2 * 128 + 128)
        key, value = wkv[:, pair].astype(F32), wvv[:, pair].astype(F32)
        if t % 2:
            both = jnp.where(low8, pltpu.roll(key, 64, 1), value)
        else:
            both = jnp.where(low8, key, pltpu.roll(value, 64, 1))
        query = wqv[:, t * 128 : (t + 1) * 128].astype(F32)
        wps[t] = jnp.concatenate([query, both], axis=0).astype(BF)
    for i in range(4):
        pair = [wov[:, (2 * i + j) * 128 : (2 * i + j + 1) * 128].astype(F32) for j in range(2)]
        wops[i * 16 : (i + 1) * 16, :] = jnp.concatenate(pair, axis=0).astype(BF)
    router = jnp.concatenate([wrv[...].astype(F32), jnp.zeros((8, 96), F32)], axis=1)
    wops[64:80, :] = jnp.concatenate([router, jnp.zeros((8, 128), F32)], axis=0).astype(BF)
    posf[...] = jnp.broadcast_to(posv[...].astype(F32), (8, 128))
    own = [
        c.here(wps.at[p.t], wst.at[p.t]),
        c.here(posf, posg.at[p.t]),
        c.here(wops, wog.at[me]),
    ]
    pl.semaphore_wait(sem, 31 + 7 + 15)

    for k in range(1, 8):
        t, dev = p.tp(k)
        c.to(dev, wps.at[t], wst.at[p.t], wr)
    for k in (1, 3):
        c.to(p.zpeer(k)[2], x, xg.at[p.t], xr.at[k])
    c.to(sib, x, xg.at[p.t], xr.at[0])
    c.to(p.cp(1, 0), routev, routep, xpr.at[0])
    c.to(p.cp(1, 0), cot, cotp, xpr.at[1])
    for k in range(1, 8):
        c.to(p.tp(k)[1], posf, posg.at[p.t], pr)
    for copy in own:
        copy.wait()

    row = lax.broadcasted_iota(jnp.int32, (128, 128), 0)
    col = lanes(128)

    def places(ref):
        number = lax.broadcasted_iota(jnp.int32, (32, 128), 0)
        hits = jnp.zeros((32, 128), F32)
        for k in range(8):
            hits = hits + jnp.where(ref[k : k + 1, :] == number, 1.0, 0.0)
        before = jnp.where(row < col, 1.0, 0.0).astype(BF)
        return jnp.where(hits > 0, dot(hits.astype(BF), before), -1.0)

    def slot_rows(place):
        within = lax.broadcasted_iota(jnp.int32, (48, 128), 0).astype(F32)
        return jnp.where(place == within, 1.0, 0.0).astype(BF)

    place = places(routev)
    for e in range(32):
        slots_t[e * 48 : (e + 1) * 48, :] = slot_rows(place[e : e + 1, :])
    load_cot.wait()

    def cot_rows(which):
        for m in which:
            i, dev = p.plane(m)
            for a, (ref, values) in enumerate(((slots_t, cotv), (slots_p, cotp))):
                first = i + p.xl * 16 if a == 0 else i
                mine = ref[pl.ds(pl.multiple_of(first * 48, 16), 48), :]
                cots[2 * m + a] = dot(mine, values[...]).astype(BF)
            pair = pl.ds(2 * m, 2)
            if m:
                c.to(dev, cots.at[pair], grads.at[pair], cr)
            else:
                c.own(cots.at[pair], grads.at[pair])

    landed(wst.at[pl.ds(0, 7)], wr)
    own_wg = c.here(wst, wg.at[me])
    for k in range(1, 16):
        c.to(p.gf(k)[1], wst, wg.at[me], gr)
    for k in range(1, 16):
        c.to(p.gf(k)[1], wops, wog.at[me], orr)
    at_own = pl.ds(pl.multiple_of(p.f * 128, 128), 128)
    at_sib = pl.ds(pl.multiple_of(256 + p.f * 128, 128), 128)
    from_partner = pl.ds(pl.multiple_of((1 - p.f) * 128, 128), 128)
    at_sib_partner = pl.ds(pl.multiple_of(256 + (1 - p.f) * 128, 128), 128)

    def part(ref, i, span):
        return ref.at[span, :] if i == 2 else ref.at[:, span]

    weights = ((eg, ewg), (eu, ewu), (ed, ewd))
    for i, (src, dst) in enumerate(weights):
        c.to(sib, src, part(dst, i, at_sib), er.at[i])
        c.own(src, part(dst, i, at_own))
    landed(routep, xpr.at[0])
    place_p[...] = places(routep)
    here = place_p[pl.ds(pl.multiple_of(p.xl * 16, 16), 16), :]
    for e in range(16):
        slots_p[e * 48 : (e + 1) * 48, :] = slot_rows(here[e : e + 1, :])
    for j in range(12):
        cols = slice(j * 128, (j + 1) * 128)
        slots[:, cols] = slots_t[cols, :].astype(F32).T.astype(BF)
    for j in range(6):
        cols = slice(j * 128, (j + 1) * 128)
        near[1, :, cols] = slots_p[cols, :].astype(F32).T.astype(BF)
    near[0] = slots[:, pl.ds(pl.multiple_of(p.xl * 768, 128), 768)]
    c.own(near, near_out)
    landed(cotp, xpr.at[1])

    def pass_on(k, n):
        landed(xg.at[0], xr.at[k])
        t = p.zpeer(-k)[1]
        half = pl.ds(0 if k == 1 else 64, 64)
        c.to(p.zpeer(k)[2], xg.at[t, half], xg.at[t, half], xr.at[n])
        c.to(sib, xg.at[t], xg.at[t], fr.at[k])
        return t

    t1 = pass_on(1, 2)
    t3 = pass_on(3, 4)
    cot_rows(ALONG_Z + ALONG_Y)
    c.to(p.partner(), eg, part(ewg, 0, at_own), hr.at[0])

    landed(posg.at[pl.ds(0, 7)], pr)
    signed = jnp.where(lax.rem(col, 64) < 32, -1.0, 1.0)
    for t in range(8):
        cosine, sine = cos_sin(column(posg[t, 0:1, :]) * ratev[...])
        tabc[t * 128 : (t + 1) * 128, :] = cosine
        tabs[t * 128 : (t + 1) * 128, :] = sine * signed

    own_wg.wait()
    landed(wg.at[pl.ds(0, 15)], gr)

    def columns(g, _):
        for t in range(8):
            one, two = wg[2 * g, t].astype(F32), wg[2 * g + 1, t].astype(F32)
            both = [jnp.concatenate([one[i : i + 8], two[i : i + 8]], axis=0) for i in (0, 8)]
            at = pl.ds(pl.multiple_of((g * 8 + t) * 16, 16), 16)
            wqkv[at, :] = jnp.concatenate(both, axis=1).astype(BF)
        return 0

    lax.fori_loop(0, 8, columns, 0)

    landed(wog.at[pl.ds(0, 15)], orr)

    def output_rows(g, _):
        one, two = wog[2 * g].astype(F32), wog[2 * g + 1].astype(F32)
        for i in range(9):
            both = [one[i * 8 : i * 8 + 8], two[i * 8 : i * 8 + 8]]
            wob[g, :, i * 128 : (i + 1) * 128] = jnp.concatenate(both, axis=0).astype(BF)
        return 0

    lax.fori_loop(0, 8, output_rows, 0)
    for k in (1, 3, 2):
        c.to(p.zpeer(k)[2], wob, wo.at[:, p.t], wor.at[k])
    c.to(sib, wob, wo.at[:, p.t], wor.at[0])
    own_wo = c.here(wob, wo.at[:, p.t])

    lane = lanes(128)
    head_q = jnp.concatenate([gqv[...], gqv[...]], axis=1)
    head_k = jnp.concatenate([gkv[...], jnp.ones((1, 64), F32)], axis=1)

    def project(t):
        rows = pl.ds(pl.multiple_of(t * 128, 128), 128)
        value = xg[t].astype(F32)
        factor = lax.rsqrt(jnp.mean(value * value, axis=1, keepdims=True) + EPS)
        value = (value * factor * gav[...]).astype(BF)
        normed[rows, :] = value
        normed_t[:, rows] = value.astype(F32).T.astype(BF)
        out = dot(value, wqkv[...])
        raw[rows, :] = out
        cosine, sine = tabc[rows, :], tabs[rows, :]
        q, k = out[:, :128], out[:, 128:]
        q = q * lax.rsqrt(head_mean(q * q) + EPS) * head_q
        q = ((q * cosine + swap(q) * sine) * (0.125 * LOG2E)).astype(BF).astype(F32)
        qp[rows, :] = jnp.where(lane < 64, q, 0.0).astype(BF)
        second = pl.ds(pl.multiple_of(1024 + t * 128, 128), 128)
        qp[second, :] = jnp.where(lane < 64, pltpu.roll(q, 64, 1), 0.0).astype(BF)
        n = k * lax.rsqrt(head_mean(k * k) + EPS) * head_k
        n = n * cosine + swap(n) * sine
        kvall[0, rows, :] = jnp.where(lane < 64, n, k).astype(BF)

    own_x.wait()
    project(p.t)
    t2 = p.zpeer(2)[1]
    landed(xg.at[0, pl.ds(0, 64)], xr.at[2])
    landed(xg.at[0, pl.ds(0, 64)], xr.at[4])
    c.to(sib, xg.at[t2], xg.at[t2], fr.at[2])
    project(t1)
    project(t3)
    landed(xg.at[0], xr.at[0])
    project(p.sibling()[0])
    project(t2)
    for k in (1, 3, 2):
        landed(xg.at[0], fr.at[k])
        project(lax.rem(p.z + 4 - k, 4) * 2 + 1 - p.core)

    def kv_to(a, b, src, n, span=None, recv=None):
        src, dst = kvall.at[src], kvall.at[n]
        if span is not None:
            src, dst = src.at[span], dst.at[span]
        c.to(p.cp(a, b), src, dst, kr.at[n if recv is None else recv])

    kv_to(0, 1, 0, 1)
    kv_to(0, 3, 0, 2)
    kv_to(1, 0, 0, 3)
    kept = (
        (qp, qp_out),
        (raw, raw_out),
        (wqkv, wqkv_out),
        (tabc, tabc_out),
        (tabs, tabs_out),
        (normed, normed_out),
        (normed_t, normed_t_out),
    )
    for src, dst in kept:
        c.own(src, dst)

    acc[...] = jnp.zeros_like(acc)
    lsum[...] = jnp.zeros_like(lsum)

    def work(n, _):
        kvb = kvall[n]

        def block(i, _):
            for u in range(UNROLL):
                rows = pl.ds(pl.multiple_of((i * UNROLL + u) * QB, QB), QB)
                e = jnp.exp2(dot(qp[rows, :], kvb, NT))
                total = e[:, 0:128]
                for j in range(1, 8):
                    total = total + e[:, j * 128 : (j + 1) * 128]
                lsum[rows, :] += total
                acc[rows, :] += dot(e.astype(BF), kvb)
            return 0

        lax.fori_loop(0, 2048 // QB // UNROLL, block, 0)
        return 0

    first, second = pl.ds(0, 512), pl.ds(512, 512)
    half = kvall.at[0, first]
    work(0, 0)
    landed(kvall.at[0], kr.at[1])
    kv_to(0, 1, 1, 4, first)
    kv_to(1, 0, 1, 5)
    landed(kvall.at[0], kr.at[2])
    kv_to(0, 3, 2, 4, second, 8)
    kv_to(1, 0, 2, 6)
    cot_rows([0] + ALONG_BOTH[0:6])
    lax.fori_loop(1, 3, work, 0)
    landed(half, kr.at[4])
    landed(half, kr.at[8])
    kv_to(1, 0, 4, 7)
    for i, (src, dst) in enumerate(weights):
        if i:
            c.to(p.partner(), src, part(dst, i, at_own), hr.at[i])
    landed(kvall.at[0], kr.at[3])
    lax.fori_loop(3, 5, work, 0)
    for k in (1, 3, 2):
        landed(wob, wor.at[k])
        block = wo.at[:, p.zpeer(-k)[1]]
        c.to(sib, block, block, wofr.at[k])

    def arrived(n, _):
        landed(kvall.at[0], kr.at[n])
        return work(n, 0)

    lax.fori_loop(5, 8, arrived, 0)

    for t in range(8):
        parts = []
        for h in range(2):
            rows = pl.ds(h * 1024 + t * 128, 128)
            total = jnp.sum(lsum[rows, :], axis=1, keepdims=True)
            parts.append(acc[rows, :] / total)
        whole = jnp.where(lane < 64, pltpu.roll(parts[0], 64, 1), parts[1])
        o[pl.ds(t * 128, 128), :] = whole
        att_t[pl.ds(t * 128, 128), :] = whole.astype(BF)
    for k in range(1, 8):
        t, dev = p.tp(k)
        block = att_t.at[pl.ds(pl.multiple_of(t * 128, 128), 128)]
        c.to(dev, block, attg.at[p.t], ar)
    own_att = c.here(att_t.at[pl.ds(pl.multiple_of(p.t * 128, 128), 128)], attg.at[p.t])
    cot_rows(ALONG_BOTH[6:9])
    ones = jnp.ones((8, 128), F32)
    for h in range(2):
        lse[h] = jnp.log2(dot_exact(ones, lsum[pl.ds(h * 1024, 1024), :], NT))
    for src, dst in ((o, o_out), (att_t, att_out), (lse, lse_out), (kvall, kv_out)):
        c.own(src, dst)
    for i, (_, dst) in enumerate(weights):
        piece = part(dst, i, from_partner)
        landed(piece, hr.at[i])
        c.to(sib, piece, part(dst, i, at_sib_partner), efr.at[i])
    own_wo.wait()
    landed(wob, wor.at[0])
    for k in (1, 3, 2):
        landed(wob, wofr.at[k])
    load_x.wait()
    own_att.wait()
    landed(attg.at[pl.ds(0, 7)], ar)

    att = jnp.concatenate([attg[t] for t in range(8)], axis=1)
    square = jnp.zeros((128, 1), F32)
    for j in range(4):
        cols = slice(j * 256, (j + 1) * 256)
        value = xv[:, cols].astype(F32) + dot(att, wo[:, :, :, cols].reshape(1024, 256))
        residual[:, cols] = value
        square = square + jnp.sum(value * value, axis=1, keepdims=True)
    factor = lax.rsqrt(square * (1.0 / 1024) + EPS)
    value = (residual[...] * factor * gmv[...]).astype(BF)
    for j in range(4):
        rows = dot(slots_t[j * 384 : (j + 1) * 384, :], value).astype(BF)
        outgoing[j * 8 : (j + 1) * 8] = rows.reshape(8, 48, 1024)

    for i, (_, dst) in enumerate(weights):
        landed(part(dst, i, at_sib), er.at[i])
        landed(part(dst, i, at_sib), efr.at[i])
    landed(grads.at[pl.ds(0, 30)], cr)
    c.done()


def front(*operands):
    shape = jax.ShapeDtypeStruct
    v = pltpu.VMEM
    return pl.pallas_call(
        front_kernel,
        out_shape=(
            shape((32, 48, 1024), BF),
            shape((128, 1024), F32),
            shape((8, 8, 16, 1152), BF),
            shape((128, 1536), BF),
            shape((32, 48, 1024), BF),
            shape((1024, 512), BF),
            shape((1024, 512), BF),
            shape((512, 1024), BF),
            shape((1024, 128), F32),
            shape((1024, 128), BF),
            shape((2, 8, 1024), F32),
            shape((8, 1024, 128), BF),
            shape((2048, 128), BF),
            shape((1024, 256), F32),
            shape((1024, 256), BF),
            shape((1024, 128), F32),
            shape((1024, 128), F32),
            shape((1024, 1024), BF),
            shape((1024, 1024), BF),
            shape((2, 128, 768), BF),
        ),
        in_specs=[HBM] * 17,
        out_specs=(VMEM,) * 4 + (HBM,) * 16,
        scratch_shapes=[
            v((128, 1024), BF),
            v((128, 1024), BF),
            v((8, 128), jnp.int32),
            v((1, 128), jnp.int32),
            v((8, 1024), BF),
            v((8, 512), BF),
            v((8, 512), BF),
            v((8, 1024), BF),
            v((8, 32), BF),
            v((1, 1024), F32),
            v((1, 1024), F32),
            v((1, 64), F32),
            v((1, 64), F32),
            v((1, 128), F32),
            v((8, 16, 128), BF),
            v((80, 128), BF),
            v((8, 128), F32),
            v((8, 128, 1024), BF),
            v((16, 8, 16, 128), BF),
            v((16, 80, 128), BF),
            v((8, 16, 1152), BF),
            v((8, 8, 128), F32),
            v((8, 16, 128), BF),
            v((32, 48, 1024), BF),
            v((1024, 1024), BF),
            v((1024, 1024), BF),
            v((1536, 128), BF),
            v((768, 128), BF),
            v((2, 128, 768), BF),
            v((32, 128), F32),
            v((8, 128), jnp.int32),
            v((128, 1024), BF),
            v((2048, 128), BF),
            v((8, 1024, 128), BF),
            v((1024, 256), F32),
            v((1024, 256), BF),
            v((1024, 128), F32),
            v((1024, 128), F32),
            v((2048, 128), F32),
            v((2048, 128), F32),
            v((1024, 128), F32),
            v((1024, 128), BF),
            v((2, 8, 1024), F32),
            v((8, 128, 128), BF),
            DMA((176,)),
            DMA((5,)),
            DMA((4,)),
            DMA,
            DMA,
            DMA,
            DMA,
            DMA,
            DMA((10,)),
            DMA,
            DMA((3,)),
            DMA((3,)),
            DMA((3,)),
            DMA((4,)),
            DMA((4,)),
            DMA((2,)),
        ],
        compiler_params=params(0, VMEM_MIB),
        name="front",
    )(*operands)


KB = 256
GB = 1024
EARLY = 4


def expert_kernel(
    outgoing,
    residual,
    wo,
    slots,
    grads_in,
    ewg,
    ewu,
    ewd,
    cot_in,
    gain_in,
    qp_in,
    kv_in,
    lse_in,
    branch,
    gat,
    grad_residual_out,
    grad_ffn_out,
    mixed_out,
    dwg_out,
    dwu_out,
    dwd_out,
    dwr_out,
    residual_out,
    weights_out,
    cot,
    gain,
    mixed,
    dwg,
    dwu,
    dwd,
    dwr,
    grad_residual,
    grad_ffn,
    rows,
    grads,
    wg,
    wu,
    wd,
    gh,
    gp,
    up,
    hid,
    gl,
    gin,
    back,
    sg,
    su,
    sd,
    rg,
    ru,
    rd,
    qp,
    kvall,
    lse,
    tiles,
    ss,
    rr,
    br,
    wr,
    ts,
):
    p = Place()
    _, sib = p.sibling()
    sem = greet(p.all_chips() + [sib])
    c = Copies(ss)
    own_rows = c.here(outgoing.at[p.chip], rows.at[0])
    local = [c.here(grads_in, grads), c.here(ewd, wd), c.here(ewg, wg), c.here(ewu, wu)]
    load_cot, load_gain = c.here(cot_in, cot), c.here(gain_in, gain)
    attention = [c.here(qp_in, qp), c.here(kv_in, kvall), c.here(lse_in, lse)]
    c.own(residual, residual_out)
    pl.semaphore_wait(sem, 31 + 1)
    for s in range(1, 32):
        e, dev = p.chips(s)
        c.to(dev, outgoing.at[e], rows.at[s], rr.at[s // 4])
    own_rows.wait()
    for copy in local:
        copy.wait()

    def hidden_grads(j, _):
        block = grads[pl.ds(j * 4, 4)].reshape(192, 1024)
        gh[pl.ds(pl.multiple_of(j * 192, 64), 192), :] = dot(block, wd[...], NT)
        return 0

    lax.fori_loop(0, 8, hidden_grads, 0)

    def weights_of(n, _):
        for j in range(1024 // KB):

            @pl.when(n > 0)
            def _(j=j):
                pltpu.make_async_copy(tiles.at[j], weights_out.at[0], ts.at[j]).wait()

            for i in range(2048 // GB):
                h, cols = i * GB // 1024, pl.ds(i * GB % 1024, GB)
                scores = dot(kvall[n, j * KB : (j + 1) * KB, :], qp[pl.ds(i * GB, GB), :], NT)
                value = jnp.exp2(scores - lse[h, 0:1, cols])
                tiles[j, :, i * GB : (i + 1) * GB] = value.astype(BF)
            tile = weights_out.at[n * (1024 // KB) + j]
            pltpu.make_async_copy(tiles.at[j], tile, ts.at[j]).start()
        return 0

    for copy in attention:
        copy.wait()
    lax.fori_loop(0, EARLY, weights_of, 0)

    lane = lax.broadcasted_iota(jnp.int32, (192, 128), 1)
    here = jnp.where(lane == p.chip, 1.0, 0.0)
    router = wo[:, :, :, 1024:].reshape(1024, 128)

    for j in range(8):
        landed(rows.at[pl.ds(0, 4 if j else 3)], rr.at[j])
        block = rows[4 * j : 4 * j + 4].reshape(192, 1024)
        span = pl.ds(j * 192, 192)
        gate_pre = dot(block, wg[...])
        up_pre = dot(block, wu[...])
        logits = jnp.where(lane < 32, dot(block, router), -1e30)
        expo = jnp.exp(logits - jnp.max(logits, axis=1, keepdims=True))
        probs = expo / jnp.sum(expo, axis=1, keepdims=True)
        gate = jnp.sum(probs * here, axis=1, keepdims=True)
        sig = jax.nn.sigmoid(gate_pre)
        act = gate_pre * sig
        hidden = act * up_pre
        grad_hidden = gh[span, :]
        weight = jnp.sum(hidden * grad_hidden, axis=1, keepdims=True) * gate
        grad_hidden = grad_hidden * gate
        grad_gate = (grad_hidden * up_pre * sig * (1.0 + gate_pre * (1.0 - sig))).astype(BF)
        grad_up = (grad_hidden * act).astype(BF)
        grad_logits = (weight * (here - probs)).astype(BF)
        hid[span, :] = (hidden * gate).astype(BF)
        gp[span, :] = grad_gate
        up[span, :] = grad_up
        gl[span, :] = grad_logits
        total = dot(grad_gate, wg[...], NT) + dot(grad_up, wu[...], NT)
        total = total + dot(grad_logits, router, NT)
        gin[4 * j : 4 * j + 4] = total.astype(BF).reshape(4, 48, 1024)
        for s in range(4 * j, 4 * j + 4):
            if s:
                c.to(p.chips(s, -1)[1], gin.at[s], back.at[p.chip], br)
            else:
                own_back = c.here(gin.at[0], back.at[p.chip])

    for m in range(4):
        cols = slice(m * 256, (m + 1) * 256)
        left = rows[:, :, cols].reshape(1536, 256)
        for src, own, sends in ((gp, dwg, sg), (up, dwu, su)):
            value = dot(left, src[...], TN).astype(BF)
            for q in range(2):
                own[q, cols, :] = value[:, q * 128 : (q + 1) * 128]
                sends[q, cols, :] = value[:, (2 + q) * 128 : (3 + q) * 128]
        dwr[cols, :] = dot(left, gl[...], TN)
    for m in range(4):
        cols = slice(m * 256, (m + 1) * 256)
        right = grads[:, :, cols].reshape(1536, 256)
        value = dot(hid[...], right, TN).astype(BF)
        dwd[:, :, cols] = value[:256].reshape(2, 128, 256)
        sd[:, :, cols] = value[256:].reshape(2, 128, 256)
    for i, (src, dst) in enumerate(((sg, rg), (su, ru), (sd, rd))):
        c.to(sib, src, dst, wr.at[i])

    def outputs(j, _):
        block = hid[pl.ds(pl.multiple_of(j * 192, 64), 192), :]
        mixed[pl.ds(j * 4, 4)] = dot(block, wd[...]).astype(BF).reshape(4, 48, 1024)
        return 0

    lax.fori_loop(0, 8, outputs, 0)
    c.own(mixed, mixed_out)
    c.own(dwr, dwr_out)
    lax.fori_loop(EARLY, 8, weights_of, 0)
    for i, (got, own) in enumerate(((rg, dwg), (ru, dwu), (rd, dwd))):
        landed(got, wr.at[i])
        own[...] = (own[...].astype(F32) + got[...].astype(F32)).astype(BF)
    for src, dst in ((dwg, dwg_out), (dwu, dwu_out), (dwd, dwd_out)):
        c.own(src, dst)
    load_cot.wait()
    load_gain.wait()

    for j in range(1024 // KB):
        pltpu.make_async_copy(tiles.at[j], weights_out.at[0], ts.at[j]).wait()

    landed(back.at[pl.ds(0, 31)], br)
    own_back.wait()
    res = residual[...]
    factor = lax.rsqrt(jnp.mean(res * res, axis=1, keepdims=True) + EPS)
    normed = res * factor
    for j in range(4):
        cols = slice(j * 256, (j + 1) * 256)
        grad_residual[:, cols] = dot(slots[...], back[:, :, cols].reshape(1536, 256))
    grad_mid = grad_residual[...]
    part = jnp.sum(grad_mid * normed, axis=0, keepdims=True)
    grad_ffn[...] = jnp.broadcast_to(part, (8, 1024))
    g = grad_mid * gain[...]
    g = factor * (g - normed * jnp.mean(g * normed, axis=1, keepdims=True))
    g = cot[...].astype(F32) + g
    grad_residual[...] = g
    low = g.astype(BF)
    branch[...] = low
    for t in range(8):
        weights = wo[t][:, :, :1024].reshape(128, 1024)
        gat[t] = dot(low, weights, NT).astype(BF)
    c.own(grad_residual, grad_residual_out)
    c.own(grad_ffn, grad_ffn_out)
    c.done()


def expert_rows(*operands):
    shape = jax.ShapeDtypeStruct
    v = pltpu.VMEM
    return pl.pallas_call(
        expert_kernel,
        out_shape=(
            shape((128, 1024), BF),
            shape((8, 128, 128), BF),
            shape((128, 1024), F32),
            shape((8, 1024), F32),
            shape((32, 48, 1024), BF),
            shape((2, 1024, 128), BF),
            shape((2, 1024, 128), BF),
            shape((2, 128, 1024), BF),
            shape((1024, 128), F32),
            shape((128, 1024), F32),
            shape((8 * 1024 // KB, KB, 2048), BF),
        ),
        in_specs=[VMEM] * 4 + [HBM] * 9,
        out_specs=(VMEM,) * 2 + (HBM,) * 9,
        scratch_shapes=[
            v((128, 1024), BF),
            v((1, 1024), F32),
            v((32, 48, 1024), BF),
            v((2, 1024, 128), BF),
            v((2, 1024, 128), BF),
            v((2, 128, 1024), BF),
            v((1024, 128), F32),
            v((128, 1024), F32),
            v((8, 1024), F32),
            v((32, 48, 1024), BF),
            v((32, 48, 1024), BF),
            v((1024, 512), BF),
            v((1024, 512), BF),
            v((512, 1024), BF),
            v((1536, 512), F32),
            v((1536, 512), BF),
            v((1536, 512), BF),
            v((1536, 512), BF),
            v((1536, 128), BF),
            v((32, 48, 1024), BF),
            v((32, 48, 1024), BF),
            v((2, 1024, 128), BF),
            v((2, 1024, 128), BF),
            v((2, 128, 1024), BF),
            v((2, 1024, 128), BF),
            v((2, 1024, 128), BF),
            v((2, 128, 1024), BF),
            v((2048, 128), BF),
            v((8, 1024, 128), BF),
            v((2, 8, 1024), F32),
            v((1024 // KB, KB, 2048), BF),
            DMA((96,)),
            DMA((8,)),
            DMA,
            DMA((3,)),
            DMA((1024 // KB,)),
        ],
        compiler_params=params(1, VMEM_MIB),
        name="experts",
    )(*operands)


ORDER = (5, 6, 7, 3, 4, 1, 2, 0)
AHEAD = 2


def back_kernel(
    branch,
    gat,
    grad_residual_in,
    grad_ffn_in,
    mixed,
    dwg,
    dwu,
    dwd,
    dwr_in,
    residual_in,
    probs,
    o_in,
    att_in,
    kv_in,
    qp_in,
    raw_in,
    wqkv_in,
    tabc_in,
    tabs_in,
    normed_in,
    normed_t_in,
    near_in,
    x_in,
    gain_a,
    gain_q,
    gain_k,
    layer_out,
    input_out,
    query_out,
    key_out,
    value_out,
    output_out,
    rows_out,
    misc_out,
    gate_out,
    up_out,
    down_out,
    layer_output,
    grad_input,
    grad_query,
    grad_key,
    grad_value,
    vectors,
    misc,
    out_g,
    out_u,
    out_d,
    grad_residual,
    grad_ffn,
    dwr,
    residual,
    near,
    ypart,
    ypeer,
    o,
    att_t,
    tiles,
    kvall,
    qp,
    raw,
    wqkv,
    tabc,
    tabs,
    normed,
    normed_t,
    xv,
    gav,
    gqv,
    gkv,
    own_g,
    own_u,
    own_d,
    rwg,
    rwu,
    rwd,
    yret,
    dqt,
    earlyr,
    gatr,
    dop,
    delta,
    acc,
    bg,
    early,
    dwos,
    dwol,
    dks,
    dkr,
    draw,
    dx,
    dwm,
    part,
    sibr,
    zsend,
    zr,
    dwin,
    d2s,
    d2l,
    ss,
    ar,
    bs,
    fs,
    yr,
    er,
    sr,
    os_,
    ors,
    dsr,
    zrs,
    wrs,
    trs,
    ypr,
    ts,
):
    p = Place()
    _, sib = p.sibling()
    c = Copies(ss)
    first = [
        c.here(src, dst)
        for src, dst in ((o_in, o), (qp_in, qp), (kv_in, kvall), (att_in, att_t))
    ]
    for k in range(AHEAD):
        pltpu.make_async_copy(probs.at[ORDER[0] * 1024 // KB + k], tiles.at[k], ts.at[k]).start()
    own_gat = c.here(gat.at[p.t], gatr.at[p.t])
    own_bg = c.here(branch, bg.at[p.t])
    sem = greet(p.all_chips() + p.all_tp() + p.all_gf())
    mirror = p.t * 8 + p.g
    at_home = p.g == p.t

    @pl.when(jnp.logical_not(at_home))
    def _():
        pl.semaphore_signal(sem, inc=1, device_id=(mirror, p.f), device_id_type=MESH)

    pl.semaphore_wait(sem, 31 + 7 + 15 + jnp.where(at_home, 0, 1))
    for k in range(1, 8):
        t, dev = p.tp(k)
        c.to(dev, gat.at[t], gatr.at[p.t], ar)
    own_gat.wait()
    for copy in first:
        copy.wait()
    landed(gatr.at[pl.ds(0, 7)], ar)
    for k in (1, 3, 2):
        c.to(p.zpeer(k)[2], branch, bg.at[p.t], bs.at[k])
    c.to(sib, branch, bg.at[p.t], bs.at[0])
    here = p.y * 4 + p.z
    own_mixed = c.here(mixed.at[pl.ds(0, 2)], yret.at[here])
    owned = ((dwg, own_g, rwg, out_g), (dwu, own_u, rwu, out_u), (dwd, own_d, rwd, out_d))
    owned_copies = []
    for i, (src, mine, got, _) in enumerate(owned):
        owned_copies.append(c.here(src.at[p.f], mine))

    def outputs(which):
        for m in which:
            c.to(p.plane(m, -1)[1], mixed.at[pl.ds(2 * m, 2)], yret.at[here], yr)

    outputs(ALONG_BOTH + ALONG_Z + ALONG_Y)
    later = (
        (raw_in, raw),
        (wqkv_in, wqkv),
        (tabc_in, tabc),
        (tabs_in, tabs),
        (normed_in, normed),
        (normed_t_in, normed_t),
        (grad_residual_in, grad_residual),
        (residual_in, residual),
        (near_in, near),
        (x_in, xv),
        (gain_a, gav),
        (gain_q, gqv),
        (gain_k, gkv),
    )
    soon = ((grad_ffn_in, grad_ffn), (dwr_in, dwr))
    soon = [c.here(src, dst) for src, dst in soon]
    later = [c.here(src, dst) for src, dst in later]

    lane = lanes(128)
    ones = jnp.ones((8, 128), F32)
    for t in range(8):
        both = gatr[t].astype(F32)
        rows = pl.ds(t * 128, 128)
        dop[rows, :] = jnp.where(lane < 64, 0.0, pltpu.roll(both, 64, 1)).astype(BF)
        dop[pl.ds(1024 + t * 128, 128), :] = jnp.where(lane < 64, 0.0, both).astype(BF)
        prod = both * o[rows, :]
        for h in range(2):
            value = jnp.where((lane < 64) == (h == 0), prod, 0.0)
            delta[h, :, rows] = dot_exact(ones, value, NT)
    dqt[...] = jnp.zeros_like(dqt)

    per = 1024 // KB

    def fetch(tile, k):
        slot = lax.rem(k, AHEAD + 1)
        return pltpu.make_async_copy(probs.at[tile], tiles.at[slot], ts.at[slot])

    def work(n):
        at = ORDER.index(n)

        def keys(j, _):
            k = at * per + j
            later = j + AHEAD

            @pl.when(k + AHEAD < 8 * per)
            def _():
                after = ORDER[min(at + 1, 7)]
                tile = jnp.where(later < per, n * per + later, after * per + later - per)
                fetch(tile, k + AHEAD).start()

            fetch(0, k).wait()
            slot = lax.rem(k, AHEAD + 1)
            krows = pl.ds(pl.multiple_of(j * KB, KB), KB)
            kvb = kvall[n, krows, :]
            kt = kvb.T[:64, :]
            total = jnp.zeros((KB, 128), F32)
            for i in range(2048 // GB):
                rows = pl.ds(i * GB, GB)
                h, cols = i * GB // 1024, pl.ds(i * GB % 1024, GB)
                q = qp[rows, :]
                d = dop[rows, :]
                w = tiles[slot, :, i * GB : (i + 1) * GB]
                ds = (w.astype(F32) * (dot(kvb, d, NT) - delta[h, 0:1, cols])).astype(BF)
                total = total + dot(w, d) + dot(ds, q)
                dqt[h * 64 : (h + 1) * 64, cols] += dot(kt, ds)
            acc[krows, :] = total
            return 0

        lax.fori_loop(0, per, keys, 0)

    def chunk_x(n):
        work(n)
        dks[n] = acc[...].astype(BF)
        m = MEMBERS.index((0, MEMBERS[n][1]))
        c.to(p.cp(1, 0), dks.at[n], dkr.at[m], sr.at[m])

    def chunk_y(n):
        work(n)
        landed(dkr.at[0], sr.at[n])
        dks[n] = (acc[...] + dkr[n].astype(F32)).astype(BF)
        m = MEMBERS.index((1, MEMBERS[n][1]))
        c.to(p.cp(0, -MEMBERS[n][1]), dks.at[n], dkr.at[m], sr.at[m])

    chunk_x(5)
    chunk_x(6)
    chunk_x(7)
    for k in (1, 3, 2):
        landed(branch, bs.at[k])
        block = bg.at[p.zpeer(-k)[1]]
        c.to(sib, block, block, fs.at[k])
    chunk_x(3)
    for i, (src, _, got, _) in enumerate(owned):
        c.to(p.partner(), src.at[1 - p.f], got, er.at[i])
    chunk_y(4)
    own_bg.wait()
    landed(branch, bs.at[0])
    for k in (1, 3, 2):
        landed(branch, fs.at[k])
    for j in range(4):
        cols = slice(j * 256, (j + 1) * 256)
        total = jnp.zeros((128, 256), F32)
        for t in range(8):
            total = total + dot(att_t[t * 128 : (t + 1) * 128, :], bg[t, :, cols], TN)
        for r in range(16):
            block = total[r * 8 : (r + 1) * 8, :]
            both = [block[:, :128], block[:, 128:]]
            early[r, j * 16 : (j + 1) * 16, :] = jnp.concatenate(both, axis=0).astype(BF)
    for copy in soon:
        copy.wait()
    spot = lax.broadcasted_iota(jnp.int32, (128, 128), 0)
    same = jnp.logical_and(lax.div(spot, 16) == lax.div(lane, 8), lax.rem(spot, 8) == lax.rem(lane, 8))
    picks = [
        jnp.where(jnp.logical_and(same, lax.rem(lax.div(spot, 8), 2) == f), 1.0, 0.0)
        for f in range(2)
    ]
    sub16 = lax.broadcasted_iota(jnp.int32, (16, 128), 0)

    def rows_of(value, f):
        return jnp.concatenate(
            [value[(2 * t + f) * 8 : (2 * t + f) * 8 + 8, :] for t in range(8)], axis=0
        )

    for g in range(8):
        span = slice(g * 128, (g + 1) * 128)
        value = dwr[span, :]
        for f in range(2):
            early[g * 2 + f, 64:128, :] = rows_of(value, f).astype(BF)
            line = dot_exact(grad_ffn[0:1, span], picks[f])
            early[g * 2 + f, 128:144, :] = jnp.where(sub16 == 0, line, 0.0).astype(BF)
    me = p.g * 2 + p.f
    for k in range(1, 16):
        r, dev = p.gf(k)
        c.to(dev, early.at[r], earlyr.at[me], ors)
    own_early = c.here(early.at[me], earlyr.at[me])

    chunk_y(1)
    chunk_y(2)
    work(0)

    for copy in later:
        copy.wait()
    head_gains = (
        jnp.concatenate([gqv[...], gqv[...]], axis=1),
        jnp.concatenate([gkv[...], jnp.ones((1, 64), F32)], axis=1),
    )

    def through(i, rows, grad):
        cosine, sine = tabc[rows, :], tabs[rows, :]
        value = raw[rows, i * 128 : (i + 1) * 128]
        grad = grad * cosine - swap(grad) * sine
        factor = lax.rsqrt(head_mean(value * value) + EPS)
        value = value * factor
        total = jnp.sum(grad * value, axis=0, keepdims=True)
        grad = grad * head_gains[i]
        return total, factor * (grad - value * head_mean(grad * value))

    gains_q = jnp.zeros((1, 128), F32)
    for t in range(8):
        rows = slice(t * 128, (t + 1) * 128)
        total, value = through(0, rows, dqt[:, rows].T * 0.125)
        gains_q = gains_q + total
        draw[rows, 0:128] = value.astype(BF)
    for n in (0, 5, 7, 6):
        landed(dkr.at[0], sr.at[n])
    gains_k = jnp.zeros((1, 128), F32)
    for t in range(8):
        rows = slice(t * 128, (t + 1) * 128)
        whole = acc[rows, :]
        for n in (0, 5, 7, 6):
            whole = whole + dkr[n, rows, :].astype(F32)
        total, value = through(1, rows, whole * LN2)
        gains_k = gains_k + total
        draw[rows, 128:256] = jnp.where(lane < 64, value, whole).astype(BF)
    part[...] = jnp.zeros_like(part)

    def input_grad(core, z):
        rows = pl.ds(pl.multiple_of((z * 2 + core) * 128, 128), 128)
        left = draw[rows, :]
        for j in range(4):
            cols = slice(j * 256, (j + 1) * 256)
            value = dot(left, wqkv[cols, :], NT)
            prod = value * normed[rows, cols].astype(F32)
            part[0:1, cols] += jnp.sum(prod, axis=0, keepdims=True)
            dx[core, z, :, cols] = value.astype(BF)

    for k in (1, 3, 2, 0):
        z = lax.rem(p.z + k, 4)
        input_grad(1 - p.core, z)
        c.to(sib, dx.at[1 - p.core, z], sibr.at[z], dsr.at[k])
    for k in (1, 3, 2):
        z, _, dev = p.zpeer(k)
        input_grad(p.core, z)
        landed(sibr.at[0], dsr.at[k])
        zsend[k] = (dx[p.core, z].astype(F32) + sibr[z].astype(F32)).astype(BF)
        c.to(dev, zsend.at[k], zr.at[k], zrs.at[k])
    input_grad(p.core, p.z)

    part[0:1, :] = part[0:1, :] / gav[...]
    gains = jnp.concatenate([gains_q, jnp.where(lanes(1) < 64, gains_k, 0.0)], axis=1)
    wide16 = lax.broadcasted_iota(jnp.int32, (16, 256), 0)
    for j in range(8):
        g = lax.rem(p.g + j, 8)
        rows = pl.ds(pl.multiple_of(g * 128, 128), 128)
        value = dot(normed_t[rows, :], draw[...])
        for f in range(2):
            dwm[g * 2 + f, 0:64, :] = rows_of(value, f).astype(BF)
            line = dot_exact(part[0:1, rows], picks[f])
            line = jnp.concatenate([line, jnp.zeros((1, 128), F32)], axis=1)
            line = jnp.where(wide16 == 0, gains, jnp.where(wide16 == 1, line, 0.0))
            dwm[g * 2 + f, 64:80, :] = line.astype(BF)
        if j:
            for f in range(2):
                c.to((g * 8 + p.t, f), dwm.at[g * 2 + f], dwin.at[me], wrs)
        else:
            c.to(p.partner(), dwm.at[g * 2 + 1 - p.f], dwin.at[me], wrs)
            own_dw = c.here(dwm.at[me], dwin.at[me])

    own_mixed.wait()
    landed(yret.at[pl.ds(0, 15)], yr)
    for j in range(4):
        cols = slice(j * 256, (j + 1) * 256)
        ypart[:, cols] = dot(near[1], yret[:, 1, :, cols].reshape(768, 256)).astype(BF)
    c.to(p.cp(1, 0), ypart, ypeer, ypr)
    for j in range(4):
        cols = slice(j * 256, (j + 1) * 256)
        residual[:, cols] += dot(near[0], yret[:, 0, :, cols].reshape(768, 256))

    landed(sibr.at[0], dsr.at[0])
    whole = dx[p.core, p.z].astype(F32) + sibr[p.z].astype(F32)
    for i, (_, mine, got, out) in enumerate(owned):
        owned_copies[i].wait()
        landed(got, er.at[i])
        out[...] = mine[...].astype(F32) + got[...].astype(F32)
    for src, dst in ((out_g, gate_out), (out_u, up_out), (out_d, down_out)):
        c.own(src, dst)
    own_early.wait()
    landed(earlyr.at[pl.ds(0, 15)], ors)
    before = earlyr[0].astype(F32)
    for r in range(1, 16):
        before = before + earlyr[r].astype(F32)
    for i in range(8):
        dwos[:, i * 128 : (i + 1) * 128] = before[i * 8 : (i + 1) * 8, :]

    @pl.when(jnp.logical_not(at_home))
    def _():
        pltpu.make_async_remote_copy(
            src_ref=dwos,
            dst_ref=dwol,
            send_sem=os_.at[0],
            recv_sem=os_.at[1],
            device_id=(mirror, p.f),
            device_id_type=MESH,
        ).start()

    @pl.when(at_home)
    def _():
        pltpu.make_async_copy(dwos, dwol, os_.at[2]).start()

    own_dw.wait()
    landed(dwin.at[pl.ds(0, 15)], wrs)
    total = dwin[0].astype(F32)
    for r in range(1, 16):
        total = total + dwin[r].astype(F32)
    eight = lax.broadcasted_iota(jnp.int32, (8, 128), 0)
    for t in range(8):
        d2s[t, 0:8, :] = total[t * 8 : (t + 1) * 8, :]
        turn = (128 - 8 * t) % 128
        lines = [total[65:66, 0:128], before[128:129, :]]
        lines = [pltpu.roll(jnp.broadcast_to(v, (8, 128)), turn, 1) if turn else v for v in lines]
        lines = jnp.where(eight == 0, total[64:65, 0:128], jnp.where(eight == 2, lines[0], lines[1]))
        lines = jnp.where(eight == 1, total[64:65, 128:256], lines)
        d2s[t, 8:16, 0:128] = lines
        d2s[t, 8:16, 128:256] = before[64 + t * 8 : 72 + t * 8, :]
    for k in range(1, 8):
        t, dev = p.tp(k)
        c.to(dev, d2s.at[t], d2l.at[p.t], trs)
    own_d2 = c.here(d2s.at[p.t], d2l.at[p.t])

    for k in (1, 3, 2):
        landed(zr.at[0], zrs.at[k])
        whole = whole + zr[k].astype(F32)
    xf = xv[...].astype(F32)
    factor = lax.rsqrt(jnp.mean(xf * xf, axis=1, keepdims=True) + EPS)
    n = xf * factor
    g = whole * gav[...]
    g = factor * (g - n * jnp.mean(g * n, axis=1, keepdims=True))
    grad_input[...] = grad_residual[...] + g
    c.own(grad_input, input_out)
    landed(ypeer, ypr)
    layer_output[...] = (residual[...] + ypeer[...].astype(F32)).astype(BF)
    c.own(layer_output, layer_out)

    @pl.when(jnp.logical_not(at_home))
    def _():
        landed(dwos, os_.at[0])
        landed(dwol, os_.at[1])

    @pl.when(at_home)
    def _():
        landed(dwol, os_.at[2])

    c.own(dwol, output_out)
    own_d2.wait()
    landed(d2l.at[pl.ds(0, 7)], trs)
    low8 = lanes(8) < 64
    totals = [jnp.zeros((8, 128), F32)] * 2
    for t in range(8):
        grad_query[:, t * 128 : (t + 1) * 128] = d2l[t, 0:8, 0:128]
        totals = [totals[i] + d2l[t, 8:16, i * 128 : (i + 1) * 128] for i in range(2)]
    for i in range(4):
        one, two = d2l[2 * i, 0:8, 128:256], d2l[2 * i + 1, 0:8, 128:256]
        cols = slice(i * 128, (i + 1) * 128)
        grad_key[:, cols] = jnp.where(low8, one, pltpu.roll(two, 64, 1))
        grad_value[:, cols] = jnp.where(low8, pltpu.roll(one, 64, 1), two)
    both = totals[0] + pltpu.roll(totals[0], 64, 1)
    vectors[...] = jnp.where(eight == 0, both, totals[0])
    misc[...] = totals[1]
    last = (
        (grad_query, query_out),
        (grad_key, key_out),
        (grad_value, value_out),
        (vectors, rows_out),
        (misc, misc_out),
    )
    for src, dst in last:
        c.own(src, dst)
    c.done()


def back(*operands):
    shape = jax.ShapeDtypeStruct
    v = pltpu.VMEM
    return pl.pallas_call(
        back_kernel,
        out_shape=(
            shape((128, 1024), BF),
            shape((128, 1024), F32),
            shape((8, 1024), F32),
            shape((8, 512), F32),
            shape((8, 512), F32),
            shape((8, 1024), F32),
            shape((8, 128), F32),
            shape((8, 128), F32),
            shape((1024, 128), F32),
            shape((1024, 128), F32),
            shape((128, 1024), F32),
        ),
        in_specs=[VMEM] * 2 + [HBM] * 24,
        out_specs=(HBM,) * 11,
        scratch_shapes=[
            v((128, 1024), BF),
            v((128, 1024), F32),
            v((8, 1024), F32),
            v((8, 512), F32),
            v((8, 512), F32),
            v((8, 128), F32),
            v((8, 128), F32),
            v((1024, 128), F32),
            v((1024, 128), F32),
            v((128, 1024), F32),
            v((128, 1024), F32),
            v((8, 1024), F32),
            v((1024, 128), F32),
            v((128, 1024), F32),
            v((2, 128, 768), BF),
            v((128, 1024), BF),
            v((128, 1024), BF),
            v((1024, 128), F32),
            v((1024, 128), BF),
            v((AHEAD + 1, KB, 2048), BF),
            v((8, 1024, 128), BF),
            v((2048, 128), BF),
            v((1024, 256), F32),
            v((1024, 256), BF),
            v((1024, 128), F32),
            v((1024, 128), F32),
            v((1024, 1024), BF),
            v((1024, 1024), BF),
            v((128, 1024), BF),
            v((1, 1024), F32),
            v((1, 64), F32),
            v((1, 64), F32),
            v((1024, 128), BF),
            v((1024, 128), BF),
            v((128, 1024), BF),
            v((1024, 128), BF),
            v((1024, 128), BF),
            v((128, 1024), BF),
            v((16, 2, 48, 1024), BF),
            v((128, 1024), F32),
            v((16, 144, 128), BF),
            v((8, 128, 128), BF),
            v((2048, 128), BF),
            v((2, 8, 1024), F32),
            v((1024, 128), F32),
            v((8, 128, 1024), BF),
            v((16, 144, 128), BF),
            v((8, 1024), F32),
            v((8, 1024), F32),
            v((8, 1024, 128), BF),
            v((8, 1024, 128), BF),
            v((1024, 256), BF),
            v((2, 4, 128, 1024), BF),
            v((16, 80, 256), BF),
            v((8, 1024), F32),
            v((4, 128, 1024), BF),
            v((4, 128, 1024), BF),
            v((4, 128, 1024), BF),
            v((16, 80, 256), BF),
            v((8, 16, 256), F32),
            v((8, 16, 256), F32),
            DMA((128,)),
            DMA,
            DMA((4,)),
            DMA((4,)),
            DMA,
            DMA((3,)),
            DMA((8,)),
            DMA((3,)),
            DMA,
            DMA((4,)),
            DMA((4,)),
            DMA,
            DMA,
            DMA,
            DMA((AHEAD + 1,)),
        ],
        compiler_params=params(2, VMEM_MIB),
        name="back",
    )(*operands)


def outputs_kernel(count, *refs):
    ins, outs, held = refs[:count], refs[count : 2 * count], refs[2 * count : 3 * count]
    sems = refs[-1]
    loads = [pltpu.make_async_copy(ins[i], held[i], sems.at[0, i]) for i in range(count)]
    for copy in loads:
        copy.start()
    stores = [
        pltpu.make_async_copy(held[i], outs[i], sems.at[1, i]) for i in range(count - 1)
    ]
    for i in range(count - 1):
        loads[i].wait()
        stores[i].start()
    loads[-1].wait()
    outs[-1][...] = held[-1][:, :32]
    for copy in stores:
        copy.wait()


def to_outputs(*arrays):
    count = len(arrays)
    shapes = [jax.ShapeDtypeStruct(a.shape, a.dtype) for a in arrays[:-1]]
    shapes.append(jax.ShapeDtypeStruct((8, 32), F32))
    return pl.pallas_call(
        functools.partial(outputs_kernel, count),
        out_shape=tuple(shapes),
        in_specs=[HBM] * count,
        out_specs=(HBM,) * (count - 1) + (VMEM,),
        scratch_shapes=[pltpu.VMEM(a.shape, a.dtype) for a in arrays] + [DMA((2, count))],
        compiler_params=pltpu.CompilerParams(vmem_limit_bytes=VMEM_MIB * 2**20),
        name="outputs",
    )(*arrays)


RATES = np.power(50000.0, -(np.arange(128) % 32) / 32.0).astype(np.float32).reshape(1, 128)


def local(
    layer_input,
    positions,
    routes,
    attn_gain,
    w_query,
    w_key,
    w_value,
    query_gain,
    key_gain,
    w_output,
    ffn_gain,
    w_router,
    w_gate,
    w_up,
    w_down,
    cotangent,
):
    x = layer_input[0]
    cot = cotangent[0]
    gain_a = attn_gain.reshape(1, 1024)
    gain_m = ffn_gain.reshape(1, 1024)
    gain_q = query_gain.reshape(1, 64)
    gain_k = key_gain.reshape(1, 64)
    (outgoing, residual, wo, slots, grads, ewg, ewu, ewd, *kept) = front(
        x,
        cot,
        routes[0].T,
        positions,
        w_query,
        w_key,
        w_value,
        w_output,
        w_router,
        gain_a,
        gain_m,
        gain_q,
        gain_k,
        jnp.asarray(RATES),
        w_gate[0],
        w_up[0],
        w_down[0],
    )
    o, att, lse, kv, qp, *rest = kept
    passed = expert_rows(
        outgoing, residual, wo, slots, grads, ewg, ewu, ewd, cot, gain_m, qp, kv, lse
    )
    results = back(*passed, o, att, kv, qp, *rest, x, gain_a, gain_q, gain_k)
    vectors = results[6]
    (
        layer_output,
        grad_input,
        grad_query,
        grad_key,
        grad_value,
        grad_output,
        grad_gate,
        grad_up,
        grad_down,
        grad_router,
    ) = to_outputs(*results[:6], *results[8:], results[7])
    return (
        layer_output[None],
        grad_input[None],
        vectors[2, :8],
        grad_query,
        grad_key,
        grad_value,
        vectors[0, :64],
        vectors[1, :64],
        grad_output,
        vectors[3, :8],
        grad_router,
        grad_gate[None],
        grad_up[None],
        grad_down[None],
    )


def solution(mesh):
    rows = P(("ctx", "fsdp"), None)
    vector = P(("ctx", "fsdp"))
    tokens = P("fsdp", "ctx", None)
    return jax.shard_map(
        local,
        mesh=mesh,
        in_specs=(
            tokens,
            P("fsdp", "ctx"),
            tokens,
            P(),
            rows,
            rows,
            rows,
            P(),
            P(),
            rows,
            P(),
            rows,
            P("ctx", None, "fsdp"),
            P("ctx", None, "fsdp"),
            P("ctx", "fsdp", None),
            tokens,
        ),
        out_specs=(
            tokens,
            tokens,
            vector,
            rows,
            rows,
            rows,
            P(),
            P(),
            rows,
            vector,
            rows,
            P("ctx", None, "fsdp"),
            P("ctx", None, "fsdp"),
            P("ctx", "fsdp", None),
        ),
        check_vma=False,
    )
```

```python
import functools

import jax
import jax.numpy as jnp
import numpy as np
from jax import lax
from jax.experimental import pallas as pl
from jax.experimental.pallas import tpu as pltpu
from jax.sharding import PartitionSpec as P

EPS = 1e-06
LOG2E = 1.4426950408889634
LN2 = 0.6931471805599453
MESH = pl.DeviceIdType.MESH
VMEM_MIB = 62
BF = jnp.bfloat16
F32 = jnp.float32
NN = (((1,), (0,)), ((), ()))
NT = (((1,), (1,)), ((), ()))
TN = (((0,), (0,)), ((), ()))
HBM = pl.BlockSpec(memory_space=pltpu.HBM)
VMEM = pl.BlockSpec(memory_space=pltpu.VMEM)
DMA = pltpu.SemaphoreType.DMA
MEMBERS = ((0, 0), (0, 1), (0, 3), (1, 0), (0, 2), (1, 1), (1, 3), (1, 2))
PLANE = ((0, 0), (2, 2), (1, 1), (3, 3), (1, 3), (3, 1), (0, 1), (2, 3))
PLANE = PLANE + ((0, 3), (2, 1), (1, 0), (3, 2), (3, 0), (1, 2), (0, 2), (2, 0))
CHIPS = tuple((a, b, c) for b, c in PLANE for a in range(2))
ALONG_Z = [m for m in range(1, 16) if PLANE[m][0] == 0]
ALONG_Y = [m for m in range(1, 16) if PLANE[m][1] == 0]
ALONG_BOTH = [m for m in range(1, 16) if PLANE[m][0] and PLANE[m][1]]


def dot(left, right, dims=NN):
    return lax.dot_general(left, right, dims, preferred_element_type=F32)


def dot_exact(left, right, dims=NN):
    return lax.dot_general(
        left, right, dims, precision=lax.Precision.HIGHEST, preferred_element_type=F32
    )


class Place:
    def __init__(self):
        ctx = lax.axis_index("ctx")
        self.f = lax.axis_index("fsdp")
        self.t = lax.rem(ctx, 8)
        self.g = lax.div(ctx, 8)
        self.core = lax.rem(ctx, 2)
        self.z = lax.rem(lax.div(ctx, 2), 4)
        self.y = lax.rem(self.g, 4)
        self.xl = lax.div(self.g, 4)
        self.chip = lax.div(ctx, 2)

    def tp(self, k):
        t = lax.rem(self.t + k, 8)
        return t, (self.g * 8 + t, self.f)

    def cp(self, a, b):
        g = lax.rem(self.xl + a, 2) * 4 + lax.rem(self.y + b + 4, 4)
        return (g * 8 + self.t, self.f)

    def gf(self, k):
        r = lax.rem(self.g * 2 + self.f + k, 16)
        return r, (lax.div(r, 2) * 8 + self.t, lax.rem(r, 2))

    def chips(self, s, sign=1):
        a, b, c = CHIPS[s]
        xl = lax.rem(self.xl + a, 2)
        y = lax.rem(self.y + sign * b + 4, 4)
        z = lax.rem(self.z + sign * c + 4, 4)
        e = (xl * 4 + y) * 4 + z
        return e, (e * 2 + self.core, self.f)

    def plane(self, m, sign=1):
        b, c = PLANE[m]
        i = lax.rem(self.y + sign * b + 4, 4) * 4 + lax.rem(self.z + sign * c + 4, 4)
        e = self.xl * 16 + i
        return i, (e * 2 + self.core, self.f)

    def zpeer(self, c):
        z = lax.rem(self.z + c + 4, 4)
        t = z * 2 + self.core
        return z, t, (self.g * 8 + t, self.f)

    def sibling(self):
        t = self.z * 2 + 1 - self.core
        return t, (self.g * 8 + t, self.f)

    def partner(self):
        return (self.g * 8 + self.t, 1 - self.f)

    def all_tp(self):
        return [self.tp(k)[1] for k in range(1, 8)]

    def all_gf(self):
        return [self.gf(k)[1] for k in range(1, 16)]

    def all_chips(self):
        return [self.chips(s)[1] for s in range(1, 32)]


def greet(devices):
    sem = pltpu.get_barrier_semaphore()
    for d in devices:
        pl.semaphore_signal(sem, inc=1, device_id=d, device_id_type=MESH)
    return sem


class Copies:
    def __init__(self, sems):
        self.sems, self.count, self.begun = sems, 0, []

    def next(self):
        self.count += 1
        return self.sems.at[self.count - 1]

    def to(self, device, src, dst, recv):
        copy = pltpu.make_async_remote_copy(
            src_ref=src,
            dst_ref=dst,
            send_sem=self.next(),
            recv_sem=recv,
            device_id=device,
            device_id_type=MESH,
        )
        copy.start()
        self.begun.append(copy.wait_send)

    def own(self, src, dst):
        copy = pltpu.make_async_copy(src, dst, self.next())
        copy.start()
        self.begun.append(copy.wait)

    def here(self, src, dst):
        copy = pltpu.make_async_copy(src, dst, self.next())
        copy.start()
        return copy

    def done(self):
        for wait in self.begun:
            wait()


def landed(ref, sem):
    pltpu.make_async_copy(ref, ref, sem).wait()


def params(number, mib):
    return pltpu.CompilerParams(
        collective_id=number, has_side_effects=True, vmem_limit_bytes=mib * 2**20
    )


def lanes(rows):
    return lax.broadcasted_iota(jnp.int32, (rows, 128), 1)


def swap(v):
    low = lax.rem(lanes(v.shape[0]), 64) < 32
    return jnp.where(low, pltpu.roll(v, 96, 1), pltpu.roll(v, 32, 1))


def head_mean(v):
    row = lax.broadcasted_iota(jnp.int32, (128, 128), 0)
    same = lax.div(row, 64) == lax.div(lanes(128), 64)
    return dot_exact(v, jnp.where(same, 1.0 / 64, 0.0))


def cos_sin(angle):
    k = jnp.floor(angle * 0.6366197723675814 + 0.5)
    r = angle - k * 1.5703125
    r = r - k * 4.837512969970703125e-4
    r = r - k * 7.54978995489188216e-8
    r2 = r * r
    s = r + r * r2 * (-1.6666654611e-1 + r2 * (8.3321608736e-3 + r2 * -1.9515295891e-4))
    c = 4.166664568298827e-2 + r2 * (-1.388731625493765e-3 + r2 * 2.443315711809948e-5)
    c = 1.0 - 0.5 * r2 + r2 * r2 * c
    q = k - 4.0 * jnp.floor(k * 0.25)
    odd = jnp.logical_or(q == 1.0, q == 3.0)
    cosine, sine = jnp.where(odd, s, c), jnp.where(odd, c, s)
    cosine = jnp.where(jnp.logical_or(q == 1.0, q == 2.0), -cosine, cosine)
    sine = jnp.where(q >= 2.0, -sine, sine)
    return cosine, sine


def column(row):
    at = lax.broadcasted_iota(jnp.int32, (128, 128), 0) == lanes(128)
    return jnp.sum(jnp.where(at, row, 0.0), axis=1, keepdims=True)


QB = 256
UNROLL = 4


def front_kernel(
    x,
    cot,
    routes,
    pos,
    wq,
    wk,
    wv,
    wo_own,
    wr_own,
    gain_a,
    gain_m,
    gain_q,
    gain_k,
    rates,
    eg,
    eu,
    ed,
    outgoing,
    residual,
    wo,
    slots,
    grads,
    ewg,
    ewu,
    ewd,
    o_out,
    att_out,
    lse_out,
    kv_out,
    qp_out,
    raw_out,
    wqkv_out,
    tabc_out,
    tabs_out,
    normed_out,
    normed_t_out,
    near_out,
    xv,
    cotv,
    routev,
    posv,
    wqv,
    wkv,
    wvv,
    wov,
    wrv,
    gav,
    gmv,
    gqv,
    gkv,
    ratev,
    wps,
    wops,
    posf,
    xg,
    wg,
    wog,
    wob,
    posg,
    wst,
    cots,
    normed,
    normed_t,
    slots_t,
    slots_p,
    near,
    place_p,
    routep,
    cotp,
    qp,
    kvall,
    raw,
    wqkv,
    tabc,
    tabs,
    acc,
    lsum,
    o,
    att_t,
    lse,
    attg,
    ss,
    xr,
    fr,
    pr,
    wr,
    gr,
    orr,
    cr,
    kr,
    ar,
    er,
    hr,
    efr,
    wor,
    wofr,
    xpr,
):
    p = Place()
    _, sib = p.sibling()
    me = p.g * 2 + p.f
    c = Copies(ss)
    small = (
        (wq, wqv),
        (wk, wkv),
        (wv, wvv),
        (wo_own, wov),
        (wr_own, wrv),
        (pos, posv),
        (routes, routev),
        (gain_q, gqv),
        (gain_k, gkv),
        (rates, ratev),
        (gain_a, gav),
        (gain_m, gmv),
    )
    loads = [c.here(src, dst) for src, dst in small]
    own_x = c.here(x, xg.at[p.t])
    load_cot = c.here(cot, cotv)
    load_x = c.here(x, xv)
    sem = greet(p.all_chips() + p.all_tp() + p.all_gf())
    for copy in loads:
        copy.wait()

    low8 = lanes(8) < 64
    for t in range(8):
        pair = slice(t // 2 * 128, t // 2 * 128 + 128)
        key, value = wkv[:, pair].astype(F32), wvv[:, pair].astype(F32)
        if t % 2:
            both = jnp.where(low8, pltpu.roll(key, 64, 1), value)
        else:
            both = jnp.where(low8, key, pltpu.roll(value, 64, 1))
        query = wqv[:, t * 128 : (t + 1) * 128].astype(F32)
        wps[t] = jnp.concatenate([query, both], axis=0).astype(BF)
    for i in range(4):
        pair = [wov[:, (2 * i + j) * 128 : (2 * i + j + 1) * 128].astype(F32) for j in range(2)]
        wops[i * 16 : (i + 1) * 16, :] = jnp.concatenate(pair, axis=0).astype(BF)
    router = jnp.concatenate([wrv[...].astype(F32), jnp.zeros((8, 96), F32)], axis=1)
    wops[64:80, :] = jnp.concatenate([router, jnp.zeros((8, 128), F32)], axis=0).astype(BF)
    posf[...] = jnp.broadcast_to(posv[...].astype(F32), (8, 128))
    own = [
        c.here(wps.at[p.t], wst.at[p.t]),
        c.here(posf, posg.at[p.t]),
        c.here(wops, wog.at[me]),
    ]
    pl.semaphore_wait(sem, 31 + 7 + 15)

    for k in range(1, 8):
        t, dev = p.tp(k)
        c.to(dev, wps.at[t], wst.at[p.t], wr)
    for k in (1, 3):
        c.to(p.zpeer(k)[2], x, xg.at[p.t], xr.at[k])
    c.to(sib, x, xg.at[p.t], xr.at[0])
    c.to(p.cp(1, 0), routev, routep, xpr.at[0])
    c.to(p.cp(1, 0), cot, cotp, xpr.at[1])
    for k in range(1, 8):
        c.to(p.tp(k)[1], posf, posg.at[p.t], pr)
    for copy in own:
        copy.wait()

    row = lax.broadcasted_iota(jnp.int32, (128, 128), 0)
    col = lanes(128)

    def places(ref):
        number = lax.broadcasted_iota(jnp.int32, (32, 128), 0)
        hits = jnp.zeros((32, 128), F32)
        for k in range(8):
            hits = hits + jnp.where(ref[k : k + 1, :] == number, 1.0, 0.0)
        before = jnp.where(row < col, 1.0, 0.0).astype(BF)
        return jnp.where(hits > 0, dot(hits.astype(BF), before), -1.0)

    def slot_rows(place):
        within = lax.broadcasted_iota(jnp.int32, (48, 128), 0).astype(F32)
        return jnp.where(place == within, 1.0, 0.0).astype(BF)

    place = places(routev)
    for e in range(32):
        slots_t[e * 48 : (e + 1) * 48, :] = slot_rows(place[e : e + 1, :])
    load_cot.wait()

    def cot_rows(which):
        for m in which:
            i, dev = p.plane(m)
            for a, (ref, values) in enumerate(((slots_t, cotv), (slots_p, cotp))):
                first = i + p.xl * 16 if a == 0 else i
                mine = ref[pl.ds(pl.multiple_of(first * 48, 16), 48), :]
                cots[2 * m + a] = dot(mine, values[...]).astype(BF)
            pair = pl.ds(2 * m, 2)
            if m:
                c.to(dev, cots.at[pair], grads.at[pair], cr)
            else:
                c.own(cots.at[pair], grads.at[pair])

    landed(wst.at[pl.ds(0, 7)], wr)
    own_wg = c.here(wst, wg.at[me])
    for k in range(1, 16):
        c.to(p.gf(k)[1], wst, wg.at[me], gr)
    for k in range(1, 16):
        c.to(p.gf(k)[1], wops, wog.at[me], orr)
    at_own = pl.ds(pl.multiple_of(p.f * 128, 128), 128)
    at_sib = pl.ds(pl.multiple_of(256 + p.f * 128, 128), 128)
    from_partner = pl.ds(pl.multiple_of((1 - p.f) * 128, 128), 128)
    at_sib_partner = pl.ds(pl.multiple_of(256 + (1 - p.f) * 128, 128), 128)

    def part(ref, i, span):
        return ref.at[span, :] if i == 2 else ref.at[:, span]

    weights = ((eg, ewg), (eu, ewu), (ed, ewd))
    for i, (src, dst) in enumerate(weights):
        c.to(sib, src, part(dst, i, at_sib), er.at[i])
        c.own(src, part(dst, i, at_own))
    landed(routep, xpr.at[0])
    place_p[...] = places(routep)
    here = place_p[pl.ds(pl.multiple_of(p.xl * 16, 16), 16), :]
    for e in range(16):
        slots_p[e * 48 : (e + 1) * 48, :] = slot_rows(here[e : e + 1, :])
    for j in range(12):
        cols = slice(j * 128, (j + 1) * 128)
        slots[:, cols] = slots_t[cols, :].astype(F32).T.astype(BF)
    for j in range(6):
        cols = slice(j * 128, (j + 1) * 128)
        near[1, :, cols] = slots_p[cols, :].astype(F32).T.astype(BF)
    near[0] = slots[:, pl.ds(pl.multiple_of(p.xl * 768, 128), 768)]
    c.own(near, near_out)
    landed(cotp, xpr.at[1])

    def pass_on(k, n):
        landed(xg.at[0], xr.at[k])
        t = p.zpeer(-k)[1]
        half = pl.ds(0 if k == 1 else 64, 64)
        c.to(p.zpeer(k)[2], xg.at[t, half], xg.at[t, half], xr.at[n])
        c.to(sib, xg.at[t], xg.at[t], fr.at[k])
        return t

    t1 = pass_on(1, 2)
    t3 = pass_on(3, 4)
    cot_rows(ALONG_Z + ALONG_Y)
    c.to(p.partner(), eg, part(ewg, 0, at_own), hr.at[0])

    landed(posg.at[pl.ds(0, 7)], pr)
    signed = jnp.where(lax.rem(col, 64) < 32, -1.0, 1.0)
    for t in range(8):
        cosine, sine = cos_sin(column(posg[t, 0:1, :]) * ratev[...])
        tabc[t * 128 : (t + 1) * 128, :] = cosine
        tabs[t * 128 : (t + 1) * 128, :] = sine * signed

    own_wg.wait()
    landed(wg.at[pl.ds(0, 15)], gr)

    def columns(g, _):
        for t in range(8):
            one, two = wg[2 * g, t].astype(F32), wg[2 * g + 1, t].astype(F32)
            both = [jnp.concatenate([one[i : i + 8], two[i : i + 8]], axis=0) for i in (0, 8)]
            at = pl.ds(pl.multiple_of((g * 8 + t) * 16, 16), 16)
            wqkv[at, :] = jnp.concatenate(both, axis=1).astype(BF)
        return 0

    lax.fori_loop(0, 8, columns, 0)

    landed(wog.at[pl.ds(0, 15)], orr)

    def output_rows(g, _):
        one, two = wog[2 * g].astype(F32), wog[2 * g + 1].astype(F32)
        for i in range(9):
            both = [one[i * 8 : i * 8 + 8], two[i * 8 : i * 8 + 8]]
            wob[g, :, i * 128 : (i + 1) * 128] = jnp.concatenate(both, axis=0).astype(BF)
        return 0

    lax.fori_loop(0, 8, output_rows, 0)
    for k in (1, 3, 2):
        c.to(p.zpeer(k)[2], wob, wo.at[:, p.t], wor.at[k])
    c.to(sib, wob, wo.at[:, p.t], wor.at[0])
    own_wo = c.here(wob, wo.at[:, p.t])

    lane = lanes(128)
    head_q = jnp.concatenate([gqv[...], gqv[...]], axis=1)
    head_k = jnp.concatenate([gkv[...], jnp.ones((1, 64), F32)], axis=1)

    def project(t):
        rows = pl.ds(pl.multiple_of(t * 128, 128), 128)
        value = xg[t].astype(F32)
        factor = lax.rsqrt(jnp.mean(value * value, axis=1, keepdims=True) + EPS)
        value = (value * factor * gav[...]).astype(BF)
        normed[rows, :] = value
        normed_t[:, rows] = value.astype(F32).T.astype(BF)
        out = dot(value, wqkv[...])
        raw[rows, :] = out
        cosine, sine = tabc[rows, :], tabs[rows, :]
        q, k = out[:, :128], out[:, 128:]
        q = q * lax.rsqrt(head_mean(q * q) + EPS) * head_q
        q = ((q * cosine + swap(q) * sine) * (0.125 * LOG2E)).astype(BF).astype(F32)
        qp[rows, :] = jnp.where(lane < 64, q, 0.0).astype(BF)
        second = pl.ds(pl.multiple_of(1024 + t * 128, 128), 128)
        qp[second, :] = jnp.where(lane < 64, pltpu.roll(q, 64, 1), 0.0).astype(BF)
        n = k * lax.rsqrt(head_mean(k * k) + EPS) * head_k
        n = n * cosine + swap(n) * sine
        kvall[0, rows, :] = jnp.where(lane < 64, n, k).astype(BF)

    own_x.wait()
    project(p.t)
    t2 = p.zpeer(2)[1]
    landed(xg.at[0, pl.ds(0, 64)], xr.at[2])
    landed(xg.at[0, pl.ds(0, 64)], xr.at[4])
    c.to(sib, xg.at[t2], xg.at[t2], fr.at[2])
    project(t1)
    project(t3)
    landed(xg.at[0], xr.at[0])
    project(p.sibling()[0])
    project(t2)
    for k in (1, 3, 2):
        landed(xg.at[0], fr.at[k])
        project(lax.rem(p.z + 4 - k, 4) * 2 + 1 - p.core)

    def kv_to(a, b, src, n, span=None, recv=None):
        src, dst = kvall.at[src], kvall.at[n]
        if span is not None:
            src, dst = src.at[span], dst.at[span]
        c.to(p.cp(a, b), src, dst, kr.at[n if recv is None else recv])

    kv_to(0, 1, 0, 1)
    kv_to(0, 3, 0, 2)
    kv_to(1, 0, 0, 3)
    kept = (
        (qp, qp_out),
        (raw, raw_out),
        (wqkv, wqkv_out),
        (tabc, tabc_out),
        (tabs, tabs_out),
        (normed, normed_out),
        (normed_t, normed_t_out),
    )
    for src, dst in kept:
        c.own(src, dst)

    acc[...] = jnp.zeros_like(acc)
    lsum[...] = jnp.zeros_like(lsum)

    def work(n, _):
        kvb = kvall[n]

        def block(i, _):
            for u in range(UNROLL):
                rows = pl.ds(pl.multiple_of((i * UNROLL + u) * QB, QB), QB)
                e = jnp.exp2(dot(qp[rows, :], kvb, NT))
                total = e[:, 0:128]
                for j in range(1, 8):
                    total = total + e[:, j * 128 : (j + 1) * 128]
                lsum[rows, :] += total
                acc[rows, :] += dot(e.astype(BF), kvb)
            return 0

        lax.fori_loop(0, 2048 // QB // UNROLL, block, 0)
        return 0

    first, second = pl.ds(0, 512), pl.ds(512, 512)
    half = kvall.at[0, first]
    work(0, 0)
    landed(kvall.at[0], kr.at[1])
    kv_to(0, 1, 1, 4, first)
    kv_to(1, 0, 1, 5)
    landed(kvall.at[0], kr.at[2])
    kv_to(0, 3, 2, 4, second, 8)
    kv_to(1, 0, 2, 6)
    cot_rows([0] + ALONG_BOTH[0:7])
    lax.fori_loop(1, 3, work, 0)
    landed(half, kr.at[4])
    landed(half, kr.at[8])
    kv_to(1, 0, 4, 7)
    for i, (src, dst) in enumerate(weights):
        if i:
            c.to(p.partner(), src, part(dst, i, at_own), hr.at[i])
    landed(kvall.at[0], kr.at[3])
    lax.fori_loop(3, 5, work, 0)
    for k in (1, 3, 2):
        landed(wob, wor.at[k])
        block = wo.at[:, p.zpeer(-k)[1]]
        c.to(sib, block, block, wofr.at[k])

    def arrived(n, _):
        landed(kvall.at[0], kr.at[n])
        return work(n, 0)

    lax.fori_loop(5, 8, arrived, 0)

    for t in range(8):
        parts = []
        for h in range(2):
            rows = pl.ds(h * 1024 + t * 128, 128)
            total = jnp.sum(lsum[rows, :], axis=1, keepdims=True)
            parts.append(acc[rows, :] / total)
        whole = jnp.where(lane < 64, pltpu.roll(parts[0], 64, 1), parts[1])
        o[pl.ds(t * 128, 128), :] = whole
        att_t[pl.ds(t * 128, 128), :] = whole.astype(BF)
    for k in range(1, 8):
        t, dev = p.tp(k)
        block = att_t.at[pl.ds(pl.multiple_of(t * 128, 128), 128)]
        c.to(dev, block, attg.at[p.t], ar)
    own_att = c.here(att_t.at[pl.ds(pl.multiple_of(p.t * 128, 128), 128)], attg.at[p.t])
    cot_rows(ALONG_BOTH[7:9])
    ones = jnp.ones((8, 128), F32)
    for h in range(2):
        lse[h] = jnp.log2(dot_exact(ones, lsum[pl.ds(h * 1024, 1024), :], NT))
    for src, dst in ((o, o_out), (att_t, att_out), (lse, lse_out), (kvall, kv_out)):
        c.own(src, dst)
    for i, (_, dst) in enumerate(weights):
        piece = part(dst, i, from_partner)
        landed(piece, hr.at[i])
        c.to(sib, piece, part(dst, i, at_sib_partner), efr.at[i])
    own_wo.wait()
    landed(wob, wor.at[0])
    for k in (1, 3, 2):
        landed(wob, wofr.at[k])
    load_x.wait()
    own_att.wait()
    landed(attg.at[pl.ds(0, 7)], ar)

    att = jnp.concatenate([attg[t] for t in range(8)], axis=1)
    square = jnp.zeros((128, 1), F32)
    for j in range(4):
        cols = slice(j * 256, (j + 1) * 256)
        value = xv[:, cols].astype(F32) + dot(att, wo[:, :, :, cols].reshape(1024, 256))
        residual[:, cols] = value
        square = square + jnp.sum(value * value, axis=1, keepdims=True)
    factor = lax.rsqrt(square * (1.0 / 1024) + EPS)
    value = (residual[...] * factor * gmv[...]).astype(BF)
    for j in range(4):
        rows = dot(slots_t[j * 384 : (j + 1) * 384, :], value).astype(BF)
        outgoing[j * 8 : (j + 1) * 8] = rows.reshape(8, 48, 1024)

    for i, (_, dst) in enumerate(weights):
        landed(part(dst, i, at_sib), er.at[i])
        landed(part(dst, i, at_sib), efr.at[i])
    landed(grads.at[pl.ds(0, 30)], cr)
    c.done()


def front(*operands):
    shape = jax.ShapeDtypeStruct
    v = pltpu.VMEM
    return pl.pallas_call(
        front_kernel,
        out_shape=(
            shape((32, 48, 1024), BF),
            shape((128, 1024), F32),
            shape((8, 8, 16, 1152), BF),
            shape((128, 1536), BF),
            shape((32, 48, 1024), BF),
            shape((1024, 512), BF),
            shape((1024, 512), BF),
            shape((512, 1024), BF),
            shape((1024, 128), F32),
            shape((1024, 128), BF),
            shape((2, 8, 1024), F32),
            shape((8, 1024, 128), BF),
            shape((2048, 128), BF),
            shape((1024, 256), F32),
            shape((1024, 256), BF),
            shape((1024, 128), F32),
            shape((1024, 128), F32),
            shape((1024, 1024), BF),
            shape((1024, 1024), BF),
            shape((2, 128, 768), BF),
        ),
        in_specs=[HBM] * 17,
        out_specs=(VMEM,) * 4 + (HBM,) * 16,
        scratch_shapes=[
            v((128, 1024), BF),
            v((128, 1024), BF),
            v((8, 128), jnp.int32),
            v((1, 128), jnp.int32),
            v((8, 1024), BF),
            v((8, 512), BF),
            v((8, 512), BF),
            v((8, 1024), BF),
            v((8, 32), BF),
            v((1, 1024), F32),
            v((1, 1024), F32),
            v((1, 64), F32),
            v((1, 64), F32),
            v((1, 128), F32),
            v((8, 16, 128), BF),
            v((80, 128), BF),
            v((8, 128), F32),
            v((8, 128, 1024), BF),
            v((16, 8, 16, 128), BF),
            v((16, 80, 128), BF),
            v((8, 16, 1152), BF),
            v((8, 8, 128), F32),
            v((8, 16, 128), BF),
            v((32, 48, 1024), BF),
            v((1024, 1024), BF),
            v((1024, 1024), BF),
            v((1536, 128), BF),
            v((768, 128), BF),
            v((2, 128, 768), BF),
            v((32, 128), F32),
            v((8, 128), jnp.int32),
            v((128, 1024), BF),
            v((2048, 128), BF),
            v((8, 1024, 128), BF),
            v((1024, 256), F32),
            v((1024, 256), BF),
            v((1024, 128), F32),
            v((1024, 128), F32),
            v((2048, 128), F32),
            v((2048, 128), F32),
            v((1024, 128), F32),
            v((1024, 128), BF),
            v((2, 8, 1024), F32),
            v((8, 128, 128), BF),
            DMA((176,)),
            DMA((5,)),
            DMA((4,)),
            DMA,
            DMA,
            DMA,
            DMA,
            DMA,
            DMA((10,)),
            DMA,
            DMA((3,)),
            DMA((3,)),
            DMA((3,)),
            DMA((4,)),
            DMA((4,)),
            DMA((2,)),
        ],
        compiler_params=params(0, VMEM_MIB),
        name="front",
    )(*operands)


KB = 256
GB = 1024
EARLY = 4


def expert_kernel(
    outgoing,
    residual,
    wo,
    slots,
    grads_in,
    ewg,
    ewu,
    ewd,
    cot_in,
    gain_in,
    qp_in,
    kv_in,
    lse_in,
    branch,
    gat,
    grad_residual_out,
    grad_ffn_out,
    mixed_out,
    dwg_out,
    dwu_out,
    dwd_out,
    dwr_out,
    residual_out,
    weights_out,
    cot,
    gain,
    mixed,
    dwg,
    dwu,
    dwd,
    dwr,
    grad_residual,
    grad_ffn,
    rows,
    grads,
    wg,
    wu,
    wd,
    gh,
    gp,
    up,
    hid,
    gl,
    gin,
    back,
    sg,
    su,
    sd,
    rg,
    ru,
    rd,
    qp,
    kvall,
    lse,
    tiles,
    ss,
    rr,
    br,
    wr,
    ts,
):
    p = Place()
    _, sib = p.sibling()
    sem = greet(p.all_chips() + [sib])
    c = Copies(ss)
    own_rows = c.here(outgoing.at[p.chip], rows.at[0])
    local = [c.here(grads_in, grads), c.here(ewd, wd), c.here(ewg, wg), c.here(ewu, wu)]
    load_cot, load_gain = c.here(cot_in, cot), c.here(gain_in, gain)
    attention = [c.here(qp_in, qp), c.here(kv_in, kvall), c.here(lse_in, lse)]
    c.own(residual, residual_out)
    pl.semaphore_wait(sem, 31 + 1)
    for s in range(1, 32):
        e, dev = p.chips(s)
        c.to(dev, outgoing.at[e], rows.at[s], rr.at[s // 4])
    own_rows.wait()
    for copy in local:
        copy.wait()

    def hidden_grads(j, _):
        block = grads[pl.ds(j * 4, 4)].reshape(192, 1024)
        gh[pl.ds(pl.multiple_of(j * 192, 64), 192), :] = dot(block, wd[...], NT)
        return 0

    lax.fori_loop(0, 8, hidden_grads, 0)

    def weights_of(n, _):
        for j in range(1024 // KB):

            @pl.when(n > 0)
            def _(j=j):
                pltpu.make_async_copy(tiles.at[j], weights_out.at[0], ts.at[j]).wait()

            for i in range(2048 // GB):
                h, cols = i * GB // 1024, pl.ds(i * GB % 1024, GB)
                scores = dot(kvall[n, j * KB : (j + 1) * KB, :], qp[pl.ds(i * GB, GB), :], NT)
                value = jnp.exp2(scores - lse[h, 0:1, cols])
                tiles[j, :, i * GB : (i + 1) * GB] = value.astype(BF)
            tile = weights_out.at[n * (1024 // KB) + j]
            pltpu.make_async_copy(tiles.at[j], tile, ts.at[j]).start()
        return 0

    for copy in attention:
        copy.wait()
    lax.fori_loop(0, EARLY, weights_of, 0)

    lane = lax.broadcasted_iota(jnp.int32, (192, 128), 1)
    here = jnp.where(lane == p.chip, 1.0, 0.0)
    router = wo[:, :, :, 1024:].reshape(1024, 128)

    for j in range(8):
        landed(rows.at[pl.ds(0, 4 if j else 3)], rr.at[j])
        block = rows[4 * j : 4 * j + 4].reshape(192, 1024)
        span = pl.ds(j * 192, 192)
        gate_pre = dot(block, wg[...])
        up_pre = dot(block, wu[...])
        logits = jnp.where(lane < 32, dot(block, router), -1e30)
        expo = jnp.exp(logits - jnp.max(logits, axis=1, keepdims=True))
        probs = expo / jnp.sum(expo, axis=1, keepdims=True)
        gate = jnp.sum(probs * here, axis=1, keepdims=True)
        sig = jax.nn.sigmoid(gate_pre)
        act = gate_pre * sig
        hidden = act * up_pre
        grad_hidden = gh[span, :]
        weight = jnp.sum(hidden * grad_hidden, axis=1, keepdims=True) * gate
        grad_hidden = grad_hidden * gate
        grad_gate = (grad_hidden * up_pre * sig * (1.0 + gate_pre * (1.0 - sig))).astype(BF)
        grad_up = (grad_hidden * act).astype(BF)
        grad_logits = (weight * (here - probs)).astype(BF)
        hid[span, :] = (hidden * gate).astype(BF)
        gp[span, :] = grad_gate
        up[span, :] = grad_up
        gl[span, :] = grad_logits
        total = dot(grad_gate, wg[...], NT) + dot(grad_up, wu[...], NT)
        total = total + dot(grad_logits, router, NT)
        gin[4 * j : 4 * j + 4] = total.astype(BF).reshape(4, 48, 1024)
        for s in range(4 * j, 4 * j + 4):
            if s:
                c.to(p.chips(s, -1)[1], gin.at[s], back.at[p.chip], br)
            else:
                own_back = c.here(gin.at[0], back.at[p.chip])

    for m in range(4):
        cols = slice(m * 256, (m + 1) * 256)
        left = rows[:, :, cols].reshape(1536, 256)
        for src, own, sends in ((gp, dwg, sg), (up, dwu, su)):
            value = dot(left, src[...], TN).astype(BF)
            for q in range(2):
                own[q, cols, :] = value[:, q * 128 : (q + 1) * 128]
                sends[q, cols, :] = value[:, (2 + q) * 128 : (3 + q) * 128]
        dwr[cols, :] = dot(left, gl[...], TN)
    for m in range(4):
        cols = slice(m * 256, (m + 1) * 256)
        right = grads[:, :, cols].reshape(1536, 256)
        value = dot(hid[...], right, TN).astype(BF)
        dwd[:, :, cols] = value[:256].reshape(2, 128, 256)
        sd[:, :, cols] = value[256:].reshape(2, 128, 256)
    for i, (src, dst) in enumerate(((sg, rg), (su, ru), (sd, rd))):
        c.to(sib, src, dst, wr.at[i])

    def outputs(j, _):
        block = hid[pl.ds(pl.multiple_of(j * 192, 64), 192), :]
        mixed[pl.ds(j * 4, 4)] = dot(block, wd[...]).astype(BF).reshape(4, 48, 1024)
        return 0

    lax.fori_loop(0, 8, outputs, 0)
    c.own(mixed, mixed_out)
    c.own(dwr, dwr_out)
    lax.fori_loop(EARLY, 8, weights_of, 0)
    for i, (got, own) in enumerate(((rg, dwg), (ru, dwu), (rd, dwd))):
        landed(got, wr.at[i])
        own[...] = (own[...].astype(F32) + got[...].astype(F32)).astype(BF)
    for src, dst in ((dwg, dwg_out), (dwu, dwu_out), (dwd, dwd_out)):
        c.own(src, dst)
    load_cot.wait()
    load_gain.wait()

    for j in range(1024 // KB):
        pltpu.make_async_copy(tiles.at[j], weights_out.at[0], ts.at[j]).wait()

    landed(back.at[pl.ds(0, 31)], br)
    own_back.wait()
    res = residual[...]
    factor = lax.rsqrt(jnp.mean(res * res, axis=1, keepdims=True) + EPS)
    normed = res * factor
    for j in range(4):
        cols = slice(j * 256, (j + 1) * 256)
        grad_residual[:, cols] = dot(slots[...], back[:, :, cols].reshape(1536, 256))
    grad_mid = grad_residual[...]
    part = jnp.sum(grad_mid * normed, axis=0, keepdims=True)
    grad_ffn[...] = jnp.broadcast_to(part, (8, 1024))
    g = grad_mid * gain[...]
    g = factor * (g - normed * jnp.mean(g * normed, axis=1, keepdims=True))
    g = cot[...].astype(F32) + g
    grad_residual[...] = g
    low = g.astype(BF)
    branch[...] = low
    for t in range(8):
        weights = wo[t][:, :, :1024].reshape(128, 1024)
        gat[t] = dot(low, weights, NT).astype(BF)
    c.own(grad_residual, grad_residual_out)
    c.own(grad_ffn, grad_ffn_out)
    c.done()


def expert_rows(*operands):
    shape = jax.ShapeDtypeStruct
    v = pltpu.VMEM
    return pl.pallas_call(
        expert_kernel,
        out_shape=(
            shape((128, 1024), BF),
            shape((8, 128, 128), BF),
            shape((128, 1024), F32),
            shape((8, 1024), F32),
            shape((32, 48, 1024), BF),
            shape((2, 1024, 128), BF),
            shape((2, 1024, 128), BF),
            shape((2, 128, 1024), BF),
            shape((1024, 128), F32),
            shape((128, 1024), F32),
            shape((8 * 1024 // KB, KB, 2048), BF),
        ),
        in_specs=[VMEM] * 4 + [HBM] * 9,
        out_specs=(VMEM,) * 2 + (HBM,) * 9,
        scratch_shapes=[
            v((128, 1024), BF),
            v((1, 1024), F32),
            v((32, 48, 1024), BF),
            v((2, 1024, 128), BF),
            v((2, 1024, 128), BF),
            v((2, 128, 1024), BF),
            v((1024, 128), F32),
            v((128, 1024), F32),
            v((8, 1024), F32),
            v((32, 48, 1024), BF),
            v((32, 48, 1024), BF),
            v((1024, 512), BF),
            v((1024, 512), BF),
            v((512, 1024), BF),
            v((1536, 512), F32),
            v((1536, 512), BF),
            v((1536, 512), BF),
            v((1536, 512), BF),
            v((1536, 128), BF),
            v((32, 48, 1024), BF),
            v((32, 48, 1024), BF),
            v((2, 1024, 128), BF),
            v((2, 1024, 128), BF),
            v((2, 128, 1024), BF),
            v((2, 1024, 128), BF),
            v((2, 1024, 128), BF),
            v((2, 128, 1024), BF),
            v((2048, 128), BF),
            v((8, 1024, 128), BF),
            v((2, 8, 1024), F32),
            v((1024 // KB, KB, 2048), BF),
            DMA((96,)),
            DMA((8,)),
            DMA,
            DMA((3,)),
            DMA((1024 // KB,)),
        ],
        compiler_params=params(1, VMEM_MIB),
        name="experts",
    )(*operands)


ORDER = (5, 6, 7, 3, 4, 1, 2, 0)
AHEAD = 2


def back_kernel(
    branch,
    gat,
    grad_residual_in,
    grad_ffn_in,
    mixed,
    dwg,
    dwu,
    dwd,
    dwr_in,
    residual_in,
    probs,
    o_in,
    att_in,
    kv_in,
    qp_in,
    raw_in,
    wqkv_in,
    tabc_in,
    tabs_in,
    normed_in,
    normed_t_in,
    near_in,
    x_in,
    gain_a,
    gain_q,
    gain_k,
    wq_in,
    wk_in,
    wv_in,
    layer_out,
    input_out,
    query_out,
    key_out,
    value_out,
    output_out,
    rows_out,
    misc_out,
    gate_out,
    up_out,
    down_out,
    layer_output,
    grad_input,
    grad_query,
    grad_key,
    grad_value,
    vectors,
    misc,
    out_g,
    out_u,
    out_d,
    grad_residual,
    grad_ffn,
    dwr,
    residual,
    near,
    ypart,
    ypeer,
    o,
    att_t,
    tiles,
    kvall,
    qp,
    raw,
    wqkv,
    tabc,
    tabs,
    normed,
    normed_t,
    xv,
    gav,
    gqv,
    gkv,
    wqv,
    wkv,
    wvv,
    own_g,
    own_u,
    own_d,
    rwg,
    rwu,
    rwd,
    yret,
    dqt,
    earlyr,
    gatr,
    dop,
    delta,
    acc,
    bg,
    early,
    dwos,
    dwol,
    dks,
    dkr,
    draw,
    dx,
    dwm,
    sibr,
    zsend,
    zr,
    dwin,
    d2s,
    d2l,
    ss,
    ar,
    bs,
    fs,
    yr,
    er,
    sr,
    os_,
    ors,
    dsr,
    zrs,
    wrs,
    trs,
    ypr,
    ts,
):
    p = Place()
    _, sib = p.sibling()
    c = Copies(ss)
    first = [
        c.here(src, dst)
        for src, dst in ((o_in, o), (qp_in, qp), (kv_in, kvall), (att_in, att_t))
    ]
    for k in range(AHEAD):
        pltpu.make_async_copy(probs.at[ORDER[0] * 1024 // KB + k], tiles.at[k], ts.at[k]).start()
    own_gat = c.here(gat.at[p.t], gatr.at[p.t])
    own_bg = c.here(branch, bg.at[p.t])
    sem = greet(p.all_chips() + p.all_tp() + p.all_gf())
    mirror = p.t * 8 + p.g
    at_home = p.g == p.t

    @pl.when(jnp.logical_not(at_home))
    def _():
        pl.semaphore_signal(sem, inc=1, device_id=(mirror, p.f), device_id_type=MESH)

    pl.semaphore_wait(sem, 31 + 7 + 15 + jnp.where(at_home, 0, 1))
    for k in range(1, 8):
        t, dev = p.tp(k)
        c.to(dev, gat.at[t], gatr.at[p.t], ar)
    here = p.y * 4 + p.z
    own_mixed = c.here(mixed.at[pl.ds(0, 2)], yret.at[here])

    def outputs(which):
        for m in which:
            c.to(p.plane(m, -1)[1], mixed.at[pl.ds(2 * m, 2)], yret.at[here], yr)

    outputs(ALONG_Y)
    own_gat.wait()
    for copy in first:
        copy.wait()
    landed(gatr.at[pl.ds(0, 7)], ar)
    owned = ((dwg, own_g, rwg, out_g), (dwu, own_u, rwu, out_u), (dwd, own_d, rwd, out_d))
    owned_copies = []
    for i, (src, mine, got, _) in enumerate(owned):
        owned_copies.append(c.here(src.at[p.f], mine))

    outputs(ALONG_BOTH + ALONG_Z)
    for k in (1, 3, 2):
        c.to(p.zpeer(k)[2], branch, bg.at[p.t], bs.at[k])
    c.to(sib, branch, bg.at[p.t], bs.at[0])
    later = (
        (raw_in, raw),
        (wqkv_in, wqkv),
        (tabc_in, tabc),
        (tabs_in, tabs),
        (normed_in, normed),
        (normed_t_in, normed_t),
        (grad_residual_in, grad_residual),
        (residual_in, residual),
        (near_in, near),
        (x_in, xv),
        (gain_a, gav),
        (gain_q, gqv),
        (gain_k, gkv),
        (wq_in, wqv),
        (wk_in, wkv),
        (wv_in, wvv),
    )
    soon = ((grad_ffn_in, grad_ffn), (dwr_in, dwr))
    soon = [c.here(src, dst) for src, dst in soon]
    later = [c.here(src, dst) for src, dst in later]

    lane = lanes(128)
    ones = jnp.ones((8, 128), F32)
    for t in range(8):
        both = gatr[t].astype(F32)
        rows = pl.ds(t * 128, 128)
        dop[rows, :] = jnp.where(lane < 64, 0.0, pltpu.roll(both, 64, 1)).astype(BF)
        dop[pl.ds(1024 + t * 128, 128), :] = jnp.where(lane < 64, 0.0, both).astype(BF)
        prod = both * o[rows, :]
        for h in range(2):
            value = jnp.where((lane < 64) == (h == 0), prod, 0.0)
            delta[h, :, rows] = dot_exact(ones, value, NT)
    dqt[...] = jnp.zeros_like(dqt)

    per = 1024 // KB

    def fetch(tile, k):
        slot = lax.rem(k, AHEAD + 1)
        return pltpu.make_async_copy(probs.at[tile], tiles.at[slot], ts.at[slot])

    def work(n):
        at = ORDER.index(n)

        def keys(j, _):
            k = at * per + j
            later = j + AHEAD

            @pl.when(k + AHEAD < 8 * per)
            def _():
                after = ORDER[min(at + 1, 7)]
                tile = jnp.where(later < per, n * per + later, after * per + later - per)
                fetch(tile, k + AHEAD).start()

            fetch(0, k).wait()
            slot = lax.rem(k, AHEAD + 1)
            krows = pl.ds(pl.multiple_of(j * KB, KB), KB)
            kvb = kvall[n, krows, :]
            kt = kvb.T[:64, :]
            total = jnp.zeros((KB, 128), F32)
            for i in range(2048 // GB):
                rows = pl.ds(i * GB, GB)
                h, cols = i * GB // 1024, pl.ds(i * GB % 1024, GB)
                q = qp[rows, :]
                d = dop[rows, :]
                w = tiles[slot, :, i * GB : (i + 1) * GB]
                ds = (w.astype(F32) * (dot(kvb, d, NT) - delta[h, 0:1, cols])).astype(BF)
                total = total + dot(w, d) + dot(ds, q)
                dqt[h * 64 : (h + 1) * 64, cols] += dot(kt, ds)
            acc[krows, :] = total
            return 0

        lax.fori_loop(0, per, keys, 0)

    def chunk_x(n):
        work(n)
        dks[n] = acc[...].astype(BF)
        m = MEMBERS.index((0, MEMBERS[n][1]))
        c.to(p.cp(1, 0), dks.at[n], dkr.at[m], sr.at[m])

    def chunk_y(n):
        work(n)
        landed(dkr.at[0], sr.at[n])
        dks[n] = (acc[...] + dkr[n].astype(F32)).astype(BF)
        m = MEMBERS.index((1, MEMBERS[n][1]))
        c.to(p.cp(0, -MEMBERS[n][1]), dks.at[n], dkr.at[m], sr.at[m])

    chunk_x(5)
    chunk_x(6)
    chunk_x(7)
    chunk_x(3)
    for i, (src, _, got, _) in enumerate(owned):
        c.to(p.partner(), src.at[1 - p.f], got, er.at[i])
    chunk_y(4)
    chunk_y(1)
    chunk_y(2)
    spot = lax.broadcasted_iota(jnp.int32, (128, 128), 0)
    same = jnp.logical_and(lax.div(spot, 16) == lax.div(lane, 8), lax.rem(spot, 8) == lax.rem(lane, 8))
    picks = [
        jnp.where(jnp.logical_and(same, lax.rem(lax.div(spot, 8), 2) == f), 1.0, 0.0)
        for f in range(2)
    ]
    sub16 = lax.broadcasted_iota(jnp.int32, (16, 128), 0)

    def rows_of(value, f):
        return jnp.concatenate(
            [value[(2 * t + f) * 8 : (2 * t + f) * 8 + 8, :] for t in range(8)], axis=0
        )
    me = p.g * 2 + p.f
    work(0)

    for copy in later:
        copy.wait()
    head_gains = (
        jnp.concatenate([gqv[...], gqv[...]], axis=1),
        jnp.concatenate([gkv[...], jnp.ones((1, 64), F32)], axis=1),
    )

    def through(i, rows, grad):
        cosine, sine = tabc[rows, :], tabs[rows, :]
        value = raw[rows, i * 128 : (i + 1) * 128]
        grad = grad * cosine - swap(grad) * sine
        factor = lax.rsqrt(head_mean(value * value) + EPS)
        value = value * factor
        total = jnp.sum(grad * value, axis=0, keepdims=True)
        grad = grad * head_gains[i]
        return total, factor * (grad - value * head_mean(grad * value))

    gains_q = jnp.zeros((1, 128), F32)
    for t in range(8):
        rows = slice(t * 128, (t + 1) * 128)
        total, value = through(0, rows, dqt[:, rows].T * 0.125)
        gains_q = gains_q + total
        draw[rows, 0:128] = value.astype(BF)
    def head_columns(g, cols):
        rows = pl.ds(pl.multiple_of(g * 128, 128), 128)
        value = dot(normed_t[rows, :], draw[:, cols])
        for f in range(2):
            dwm[g * 2 + f, 0:64, cols] = rows_of(value, f).astype(BF)

    for g in range(8):
        head_columns(g, slice(0, 128))
    for k in (1, 3, 2):
        landed(branch, bs.at[k])
        block = bg.at[p.zpeer(-k)[1]]
        c.to(sib, block, block, fs.at[k])
    for n in (0, 5, 7, 6):
        landed(dkr.at[0], sr.at[n])
    gains_k = jnp.zeros((1, 128), F32)
    for t in range(8):
        rows = slice(t * 128, (t + 1) * 128)
        whole = acc[rows, :]
        for n in (0, 5, 7, 6):
            whole = whole + dkr[n, rows, :].astype(F32)
        total, value = through(1, rows, whole * LN2)
        gains_k = gains_k + total
        draw[rows, 128:256] = jnp.where(lane < 64, value, whole).astype(BF)
    gains = jnp.concatenate([gains_q, jnp.where(lanes(1) < 64, gains_k, 0.0)], axis=1)
    wide16 = lax.broadcasted_iota(jnp.int32, (16, 256), 0)
    gains = jnp.where(wide16 == 0, gains, 0.0).astype(BF)
    for r in range(16):
        dwm[r, 64:80, :] = gains
    for j in range(8):
        g = lax.rem(p.g + j, 8)
        head_columns(g, slice(128, 256))
        if j:
            for f in range(2):
                c.to((g * 8 + p.t, f), dwm.at[g * 2 + f], dwin.at[me], wrs)
        else:
            c.to(p.partner(), dwm.at[g * 2 + 1 - p.f], dwin.at[me], wrs)
            own_dw = c.here(dwm.at[me], dwin.at[me])

    def input_grad(core, z):
        rows = pl.ds(pl.multiple_of((z * 2 + core) * 128, 128), 128)
        left = draw[rows, :]
        for j in range(4):
            cols = slice(j * 256, (j + 1) * 256)
            dx[core, z, :, cols] = dot(left, wqkv[cols, :], NT).astype(BF)

    for k in (1, 3, 2, 0):
        z = lax.rem(p.z + k, 4)
        input_grad(1 - p.core, z)
        c.to(sib, dx.at[1 - p.core, z], sibr.at[z], dsr.at[k])
    for k in (1, 3, 2):
        z, _, dev = p.zpeer(k)
        input_grad(p.core, z)
        landed(sibr.at[0], dsr.at[k])
        zsend[k] = (dx[p.core, z].astype(F32) + sibr[z].astype(F32)).astype(BF)
        c.to(dev, zsend.at[k], zr.at[k], zrs.at[k])
    input_grad(p.core, p.z)

    own_bg.wait()
    landed(branch, bs.at[0])
    for k in (1, 3, 2):
        landed(branch, fs.at[k])
    for j in range(4):
        cols = slice(j * 256, (j + 1) * 256)
        total = jnp.zeros((128, 256), F32)
        for t in range(8):
            total = total + dot(att_t[t * 128 : (t + 1) * 128, :], bg[t, :, cols], TN)
        for r in range(16):
            block = total[r * 8 : (r + 1) * 8, :]
            both = [block[:, :128], block[:, 128:]]
            early[r, j * 16 : (j + 1) * 16, :] = jnp.concatenate(both, axis=0).astype(BF)
    for copy in soon:
        copy.wait()
    for g in range(8):
        span = slice(g * 128, (g + 1) * 128)
        value = dwr[span, :]
        for f in range(2):
            early[g * 2 + f, 64:128, :] = rows_of(value, f).astype(BF)
            line = dot_exact(grad_ffn[0:1, span], picks[f])
            early[g * 2 + f, 128:144, :] = jnp.where(sub16 == 0, line, 0.0).astype(BF)
    for k in range(1, 16):
        r, dev = p.gf(k)
        c.to(dev, early.at[r], earlyr.at[me], ors)
    own_early = c.here(early.at[me], earlyr.at[me])

    own_mixed.wait()
    landed(yret.at[pl.ds(0, 15)], yr)
    for j in range(4):
        cols = slice(j * 256, (j + 1) * 256)
        ypart[:, cols] = dot(near[1], yret[:, 1, :, cols].reshape(768, 256)).astype(BF)
    c.to(p.cp(1, 0), ypart, ypeer, ypr)
    for j in range(4):
        cols = slice(j * 256, (j + 1) * 256)
        residual[:, cols] += dot(near[0], yret[:, 0, :, cols].reshape(768, 256))

    landed(sibr.at[0], dsr.at[0])
    whole = dx[p.core, p.z].astype(F32) + sibr[p.z].astype(F32)
    for i, (_, mine, got, out) in enumerate(owned):
        owned_copies[i].wait()
        landed(got, er.at[i])
        out[...] = mine[...].astype(F32) + got[...].astype(F32)
    for src, dst in ((out_g, gate_out), (out_u, up_out), (out_d, down_out)):
        c.own(src, dst)
    own_early.wait()
    landed(earlyr.at[pl.ds(0, 15)], ors)
    before = earlyr[0].astype(F32)
    for r in range(1, 16):
        before = before + earlyr[r].astype(F32)
    for i in range(8):
        dwos[:, i * 128 : (i + 1) * 128] = before[i * 8 : (i + 1) * 8, :]

    @pl.when(jnp.logical_not(at_home))
    def _():
        pltpu.make_async_remote_copy(
            src_ref=dwos,
            dst_ref=dwol,
            send_sem=os_.at[0],
            recv_sem=os_.at[1],
            device_id=(mirror, p.f),
            device_id_type=MESH,
        ).start()

    @pl.when(at_home)
    def _():
        pltpu.make_async_copy(dwos, dwol, os_.at[2]).start()

    own_dw.wait()
    landed(dwin.at[pl.ds(0, 15)], wrs)
    total = dwin[0].astype(F32)
    for r in range(1, 16):
        total = total + dwin[r].astype(F32)
    eight = lax.broadcasted_iota(jnp.int32, (8, 128), 0)
    for t in range(8):
        d2s[t, 0:8, :] = total[t * 8 : (t + 1) * 8, :]
        turn = (128 - 8 * t) % 128
        line = jnp.broadcast_to(before[128:129, :], (8, 128))
        line = pltpu.roll(line, turn, 1) if turn else line
        lines = jnp.where(eight == 0, total[64:65, 0:128], line)
        lines = jnp.where(eight == 1, total[64:65, 128:256], lines)
        d2s[t, 8:16, 0:128] = lines
        d2s[t, 8:16, 128:256] = before[64 + t * 8 : 72 + t * 8, :]
    for k in range(1, 8):
        t, dev = p.tp(k)
        c.to(dev, d2s.at[t], d2l.at[p.t], trs)
    own_d2 = c.here(d2s.at[p.t], d2l.at[p.t])

    for k in (1, 3, 2):
        landed(zr.at[0], zrs.at[k])
        whole = whole + zr[k].astype(F32)
    xf = xv[...].astype(F32)
    factor = lax.rsqrt(jnp.mean(xf * xf, axis=1, keepdims=True) + EPS)
    n = xf * factor
    g = whole * gav[...]
    g = factor * (g - n * jnp.mean(g * n, axis=1, keepdims=True))
    grad_input[...] = grad_residual[...] + g
    c.own(grad_input, input_out)
    landed(ypeer, ypr)
    layer_output[...] = (residual[...] + ypeer[...].astype(F32)).astype(BF)
    c.own(layer_output, layer_out)

    @pl.when(jnp.logical_not(at_home))
    def _():
        landed(dwos, os_.at[0])
        landed(dwol, os_.at[1])

    @pl.when(at_home)
    def _():
        landed(dwol, os_.at[2])

    c.own(dwol, output_out)
    own_d2.wait()
    landed(d2l.at[pl.ds(0, 7)], trs)
    low8 = lanes(8) < 64
    totals = [jnp.zeros((8, 128), F32)] * 2
    for t in range(8):
        grad_query[:, t * 128 : (t + 1) * 128] = d2l[t, 0:8, 0:128]
        totals = [totals[i] + d2l[t, 8:16, i * 128 : (i + 1) * 128] for i in range(2)]
    for i in range(4):
        one, two = d2l[2 * i, 0:8, 128:256], d2l[2 * i + 1, 0:8, 128:256]
        cols = slice(i * 128, (i + 1) * 128)
        grad_key[:, cols] = jnp.where(low8, one, pltpu.roll(two, 64, 1))
        grad_value[:, cols] = jnp.where(low8, pltpu.roll(one, 64, 1), two)
    both = totals[0] + pltpu.roll(totals[0], 64, 1)
    vectors[...] = jnp.where(eight == 0, both, totals[0])
    share = jnp.zeros((8, 1), F32)
    for weights, grads in ((wqv, grad_query), (wkv, grad_key), (wvv, grad_value)):
        product = weights[...].astype(F32) * grads[...]
        share = share + jnp.sum(product, axis=1, keepdims=True)
    wide = lax.broadcasted_iota(jnp.int32, (8, 1024), 1)
    feature = ((p.g * 8 + p.t) * 2 + p.f) * 8 + lax.broadcasted_iota(jnp.int32, (8, 1024), 0)
    own_gain = jnp.sum(jnp.where(wide == feature, gav[...], 0.0), axis=1, keepdims=True)
    misc[...] = jnp.where(lanes(8) == 33, share / own_gain, totals[1])
    last = (
        (grad_query, query_out),
        (grad_key, key_out),
        (grad_value, value_out),
        (vectors, rows_out),
        (misc, misc_out),
    )
    for src, dst in last:
        c.own(src, dst)
    c.done()


def back(*operands):
    shape = jax.ShapeDtypeStruct
    v = pltpu.VMEM
    return pl.pallas_call(
        back_kernel,
        out_shape=(
            shape((128, 1024), BF),
            shape((128, 1024), F32),
            shape((8, 1024), F32),
            shape((8, 512), F32),
            shape((8, 512), F32),
            shape((8, 1024), F32),
            shape((8, 128), F32),
            shape((8, 128), F32),
            shape((1024, 128), F32),
            shape((1024, 128), F32),
            shape((128, 1024), F32),
        ),
        in_specs=[VMEM] * 2 + [HBM] * 27,
        out_specs=(HBM,) * 11,
        scratch_shapes=[
            v((128, 1024), BF),
            v((128, 1024), F32),
            v((8, 1024), F32),
            v((8, 512), F32),
            v((8, 512), F32),
            v((8, 128), F32),
            v((8, 128), F32),
            v((1024, 128), F32),
            v((1024, 128), F32),
            v((128, 1024), F32),
            v((128, 1024), F32),
            v((8, 1024), F32),
            v((1024, 128), F32),
            v((128, 1024), F32),
            v((2, 128, 768), BF),
            v((128, 1024), BF),
            v((128, 1024), BF),
            v((1024, 128), F32),
            v((1024, 128), BF),
            v((AHEAD + 1, KB, 2048), BF),
            v((8, 1024, 128), BF),
            v((2048, 128), BF),
            v((1024, 256), F32),
            v((1024, 256), BF),
            v((1024, 128), F32),
            v((1024, 128), F32),
            v((1024, 1024), BF),
            v((1024, 1024), BF),
            v((128, 1024), BF),
            v((1, 1024), F32),
            v((1, 64), F32),
            v((1, 64), F32),
            v((8, 1024), BF),
            v((8, 512), BF),
            v((8, 512), BF),
            v((1024, 128), BF),
            v((1024, 128), BF),
            v((128, 1024), BF),
            v((1024, 128), BF),
            v((1024, 128), BF),
            v((128, 1024), BF),
            v((16, 2, 48, 1024), BF),
            v((128, 1024), F32),
            v((16, 144, 128), BF),
            v((8, 128, 128), BF),
            v((2048, 128), BF),
            v((2, 8, 1024), F32),
            v((1024, 128), F32),
            v((8, 128, 1024), BF),
            v((16, 144, 128), BF),
            v((8, 1024), F32),
            v((8, 1024), F32),
            v((8, 1024, 128), BF),
            v((8, 1024, 128), BF),
            v((1024, 256), BF),
            v((2, 4, 128, 1024), BF),
            v((16, 80, 256), BF),
            v((4, 128, 1024), BF),
            v((4, 128, 1024), BF),
            v((4, 128, 1024), BF),
            v((16, 80, 256), BF),
            v((8, 16, 256), F32),
            v((8, 16, 256), F32),
            DMA((128,)),
            DMA,
            DMA((4,)),
            DMA((4,)),
            DMA,
            DMA((3,)),
            DMA((8,)),
            DMA((3,)),
            DMA,
            DMA((4,)),
            DMA((4,)),
            DMA,
            DMA,
            DMA,
            DMA((AHEAD + 1,)),
        ],
        compiler_params=params(2, VMEM_MIB),
        name="back",
    )(*operands)


def outputs_kernel(count, *refs):
    ins, outs, held = refs[:count], refs[count : 2 * count], refs[2 * count : 3 * count]
    sems = refs[-1]
    loads = [pltpu.make_async_copy(ins[i], held[i], sems.at[0, i]) for i in range(count)]
    for copy in loads:
        copy.start()
    stores = [
        pltpu.make_async_copy(held[i], outs[i], sems.at[1, i]) for i in range(count - 1)
    ]
    for i in range(count - 1):
        loads[i].wait()
        stores[i].start()
    loads[-1].wait()
    outs[-1][...] = held[-1][:, :32]
    for copy in stores:
        copy.wait()


def to_outputs(*arrays):
    count = len(arrays)
    shapes = [jax.ShapeDtypeStruct(a.shape, a.dtype) for a in arrays[:-1]]
    shapes.append(jax.ShapeDtypeStruct((8, 32), F32))
    return pl.pallas_call(
        functools.partial(outputs_kernel, count),
        out_shape=tuple(shapes),
        in_specs=[HBM] * count,
        out_specs=(HBM,) * (count - 1) + (VMEM,),
        scratch_shapes=[pltpu.VMEM(a.shape, a.dtype) for a in arrays] + [DMA((2, count))],
        compiler_params=pltpu.CompilerParams(vmem_limit_bytes=VMEM_MIB * 2**20),
        name="outputs",
    )(*arrays)


RATES = np.power(50000.0, -(np.arange(128) % 32) / 32.0).astype(np.float32).reshape(1, 128)


def local(
    layer_input,
    positions,
    routes,
    attn_gain,
    w_query,
    w_key,
    w_value,
    query_gain,
    key_gain,
    w_output,
    ffn_gain,
    w_router,
    w_gate,
    w_up,
    w_down,
    cotangent,
):
    x = layer_input[0]
    cot = cotangent[0]
    gain_a = attn_gain.reshape(1, 1024)
    gain_m = ffn_gain.reshape(1, 1024)
    gain_q = query_gain.reshape(1, 64)
    gain_k = key_gain.reshape(1, 64)
    (outgoing, residual, wo, slots, grads, ewg, ewu, ewd, *kept) = front(
        x,
        cot,
        routes[0].T,
        positions,
        w_query,
        w_key,
        w_value,
        w_output,
        w_router,
        gain_a,
        gain_m,
        gain_q,
        gain_k,
        jnp.asarray(RATES),
        w_gate[0],
        w_up[0],
        w_down[0],
    )
    o, att, lse, kv, qp, *rest = kept
    passed = expert_rows(
        outgoing, residual, wo, slots, grads, ewg, ewu, ewd, cot, gain_m, qp, kv, lse
    )
    results = back(*passed, o, att, kv, qp, *rest, x, gain_a, gain_q, gain_k, w_query, w_key, w_value)
    vectors = results[6]
    (
        layer_output,
        grad_input,
        grad_query,
        grad_key,
        grad_value,
        grad_output,
        grad_gate,
        grad_up,
        grad_down,
        grad_router,
    ) = to_outputs(*results[:6], *results[8:], results[7])
    return (
        layer_output[None],
        grad_input[None],
        results[7][:, 33],
        grad_query,
        grad_key,
        grad_value,
        vectors[0, :64],
        vectors[1, :64],
        grad_output,
        vectors[3, :8],
        grad_router,
        grad_gate[None],
        grad_up[None],
        grad_down[None],
    )


def solution(mesh):
    rows = P(("ctx", "fsdp"), None)
    vector = P(("ctx", "fsdp"))
    tokens = P("fsdp", "ctx", None)
    return jax.shard_map(
        local,
        mesh=mesh,
        in_specs=(
            tokens,
            P("fsdp", "ctx"),
            tokens,
            P(),
            rows,
            rows,
            rows,
            P(),
            P(),
            rows,
            P(),
            rows,
            P("ctx", None, "fsdp"),
            P("ctx", None, "fsdp"),
            P("ctx", "fsdp", None),
            tokens,
        ),
        out_specs=(
            tokens,
            tokens,
            vector,
            rows,
            rows,
            rows,
            P(),
            P(),
            rows,
            vector,
            rows,
            P("ctx", None, "fsdp"),
            P("ctx", None, "fsdp"),
            P("ctx", "fsdp", None),
        ),
        check_vma=False,
    )
```

```python
import functools

import jax
import jax.numpy as jnp
import numpy as np
from jax import lax
from jax.experimental import pallas as pl
from jax.experimental.pallas import tpu as pltpu
from jax.sharding import PartitionSpec as P

EPS = 1e-06
LOG2E = 1.4426950408889634
LN2 = 0.6931471805599453
MESH = pl.DeviceIdType.MESH
VMEM_MIB = 62
BF = jnp.bfloat16
F32 = jnp.float32
NN = (((1,), (0,)), ((), ()))
NT = (((1,), (1,)), ((), ()))
TN = (((0,), (0,)), ((), ()))
HBM = pl.BlockSpec(memory_space=pltpu.HBM)
VMEM = pl.BlockSpec(memory_space=pltpu.VMEM)
DMA = pltpu.SemaphoreType.DMA
MEMBERS = ((0, 0), (0, 1), (0, 3), (1, 0), (0, 2), (1, 1), (1, 3), (1, 2))
PLANE = ((0, 0), (2, 2), (1, 1), (3, 3), (1, 3), (3, 1), (0, 1), (2, 3))
PLANE = PLANE + ((0, 3), (2, 1), (1, 0), (3, 2), (3, 0), (1, 2), (0, 2), (2, 0))
CHIPS = tuple((a, b, c) for b, c in PLANE for a in range(2))
ALONG_Z = [m for m in range(1, 16) if PLANE[m][0] == 0]
ALONG_Y = [m for m in range(1, 16) if PLANE[m][1] == 0]
ALONG_BOTH = [m for m in range(1, 16) if PLANE[m][0] and PLANE[m][1]]


def dot(left, right, dims=NN):
    return lax.dot_general(left, right, dims, preferred_element_type=F32)


def dot_exact(left, right, dims=NN):
    return lax.dot_general(
        left, right, dims, precision=lax.Precision.HIGHEST, preferred_element_type=F32
    )


class Place:
    def __init__(self):
        ctx = lax.axis_index("ctx")
        self.f = lax.axis_index("fsdp")
        self.t = lax.rem(ctx, 8)
        self.g = lax.div(ctx, 8)
        self.core = lax.rem(ctx, 2)
        self.z = lax.rem(lax.div(ctx, 2), 4)
        self.y = lax.rem(self.g, 4)
        self.xl = lax.div(self.g, 4)
        self.chip = lax.div(ctx, 2)

    def tp(self, k):
        t = lax.rem(self.t + k, 8)
        return t, (self.g * 8 + t, self.f)

    def cp(self, a, b):
        g = lax.rem(self.xl + a, 2) * 4 + lax.rem(self.y + b + 4, 4)
        return (g * 8 + self.t, self.f)

    def gf(self, k):
        r = lax.rem(self.g * 2 + self.f + k, 16)
        return r, (lax.div(r, 2) * 8 + self.t, lax.rem(r, 2))

    def chips(self, s, sign=1):
        a, b, c = CHIPS[s]
        xl = lax.rem(self.xl + a, 2)
        y = lax.rem(self.y + sign * b + 4, 4)
        z = lax.rem(self.z + sign * c + 4, 4)
        e = (xl * 4 + y) * 4 + z
        return e, (e * 2 + self.core, self.f)

    def plane(self, m, sign=1):
        b, c = PLANE[m]
        i = lax.rem(self.y + sign * b + 4, 4) * 4 + lax.rem(self.z + sign * c + 4, 4)
        e = self.xl * 16 + i
        return i, (e * 2 + self.core, self.f)

    def zpeer(self, c):
        z = lax.rem(self.z + c + 4, 4)
        t = z * 2 + self.core
        return z, t, (self.g * 8 + t, self.f)

    def sibling(self):
        t = self.z * 2 + 1 - self.core
        return t, (self.g * 8 + t, self.f)

    def partner(self):
        return (self.g * 8 + self.t, 1 - self.f)

    def all_tp(self):
        return [self.tp(k)[1] for k in range(1, 8)]

    def all_gf(self):
        return [self.gf(k)[1] for k in range(1, 16)]

    def all_chips(self):
        return [self.chips(s)[1] for s in range(1, 32)]


def greet(devices):
    sem = pltpu.get_barrier_semaphore()
    for d in devices:
        pl.semaphore_signal(sem, inc=1, device_id=d, device_id_type=MESH)
    return sem


class Copies:
    def __init__(self, sems):
        self.sems, self.count, self.begun = sems, 0, []

    def next(self):
        self.count += 1
        return self.sems.at[self.count - 1]

    def to(self, device, src, dst, recv):
        copy = pltpu.make_async_remote_copy(
            src_ref=src,
            dst_ref=dst,
            send_sem=self.next(),
            recv_sem=recv,
            device_id=device,
            device_id_type=MESH,
        )
        copy.start()
        self.begun.append(copy.wait_send)

    def own(self, src, dst):
        copy = pltpu.make_async_copy(src, dst, self.next())
        copy.start()
        self.begun.append(copy.wait)

    def here(self, src, dst):
        copy = pltpu.make_async_copy(src, dst, self.next())
        copy.start()
        return copy

    def done(self):
        for wait in self.begun:
            wait()


def landed(ref, sem):
    pltpu.make_async_copy(ref, ref, sem).wait()


def params(number, mib):
    return pltpu.CompilerParams(
        collective_id=number, has_side_effects=True, vmem_limit_bytes=mib * 2**20
    )


def lanes(rows):
    return lax.broadcasted_iota(jnp.int32, (rows, 128), 1)


def swap(v):
    low = lax.rem(lanes(v.shape[0]), 64) < 32
    return jnp.where(low, pltpu.roll(v, 96, 1), pltpu.roll(v, 32, 1))


def head_mean(v):
    row = lax.broadcasted_iota(jnp.int32, (128, 128), 0)
    same = lax.div(row, 64) == lax.div(lanes(128), 64)
    return dot_exact(v, jnp.where(same, 1.0 / 64, 0.0))


def cos_sin(angle):
    k = jnp.floor(angle * 0.6366197723675814 + 0.5)
    r = angle - k * 1.5703125
    r = r - k * 4.837512969970703125e-4
    r = r - k * 7.54978995489188216e-8
    r2 = r * r
    s = r + r * r2 * (-1.6666654611e-1 + r2 * (8.3321608736e-3 + r2 * -1.9515295891e-4))
    c = 4.166664568298827e-2 + r2 * (-1.388731625493765e-3 + r2 * 2.443315711809948e-5)
    c = 1.0 - 0.5 * r2 + r2 * r2 * c
    q = k - 4.0 * jnp.floor(k * 0.25)
    odd = jnp.logical_or(q == 1.0, q == 3.0)
    cosine, sine = jnp.where(odd, s, c), jnp.where(odd, c, s)
    cosine = jnp.where(jnp.logical_or(q == 1.0, q == 2.0), -cosine, cosine)
    sine = jnp.where(q >= 2.0, -sine, sine)
    return cosine, sine


def column(row):
    at = lax.broadcasted_iota(jnp.int32, (128, 128), 0) == lanes(128)
    return jnp.sum(jnp.where(at, row, 0.0), axis=1, keepdims=True)


QB = 256
UNROLL = 4


def front_kernel(
    x,
    cot,
    routes,
    pos,
    wq,
    wk,
    wv,
    wo_own,
    wr_own,
    gain_a,
    gain_m,
    gain_q,
    gain_k,
    rates,
    eg,
    eu,
    ed,
    outgoing,
    residual,
    wo,
    slots,
    grads,
    ewg,
    ewu,
    ewd,
    o_out,
    att_out,
    lse_out,
    kv_out,
    qp_out,
    raw_out,
    wqkv_out,
    tabc_out,
    tabs_out,
    normed_out,
    normed_t_out,
    near_out,
    xv,
    cotv,
    routev,
    posv,
    wqv,
    wkv,
    wvv,
    wov,
    wrv,
    gav,
    gmv,
    gqv,
    gkv,
    ratev,
    wps,
    wops,
    posf,
    xg,
    wg,
    wog,
    wob,
    posg,
    wst,
    cots,
    normed,
    normed_t,
    slots_t,
    slots_p,
    near,
    place_p,
    routep,
    cotp,
    qp,
    kvall,
    raw,
    wqkv,
    tabc,
    tabs,
    acc,
    lsum,
    o,
    att_t,
    lse,
    attg,
    ss,
    xr,
    fr,
    pr,
    wr,
    gr,
    orr,
    cr,
    kr,
    ar,
    er,
    hr,
    efr,
    wor,
    wofr,
    xpr,
):
    p = Place()
    _, sib = p.sibling()
    me = p.g * 2 + p.f
    c = Copies(ss)
    small = (
        (wq, wqv),
        (wk, wkv),
        (wv, wvv),
        (wo_own, wov),
        (wr_own, wrv),
        (pos, posv),
        (routes, routev),
        (gain_q, gqv),
        (gain_k, gkv),
        (rates, ratev),
        (gain_a, gav),
        (gain_m, gmv),
    )
    loads = [c.here(src, dst) for src, dst in small]
    own_x = c.here(x, xg.at[p.t])
    load_cot = c.here(cot, cotv)
    load_x = c.here(x, xv)
    sem = greet(p.all_chips() + p.all_tp() + p.all_gf())
    for copy in loads:
        copy.wait()

    low8 = lanes(8) < 64
    for t in range(8):
        pair = slice(t // 2 * 128, t // 2 * 128 + 128)
        key, value = wkv[:, pair].astype(F32), wvv[:, pair].astype(F32)
        if t % 2:
            both = jnp.where(low8, pltpu.roll(key, 64, 1), value)
        else:
            both = jnp.where(low8, key, pltpu.roll(value, 64, 1))
        query = wqv[:, t * 128 : (t + 1) * 128].astype(F32)
        wps[t] = jnp.concatenate([query, both], axis=0).astype(BF)
    for i in range(4):
        pair = [wov[:, (2 * i + j) * 128 : (2 * i + j + 1) * 128].astype(F32) for j in range(2)]
        wops[i * 16 : (i + 1) * 16, :] = jnp.concatenate(pair, axis=0).astype(BF)
    router = jnp.concatenate([wrv[...].astype(F32), jnp.zeros((8, 96), F32)], axis=1)
    wops[64:80, :] = jnp.concatenate([router, jnp.zeros((8, 128), F32)], axis=0).astype(BF)
    posf[...] = jnp.broadcast_to(posv[...].astype(F32), (8, 128))
    own = [
        c.here(wps.at[p.t], wst.at[p.t]),
        c.here(posf, posg.at[p.t]),
        c.here(wops, wog.at[me]),
    ]
    pl.semaphore_wait(sem, 31 + 7 + 15)

    for k in range(1, 8):
        t, dev = p.tp(k)
        c.to(dev, wps.at[t], wst.at[p.t], wr)
    for k in (1, 3):
        c.to(p.zpeer(k)[2], x, xg.at[p.t], xr.at[k])
    c.to(sib, x, xg.at[p.t], xr.at[0])
    c.to(p.cp(1, 0), routev, routep, xpr.at[0])
    c.to(p.cp(1, 0), cot, cotp, xpr.at[1])
    for k in range(1, 8):
        c.to(p.tp(k)[1], posf, posg.at[p.t], pr)
    for copy in own:
        copy.wait()

    row = lax.broadcasted_iota(jnp.int32, (128, 128), 0)
    col = lanes(128)

    def places(ref):
        number = lax.broadcasted_iota(jnp.int32, (32, 128), 0)
        hits = jnp.zeros((32, 128), F32)
        for k in range(8):
            hits = hits + jnp.where(ref[k : k + 1, :] == number, 1.0, 0.0)
        before = jnp.where(row < col, 1.0, 0.0).astype(BF)
        return jnp.where(hits > 0, dot(hits.astype(BF), before), -1.0)

    def slot_rows(place):
        within = lax.broadcasted_iota(jnp.int32, (48, 128), 0).astype(F32)
        return jnp.where(place == within, 1.0, 0.0).astype(BF)

    place = places(routev)
    for e in range(32):
        slots_t[e * 48 : (e + 1) * 48, :] = slot_rows(place[e : e + 1, :])
    load_cot.wait()

    def cot_rows(which):
        for m in which:
            i, dev = p.plane(m)
            for a, (ref, values) in enumerate(((slots_t, cotv), (slots_p, cotp))):
                first = i + p.xl * 16 if a == 0 else i
                mine = ref[pl.ds(pl.multiple_of(first * 48, 16), 48), :]
                cots[2 * m + a] = dot(mine, values[...]).astype(BF)
            pair = pl.ds(2 * m, 2)
            if m:
                c.to(dev, cots.at[pair], grads.at[pair], cr)
            else:
                c.own(cots.at[pair], grads.at[pair])

    landed(wst.at[pl.ds(0, 7)], wr)
    own_wg = c.here(wst, wg.at[me])
    for k in range(1, 16):
        c.to(p.gf(k)[1], wst, wg.at[me], gr)
    for k in range(1, 16):
        c.to(p.gf(k)[1], wops, wog.at[me], orr)
    at_own = pl.ds(pl.multiple_of(p.f * 128, 128), 128)
    at_sib = pl.ds(pl.multiple_of(256 + p.f * 128, 128), 128)
    from_partner = pl.ds(pl.multiple_of((1 - p.f) * 128, 128), 128)
    at_sib_partner = pl.ds(pl.multiple_of(256 + (1 - p.f) * 128, 128), 128)

    def part(ref, i, span):
        return ref.at[span, :] if i == 2 else ref.at[:, span]

    weights = ((eg, ewg), (eu, ewu), (ed, ewd))
    for i, (src, dst) in enumerate(weights):
        c.to(sib, src, part(dst, i, at_sib), er.at[i])
        c.own(src, part(dst, i, at_own))
    landed(routep, xpr.at[0])
    place_p[...] = places(routep)
    here = place_p[pl.ds(pl.multiple_of(p.xl * 16, 16), 16), :]
    for e in range(16):
        slots_p[e * 48 : (e + 1) * 48, :] = slot_rows(here[e : e + 1, :])
    for j in range(12):
        cols = slice(j * 128, (j + 1) * 128)
        slots[:, cols] = slots_t[cols, :].astype(F32).T.astype(BF)
    for j in range(6):
        cols = slice(j * 128, (j + 1) * 128)
        near[1, :, cols] = slots_p[cols, :].astype(F32).T.astype(BF)
    near[0] = slots[:, pl.ds(pl.multiple_of(p.xl * 768, 128), 768)]
    c.own(near, near_out)
    landed(cotp, xpr.at[1])

    def pass_on(k, n):
        landed(xg.at[0], xr.at[k])
        t = p.zpeer(-k)[1]
        half = pl.ds(0 if k == 1 else 64, 64)
        c.to(p.zpeer(k)[2], xg.at[t, half], xg.at[t, half], xr.at[n])
        c.to(sib, xg.at[t], xg.at[t], fr.at[k])
        return t

    t1 = pass_on(1, 2)
    t3 = pass_on(3, 4)
    cot_rows(ALONG_Z + ALONG_Y)
    c.to(p.partner(), eg, part(ewg, 0, at_own), hr.at[0])

    landed(posg.at[pl.ds(0, 7)], pr)
    signed = jnp.where(lax.rem(col, 64) < 32, -1.0, 1.0)
    for t in range(8):
        cosine, sine = cos_sin(column(posg[t, 0:1, :]) * ratev[...])
        tabc[t * 128 : (t + 1) * 128, :] = cosine
        tabs[t * 128 : (t + 1) * 128, :] = sine * signed

    own_wg.wait()
    landed(wg.at[pl.ds(0, 15)], gr)

    def columns(g, _):
        for t in range(8):
            one, two = wg[2 * g, t].astype(F32), wg[2 * g + 1, t].astype(F32)
            both = [jnp.concatenate([one[i : i + 8], two[i : i + 8]], axis=0) for i in (0, 8)]
            at = pl.ds(pl.multiple_of((g * 8 + t) * 16, 16), 16)
            wqkv[at, :] = jnp.concatenate(both, axis=1).astype(BF)
        return 0

    lax.fori_loop(0, 8, columns, 0)

    landed(wog.at[pl.ds(0, 15)], orr)

    def output_rows(g, _):
        one, two = wog[2 * g].astype(F32), wog[2 * g + 1].astype(F32)
        for i in range(9):
            both = [one[i * 8 : i * 8 + 8], two[i * 8 : i * 8 + 8]]
            wob[g, :, i * 128 : (i + 1) * 128] = jnp.concatenate(both, axis=0).astype(BF)
        return 0

    lax.fori_loop(0, 8, output_rows, 0)
    for k in (1, 3, 2):
        c.to(p.zpeer(k)[2], wob, wo.at[:, p.t], wor.at[k])
    c.to(sib, wob, wo.at[:, p.t], wor.at[0])
    own_wo = c.here(wob, wo.at[:, p.t])

    lane = lanes(128)
    head_q = jnp.concatenate([gqv[...], gqv[...]], axis=1)
    head_k = jnp.concatenate([gkv[...], jnp.ones((1, 64), F32)], axis=1)

    def project(t):
        rows = pl.ds(pl.multiple_of(t * 128, 128), 128)
        value = xg[t].astype(F32)
        factor = lax.rsqrt(jnp.mean(value * value, axis=1, keepdims=True) + EPS)
        value = (value * factor * gav[...]).astype(BF)
        normed[rows, :] = value
        normed_t[:, rows] = value.astype(F32).T.astype(BF)
        out = dot(value, wqkv[...])
        raw[rows, :] = out
        cosine, sine = tabc[rows, :], tabs[rows, :]
        q, k = out[:, :128], out[:, 128:]
        q = q * lax.rsqrt(head_mean(q * q) + EPS) * head_q
        q = ((q * cosine + swap(q) * sine) * (0.125 * LOG2E)).astype(BF).astype(F32)
        qp[rows, :] = jnp.where(lane < 64, q, 0.0).astype(BF)
        second = pl.ds(pl.multiple_of(1024 + t * 128, 128), 128)
        qp[second, :] = jnp.where(lane < 64, pltpu.roll(q, 64, 1), 0.0).astype(BF)
        n = k * lax.rsqrt(head_mean(k * k) + EPS) * head_k
        n = n * cosine + swap(n) * sine
        kvall[0, rows, :] = jnp.where(lane < 64, n, k).astype(BF)

    own_x.wait()
    project(p.t)
    t2 = p.zpeer(2)[1]
    landed(xg.at[0, pl.ds(0, 64)], xr.at[2])
    landed(xg.at[0, pl.ds(0, 64)], xr.at[4])
    c.to(sib, xg.at[t2], xg.at[t2], fr.at[2])
    project(t1)
    project(t3)
    landed(xg.at[0], xr.at[0])
    project(p.sibling()[0])
    project(t2)
    for k in (1, 3, 2):
        landed(xg.at[0], fr.at[k])
        project(lax.rem(p.z + 4 - k, 4) * 2 + 1 - p.core)

    def kv_to(a, b, src, n, span=None, recv=None):
        src, dst = kvall.at[src], kvall.at[n]
        if span is not None:
            src, dst = src.at[span], dst.at[span]
        c.to(p.cp(a, b), src, dst, kr.at[n if recv is None else recv])

    kv_to(0, 1, 0, 1)
    kv_to(0, 3, 0, 2)
    kv_to(1, 0, 0, 3)
    kept = (
        (qp, qp_out),
        (raw, raw_out),
        (wqkv, wqkv_out),
        (tabc, tabc_out),
        (tabs, tabs_out),
        (normed, normed_out),
        (normed_t, normed_t_out),
    )
    for src, dst in kept:
        c.own(src, dst)

    acc[...] = jnp.zeros_like(acc)
    lsum[...] = jnp.zeros_like(lsum)

    def work(n, _):
        kvb = kvall[n]

        def block(i, _):
            for u in range(UNROLL):
                rows = pl.ds(pl.multiple_of((i * UNROLL + u) * QB, QB), QB)
                e = jnp.exp2(dot(qp[rows, :], kvb, NT))
                total = e[:, 0:128]
                for j in range(1, 8):
                    total = total + e[:, j * 128 : (j + 1) * 128]
                lsum[rows, :] += total
                acc[rows, :] += dot(e.astype(BF), kvb)
            return 0

        lax.fori_loop(0, 2048 // QB // UNROLL, block, 0)
        return 0

    first, second = pl.ds(0, 512), pl.ds(512, 512)
    half = kvall.at[0, first]
    work(0, 0)
    landed(kvall.at[0], kr.at[1])
    kv_to(0, 1, 1, 4, first)
    kv_to(1, 0, 1, 5)
    landed(kvall.at[0], kr.at[2])
    kv_to(0, 3, 2, 4, second, 8)
    kv_to(1, 0, 2, 6)
    cot_rows([0] + ALONG_BOTH[0:7])
    lax.fori_loop(1, 3, work, 0)
    landed(half, kr.at[4])
    landed(half, kr.at[8])
    kv_to(1, 0, 4, 7)
    for i, (src, dst) in enumerate(weights):
        if i:
            c.to(p.partner(), src, part(dst, i, at_own), hr.at[i])
    landed(kvall.at[0], kr.at[3])
    lax.fori_loop(3, 5, work, 0)
    for k in (1, 3, 2):
        landed(wob, wor.at[k])
        block = wo.at[:, p.zpeer(-k)[1]]
        c.to(sib, block, block, wofr.at[k])

    def arrived(n, _):
        landed(kvall.at[0], kr.at[n])
        return work(n, 0)

    lax.fori_loop(5, 8, arrived, 0)

    for t in range(8):
        parts = []
        for h in range(2):
            rows = pl.ds(h * 1024 + t * 128, 128)
            total = jnp.sum(lsum[rows, :], axis=1, keepdims=True)
            parts.append(acc[rows, :] / total)
        whole = jnp.where(lane < 64, pltpu.roll(parts[0], 64, 1), parts[1])
        o[pl.ds(t * 128, 128), :] = whole
        att_t[pl.ds(t * 128, 128), :] = whole.astype(BF)
    for k in range(1, 8):
        t, dev = p.tp(k)
        block = att_t.at[pl.ds(pl.multiple_of(t * 128, 128), 128)]
        c.to(dev, block, attg.at[p.t], ar)
    own_att = c.here(att_t.at[pl.ds(pl.multiple_of(p.t * 128, 128), 128)], attg.at[p.t])
    cot_rows(ALONG_BOTH[7:9])
    ones = jnp.ones((8, 128), F32)
    for h in range(2):
        lse[h] = jnp.log2(dot_exact(ones, lsum[pl.ds(h * 1024, 1024), :], NT))
    for src, dst in ((o, o_out), (att_t, att_out), (lse, lse_out), (kvall, kv_out)):
        c.own(src, dst)
    for i, (_, dst) in enumerate(weights):
        piece = part(dst, i, from_partner)
        landed(piece, hr.at[i])
        c.to(sib, piece, part(dst, i, at_sib_partner), efr.at[i])
    own_wo.wait()
    landed(wob, wor.at[0])
    for k in (1, 3, 2):
        landed(wob, wofr.at[k])
    load_x.wait()
    own_att.wait()
    landed(attg.at[pl.ds(0, 7)], ar)

    att = jnp.concatenate([attg[t] for t in range(8)], axis=1)
    square = jnp.zeros((128, 1), F32)
    for j in range(4):
        cols = slice(j * 256, (j + 1) * 256)
        value = xv[:, cols].astype(F32) + dot(att, wo[:, :, :, cols].reshape(1024, 256))
        residual[:, cols] = value
        square = square + jnp.sum(value * value, axis=1, keepdims=True)
    factor = lax.rsqrt(square * (1.0 / 1024) + EPS)
    value = (residual[...] * factor * gmv[...]).astype(BF)
    for j in range(4):
        rows = dot(slots_t[j * 384 : (j + 1) * 384, :], value).astype(BF)
        outgoing[j * 8 : (j + 1) * 8] = rows.reshape(8, 48, 1024)

    for i, (_, dst) in enumerate(weights):
        landed(part(dst, i, at_sib), er.at[i])
        landed(part(dst, i, at_sib), efr.at[i])
    landed(grads.at[pl.ds(0, 30)], cr)
    c.done()


def front(*operands):
    shape = jax.ShapeDtypeStruct
    v = pltpu.VMEM
    return pl.pallas_call(
        front_kernel,
        out_shape=(
            shape((32, 48, 1024), BF),
            shape((128, 1024), F32),
            shape((8, 8, 16, 1152), BF),
            shape((128, 1536), BF),
            shape((32, 48, 1024), BF),
            shape((1024, 512), BF),
            shape((1024, 512), BF),
            shape((512, 1024), BF),
            shape((1024, 128), F32),
            shape((1024, 128), BF),
            shape((2, 8, 1024), F32),
            shape((8, 1024, 128), BF),
            shape((2048, 128), BF),
            shape((1024, 256), F32),
            shape((1024, 256), BF),
            shape((1024, 128), F32),
            shape((1024, 128), F32),
            shape((1024, 1024), BF),
            shape((1024, 1024), BF),
            shape((2, 128, 768), BF),
        ),
        in_specs=[HBM] * 17,
        out_specs=(VMEM,) * 4 + (HBM,) * 16,
        scratch_shapes=[
            v((128, 1024), BF),
            v((128, 1024), BF),
            v((8, 128), jnp.int32),
            v((1, 128), jnp.int32),
            v((8, 1024), F32),
            v((8, 512), F32),
            v((8, 512), F32),
            v((8, 1024), F32),
            v((8, 32), F32),
            v((1, 1024), F32),
            v((1, 1024), F32),
            v((1, 64), F32),
            v((1, 64), F32),
            v((1, 128), F32),
            v((8, 16, 128), BF),
            v((80, 128), BF),
            v((8, 128), F32),
            v((8, 128, 1024), BF),
            v((16, 8, 16, 128), BF),
            v((16, 80, 128), BF),
            v((8, 16, 1152), BF),
            v((8, 8, 128), F32),
            v((8, 16, 128), BF),
            v((32, 48, 1024), BF),
            v((1024, 1024), BF),
            v((1024, 1024), BF),
            v((1536, 128), BF),
            v((768, 128), BF),
            v((2, 128, 768), BF),
            v((32, 128), F32),
            v((8, 128), jnp.int32),
            v((128, 1024), BF),
            v((2048, 128), BF),
            v((8, 1024, 128), BF),
            v((1024, 256), F32),
            v((1024, 256), BF),
            v((1024, 128), F32),
            v((1024, 128), F32),
            v((2048, 128), F32),
            v((2048, 128), F32),
            v((1024, 128), F32),
            v((1024, 128), BF),
            v((2, 8, 1024), F32),
            v((8, 128, 128), BF),
            DMA((176,)),
            DMA((5,)),
            DMA((4,)),
            DMA,
            DMA,
            DMA,
            DMA,
            DMA,
            DMA((10,)),
            DMA,
            DMA((3,)),
            DMA((3,)),
            DMA((3,)),
            DMA((4,)),
            DMA((4,)),
            DMA((2,)),
        ],
        compiler_params=params(0, VMEM_MIB),
        name="front",
    )(*operands)


KB = 256
GB = 1024
EARLY = 4


def expert_kernel(
    outgoing,
    residual,
    wo,
    slots,
    grads_in,
    ewg,
    ewu,
    ewd,
    cot_in,
    gain_in,
    qp_in,
    kv_in,
    lse_in,
    branch,
    gat,
    grad_residual_out,
    grad_ffn_out,
    mixed_out,
    dwg_out,
    dwu_out,
    dwd_out,
    dwr_out,
    residual_out,
    weights_out,
    cot,
    gain,
    mixed,
    dwg,
    dwu,
    dwd,
    dwr,
    grad_residual,
    grad_ffn,
    rows,
    grads,
    wg,
    wu,
    wd,
    gh,
    gp,
    up,
    hid,
    gl,
    gin,
    back,
    sg,
    su,
    sd,
    rg,
    ru,
    rd,
    qp,
    kvall,
    lse,
    tiles,
    ss,
    rr,
    br,
    wr,
    ts,
):
    p = Place()
    _, sib = p.sibling()
    sem = greet(p.all_chips() + [sib])
    c = Copies(ss)
    own_rows = c.here(outgoing.at[p.chip], rows.at[0])
    local = [c.here(grads_in, grads), c.here(ewd, wd), c.here(ewg, wg), c.here(ewu, wu)]
    load_cot, load_gain = c.here(cot_in, cot), c.here(gain_in, gain)
    attention = [c.here(qp_in, qp), c.here(kv_in, kvall), c.here(lse_in, lse)]
    c.own(residual, residual_out)
    pl.semaphore_wait(sem, 31 + 1)
    for s in range(1, 32):
        e, dev = p.chips(s)
        c.to(dev, outgoing.at[e], rows.at[s], rr.at[s // 4])
    own_rows.wait()
    for copy in local:
        copy.wait()

    def hidden_grads(j, _):
        block = grads[pl.ds(j * 4, 4)].reshape(192, 1024)
        gh[pl.ds(pl.multiple_of(j * 192, 64), 192), :] = dot(block, wd[...], NT)
        return 0

    lax.fori_loop(0, 8, hidden_grads, 0)

    def weights_of(n, _):
        for j in range(1024 // KB):

            @pl.when(n > 0)
            def _(j=j):
                pltpu.make_async_copy(tiles.at[j], weights_out.at[0], ts.at[j]).wait()

            for i in range(2048 // GB):
                h, cols = i * GB // 1024, pl.ds(i * GB % 1024, GB)
                scores = dot(kvall[n, j * KB : (j + 1) * KB, :], qp[pl.ds(i * GB, GB), :], NT)
                value = jnp.exp2(scores - lse[h, 0:1, cols])
                tiles[j, :, i * GB : (i + 1) * GB] = value.astype(BF)
            tile = weights_out.at[n * (1024 // KB) + j]
            pltpu.make_async_copy(tiles.at[j], tile, ts.at[j]).start()
        return 0

    for copy in attention:
        copy.wait()
    lax.fori_loop(0, EARLY, weights_of, 0)

    lane = lax.broadcasted_iota(jnp.int32, (192, 128), 1)
    here = jnp.where(lane == p.chip, 1.0, 0.0)
    router = wo[:, :, :, 1024:].reshape(1024, 128)

    for j in range(8):
        landed(rows.at[pl.ds(0, 4 if j else 3)], rr.at[j])
        block = rows[4 * j : 4 * j + 4].reshape(192, 1024)
        span = pl.ds(j * 192, 192)
        gate_pre = dot(block, wg[...])
        up_pre = dot(block, wu[...])
        logits = jnp.where(lane < 32, dot(block, router), -1e30)
        expo = jnp.exp(logits - jnp.max(logits, axis=1, keepdims=True))
        probs = expo / jnp.sum(expo, axis=1, keepdims=True)
        gate = jnp.sum(probs * here, axis=1, keepdims=True)
        sig = jax.nn.sigmoid(gate_pre)
        act = gate_pre * sig
        hidden = act * up_pre
        grad_hidden = gh[span, :]
        weight = jnp.sum(hidden * grad_hidden, axis=1, keepdims=True) * gate
        grad_hidden = grad_hidden * gate
        grad_gate = (grad_hidden * up_pre * sig * (1.0 + gate_pre * (1.0 - sig))).astype(BF)
        grad_up = (grad_hidden * act).astype(BF)
        grad_logits = (weight * (here - probs)).astype(BF)
        hid[span, :] = (hidden * gate).astype(BF)
        gp[span, :] = grad_gate
        up[span, :] = grad_up
        gl[span, :] = grad_logits
        total = dot(grad_gate, wg[...], NT) + dot(grad_up, wu[...], NT)
        total = total + dot(grad_logits, router, NT)
        gin[4 * j : 4 * j + 4] = total.astype(BF).reshape(4, 48, 1024)
        for s in range(4 * j, 4 * j + 4):
            if s:
                c.to(p.chips(s, -1)[1], gin.at[s], back.at[p.chip], br)
            else:
                own_back = c.here(gin.at[0], back.at[p.chip])

    for m in range(4):
        cols = slice(m * 256, (m + 1) * 256)
        left = rows[:, :, cols].reshape(1536, 256)
        for src, own, sends in ((gp, dwg, sg), (up, dwu, su)):
            value = dot(left, src[...], TN).astype(BF)
            for q in range(2):
                own[q, cols, :] = value[:, q * 128 : (q + 1) * 128]
                sends[q, cols, :] = value[:, (2 + q) * 128 : (3 + q) * 128]
        dwr[cols, :] = dot(left, gl[...], TN)
    for m in range(4):
        cols = slice(m * 256, (m + 1) * 256)
        right = grads[:, :, cols].reshape(1536, 256)
        value = dot(hid[...], right, TN).astype(BF)
        dwd[:, :, cols] = value[:256].reshape(2, 128, 256)
        sd[:, :, cols] = value[256:].reshape(2, 128, 256)
    for i, (src, dst) in enumerate(((sg, rg), (su, ru), (sd, rd))):
        c.to(sib, src, dst, wr.at[i])

    def outputs(j, _):
        block = hid[pl.ds(pl.multiple_of(j * 192, 64), 192), :]
        mixed[pl.ds(j * 4, 4)] = dot(block, wd[...]).astype(BF).reshape(4, 48, 1024)
        return 0

    lax.fori_loop(0, 8, outputs, 0)
    c.own(mixed, mixed_out)
    c.own(dwr, dwr_out)
    lax.fori_loop(EARLY, 8, weights_of, 0)
    for i, (got, own) in enumerate(((rg, dwg), (ru, dwu), (rd, dwd))):
        landed(got, wr.at[i])
        own[...] = (own[...].astype(F32) + got[...].astype(F32)).astype(BF)
    for src, dst in ((dwg, dwg_out), (dwu, dwu_out), (dwd, dwd_out)):
        c.own(src, dst)
    load_cot.wait()
    load_gain.wait()

    for j in range(1024 // KB):
        pltpu.make_async_copy(tiles.at[j], weights_out.at[0], ts.at[j]).wait()

    landed(back.at[pl.ds(0, 31)], br)
    own_back.wait()
    res = residual[...]
    factor = lax.rsqrt(jnp.mean(res * res, axis=1, keepdims=True) + EPS)
    normed = res * factor
    for j in range(4):
        cols = slice(j * 256, (j + 1) * 256)
        grad_residual[:, cols] = dot(slots[...], back[:, :, cols].reshape(1536, 256))
    grad_mid = grad_residual[...]
    part = jnp.sum(grad_mid * normed, axis=0, keepdims=True)
    grad_ffn[...] = jnp.broadcast_to(part, (8, 1024))
    g = grad_mid * gain[...]
    g = factor * (g - normed * jnp.mean(g * normed, axis=1, keepdims=True))
    g = cot[...].astype(F32) + g
    grad_residual[...] = g
    low = g.astype(BF)
    branch[...] = low
    for t in range(8):
        weights = wo[t][:, :, :1024].reshape(128, 1024)
        gat[t] = dot(low, weights, NT).astype(BF)
    c.own(grad_residual, grad_residual_out)
    c.own(grad_ffn, grad_ffn_out)
    c.done()


def expert_rows(*operands):
    shape = jax.ShapeDtypeStruct
    v = pltpu.VMEM
    return pl.pallas_call(
        expert_kernel,
        out_shape=(
            shape((128, 1024), BF),
            shape((8, 128, 128), BF),
            shape((128, 1024), F32),
            shape((8, 1024), F32),
            shape((32, 48, 1024), BF),
            shape((2, 1024, 128), BF),
            shape((2, 1024, 128), BF),
            shape((2, 128, 1024), BF),
            shape((1024, 128), F32),
            shape((128, 1024), F32),
            shape((8 * 1024 // KB, KB, 2048), BF),
        ),
        in_specs=[VMEM] * 4 + [HBM] * 9,
        out_specs=(VMEM,) * 2 + (HBM,) * 9,
        scratch_shapes=[
            v((128, 1024), BF),
            v((1, 1024), F32),
            v((32, 48, 1024), BF),
            v((2, 1024, 128), BF),
            v((2, 1024, 128), BF),
            v((2, 128, 1024), BF),
            v((1024, 128), F32),
            v((128, 1024), F32),
            v((8, 1024), F32),
            v((32, 48, 1024), BF),
            v((32, 48, 1024), BF),
            v((1024, 512), BF),
            v((1024, 512), BF),
            v((512, 1024), BF),
            v((1536, 512), F32),
            v((1536, 512), BF),
            v((1536, 512), BF),
            v((1536, 512), BF),
            v((1536, 128), BF),
            v((32, 48, 1024), BF),
            v((32, 48, 1024), BF),
            v((2, 1024, 128), BF),
            v((2, 1024, 128), BF),
            v((2, 128, 1024), BF),
            v((2, 1024, 128), BF),
            v((2, 1024, 128), BF),
            v((2, 128, 1024), BF),
            v((2048, 128), BF),
            v((8, 1024, 128), BF),
            v((2, 8, 1024), F32),
            v((1024 // KB, KB, 2048), BF),
            DMA((96,)),
            DMA((8,)),
            DMA,
            DMA((3,)),
            DMA((1024 // KB,)),
        ],
        compiler_params=params(1, VMEM_MIB),
        name="experts",
    )(*operands)


ORDER = (5, 6, 7, 3, 4, 1, 2, 0)
AHEAD = 2


def back_kernel(
    branch,
    gat,
    grad_residual_in,
    grad_ffn_in,
    mixed,
    dwg,
    dwu,
    dwd,
    dwr_in,
    residual_in,
    probs,
    o_in,
    att_in,
    kv_in,
    qp_in,
    raw_in,
    wqkv_in,
    tabc_in,
    tabs_in,
    normed_in,
    normed_t_in,
    near_in,
    x_in,
    gain_a,
    gain_q,
    gain_k,
    wq_in,
    wk_in,
    wv_in,
    layer_out,
    input_out,
    query_out,
    key_out,
    value_out,
    output_out,
    rows_out,
    misc_out,
    gate_out,
    up_out,
    down_out,
    layer_output,
    grad_input,
    grad_query,
    grad_key,
    grad_value,
    vectors,
    misc,
    out_g,
    out_u,
    out_d,
    grad_residual,
    grad_ffn,
    dwr,
    residual,
    near,
    ypart,
    ypeer,
    o,
    att_t,
    tiles,
    kvall,
    qp,
    raw,
    wqkv,
    tabc,
    tabs,
    normed,
    normed_t,
    xv,
    gav,
    gqv,
    gkv,
    wqv,
    wkv,
    wvv,
    own_g,
    own_u,
    own_d,
    rwg,
    rwu,
    rwd,
    yret,
    dqt,
    earlyr,
    gatr,
    dop,
    delta,
    acc,
    bg,
    early,
    dwos,
    dwol,
    dks,
    dkr,
    draw,
    dx,
    dwm,
    sibr,
    zsend,
    zr,
    dwin,
    d2s,
    d2l,
    ss,
    ar,
    bs,
    fs,
    yr,
    er,
    sr,
    os_,
    ors,
    dsr,
    zrs,
    wrs,
    trs,
    ypr,
    ts,
):
    p = Place()
    _, sib = p.sibling()
    c = Copies(ss)
    first = [
        c.here(src, dst)
        for src, dst in ((o_in, o), (qp_in, qp), (kv_in, kvall), (att_in, att_t))
    ]
    for k in range(AHEAD):
        pltpu.make_async_copy(probs.at[ORDER[0] * 1024 // KB + k], tiles.at[k], ts.at[k]).start()
    own_gat = c.here(gat.at[p.t], gatr.at[p.t])
    own_bg = c.here(branch, bg.at[p.t])
    sem = greet(p.all_chips() + p.all_tp() + p.all_gf())
    mirror = p.t * 8 + p.g
    at_home = p.g == p.t

    @pl.when(jnp.logical_not(at_home))
    def _():
        pl.semaphore_signal(sem, inc=1, device_id=(mirror, p.f), device_id_type=MESH)

    pl.semaphore_wait(sem, 31 + 7 + 15 + jnp.where(at_home, 0, 1))
    for k in range(1, 8):
        t, dev = p.tp(k)
        c.to(dev, gat.at[t], gatr.at[p.t], ar)
    here = p.y * 4 + p.z
    own_mixed = c.here(mixed.at[pl.ds(0, 2)], yret.at[here])

    def outputs(which):
        for m in which:
            c.to(p.plane(m, -1)[1], mixed.at[pl.ds(2 * m, 2)], yret.at[here], yr)

    outputs(ALONG_Y)
    own_gat.wait()
    for copy in first:
        copy.wait()
    landed(gatr.at[pl.ds(0, 7)], ar)
    owned = ((dwg, own_g, rwg, out_g), (dwu, own_u, rwu, out_u), (dwd, own_d, rwd, out_d))
    owned_copies = []
    for i, (src, mine, got, _) in enumerate(owned):
        owned_copies.append(c.here(src.at[p.f], mine))

    outputs(ALONG_BOTH + ALONG_Z)
    for k in (1, 3, 2):
        c.to(p.zpeer(k)[2], branch, bg.at[p.t], bs.at[k])
    c.to(sib, branch, bg.at[p.t], bs.at[0])
    later = (
        (raw_in, raw),
        (wqkv_in, wqkv),
        (tabc_in, tabc),
        (tabs_in, tabs),
        (normed_in, normed),
        (normed_t_in, normed_t),
        (grad_residual_in, grad_residual),
        (residual_in, residual),
        (near_in, near),
        (x_in, xv),
        (gain_a, gav),
        (gain_q, gqv),
        (gain_k, gkv),
        (wq_in, wqv),
        (wk_in, wkv),
        (wv_in, wvv),
    )
    soon = ((grad_ffn_in, grad_ffn), (dwr_in, dwr))
    soon = [c.here(src, dst) for src, dst in soon]
    later = [c.here(src, dst) for src, dst in later]

    lane = lanes(128)
    ones = jnp.ones((8, 128), F32)
    for t in range(8):
        both = gatr[t].astype(F32)
        rows = pl.ds(t * 128, 128)
        dop[rows, :] = jnp.where(lane < 64, 0.0, pltpu.roll(both, 64, 1)).astype(BF)
        dop[pl.ds(1024 + t * 128, 128), :] = jnp.where(lane < 64, 0.0, both).astype(BF)
        prod = both * o[rows, :]
        for h in range(2):
            value = jnp.where((lane < 64) == (h == 0), prod, 0.0)
            delta[h, :, rows] = dot_exact(ones, value, NT)
    dqt[...] = jnp.zeros_like(dqt)

    per = 1024 // KB

    def fetch(tile, k):
        slot = lax.rem(k, AHEAD + 1)
        return pltpu.make_async_copy(probs.at[tile], tiles.at[slot], ts.at[slot])

    def work(n):
        at = ORDER.index(n)

        def keys(j, _):
            k = at * per + j
            later = j + AHEAD

            @pl.when(k + AHEAD < 8 * per)
            def _():
                after = ORDER[min(at + 1, 7)]
                tile = jnp.where(later < per, n * per + later, after * per + later - per)
                fetch(tile, k + AHEAD).start()

            fetch(0, k).wait()
            slot = lax.rem(k, AHEAD + 1)
            krows = pl.ds(pl.multiple_of(j * KB, KB), KB)
            kvb = kvall[n, krows, :]
            kt = kvb.T[:64, :]
            total = jnp.zeros((KB, 128), F32)
            for i in range(2048 // GB):
                rows = pl.ds(i * GB, GB)
                h, cols = i * GB // 1024, pl.ds(i * GB % 1024, GB)
                q = qp[rows, :]
                d = dop[rows, :]
                w = tiles[slot, :, i * GB : (i + 1) * GB]
                ds = (w.astype(F32) * (dot(kvb, d, NT) - delta[h, 0:1, cols])).astype(BF)
                total = total + dot(w, d) + dot(ds, q)
                dqt[h * 64 : (h + 1) * 64, cols] += dot(kt, ds)
            acc[krows, :] = total
            return 0

        lax.fori_loop(0, per, keys, 0)

    def chunk_x(n):
        work(n)
        dks[n] = acc[...].astype(BF)
        m = MEMBERS.index((0, MEMBERS[n][1]))
        c.to(p.cp(1, 0), dks.at[n], dkr.at[m], sr.at[m])

    def chunk_y(n):
        work(n)
        landed(dkr.at[0], sr.at[n])
        dks[n] = (acc[...] + dkr[n].astype(F32)).astype(BF)
        m = MEMBERS.index((1, MEMBERS[n][1]))
        c.to(p.cp(0, -MEMBERS[n][1]), dks.at[n], dkr.at[m], sr.at[m])

    chunk_x(5)
    chunk_x(6)
    chunk_x(7)
    chunk_x(3)
    for i, (src, _, got, _) in enumerate(owned):
        c.to(p.partner(), src.at[1 - p.f], got, er.at[i])
    chunk_y(4)
    chunk_y(1)
    chunk_y(2)
    spot = lax.broadcasted_iota(jnp.int32, (128, 128), 0)
    same = jnp.logical_and(lax.div(spot, 16) == lax.div(lane, 8), lax.rem(spot, 8) == lax.rem(lane, 8))
    picks = [
        jnp.where(jnp.logical_and(same, lax.rem(lax.div(spot, 8), 2) == f), 1.0, 0.0)
        for f in range(2)
    ]
    sub16 = lax.broadcasted_iota(jnp.int32, (16, 128), 0)

    def rows_of(value, f):
        return jnp.concatenate(
            [value[(2 * t + f) * 8 : (2 * t + f) * 8 + 8, :] for t in range(8)], axis=0
        )
    me = p.g * 2 + p.f
    work(0)

    for copy in later:
        copy.wait()
    head_gains = (
        jnp.concatenate([gqv[...], gqv[...]], axis=1),
        jnp.concatenate([gkv[...], jnp.ones((1, 64), F32)], axis=1),
    )

    def through(i, rows, grad):
        cosine, sine = tabc[rows, :], tabs[rows, :]
        value = raw[rows, i * 128 : (i + 1) * 128]
        grad = grad * cosine - swap(grad) * sine
        factor = lax.rsqrt(head_mean(value * value) + EPS)
        value = value * factor
        total = jnp.sum(grad * value, axis=0, keepdims=True)
        grad = grad * head_gains[i]
        return total, factor * (grad - value * head_mean(grad * value))

    gains_q = jnp.zeros((1, 128), F32)
    for t in range(8):
        rows = slice(t * 128, (t + 1) * 128)
        total, value = through(0, rows, dqt[:, rows].T * 0.125)
        gains_q = gains_q + total
        draw[rows, 0:128] = value.astype(BF)
    def head_columns(g, cols):
        rows = pl.ds(pl.multiple_of(g * 128, 128), 128)
        value = dot(normed_t[rows, :], draw[:, cols])
        for f in range(2):
            dwm[g * 2 + f, 0:64, cols] = rows_of(value, f).astype(BF)

    for g in range(8):
        head_columns(g, slice(0, 128))
    for k in (1, 3, 2):
        landed(branch, bs.at[k])
        block = bg.at[p.zpeer(-k)[1]]
        c.to(sib, block, block, fs.at[k])
    for n in (0, 5, 7, 6):
        landed(dkr.at[0], sr.at[n])
    gains_k = jnp.zeros((1, 128), F32)
    for t in range(8):
        rows = slice(t * 128, (t + 1) * 128)
        whole = acc[rows, :]
        for n in (0, 5, 7, 6):
            whole = whole + dkr[n, rows, :].astype(F32)
        total, value = through(1, rows, whole * LN2)
        gains_k = gains_k + total
        draw[rows, 128:256] = jnp.where(lane < 64, value, whole).astype(BF)
    gains = jnp.concatenate([gains_q, jnp.where(lanes(1) < 64, gains_k, 0.0)], axis=1)
    wide16 = lax.broadcasted_iota(jnp.int32, (16, 256), 0)
    gains = jnp.where(wide16 == 0, gains, 0.0).astype(BF)
    for r in range(16):
        dwm[r, 64:80, :] = gains
    for j in range(8):
        g = lax.rem(p.g + j, 8)
        head_columns(g, slice(128, 256))
        if j:
            for f in range(2):
                c.to((g * 8 + p.t, f), dwm.at[g * 2 + f], dwin.at[me], wrs)
        else:
            c.to(p.partner(), dwm.at[g * 2 + 1 - p.f], dwin.at[me], wrs)
            own_dw = c.here(dwm.at[me], dwin.at[me])

    def input_grad(core, z):
        rows = pl.ds(pl.multiple_of((z * 2 + core) * 128, 128), 128)
        left = draw[rows, :]
        for j in range(4):
            cols = slice(j * 256, (j + 1) * 256)
            dx[core, z, :, cols] = dot(left, wqkv[cols, :], NT).astype(BF)

    for k in (1, 3, 2, 0):
        z = lax.rem(p.z + k, 4)
        input_grad(1 - p.core, z)
        c.to(sib, dx.at[1 - p.core, z], sibr.at[z], dsr.at[k])
    for k in (1, 3, 2):
        z, _, dev = p.zpeer(k)
        input_grad(p.core, z)
        landed(sibr.at[0], dsr.at[k])
        zsend[k] = (dx[p.core, z].astype(F32) + sibr[z].astype(F32)).astype(BF)
        c.to(dev, zsend.at[k], zr.at[k], zrs.at[k])
    input_grad(p.core, p.z)

    own_bg.wait()
    landed(branch, bs.at[0])
    for k in (1, 3, 2):
        landed(branch, fs.at[k])
    for j in range(4):
        cols = slice(j * 256, (j + 1) * 256)
        total = jnp.zeros((128, 256), F32)
        for t in range(8):
            total = total + dot(att_t[t * 128 : (t + 1) * 128, :], bg[t, :, cols], TN)
        for r in range(16):
            block = total[r * 8 : (r + 1) * 8, :]
            both = [block[:, :128], block[:, 128:]]
            early[r, j * 16 : (j + 1) * 16, :] = jnp.concatenate(both, axis=0).astype(BF)
    for copy in soon:
        copy.wait()
    for g in range(8):
        span = slice(g * 128, (g + 1) * 128)
        value = dwr[span, :]
        for f in range(2):
            early[g * 2 + f, 64:128, :] = rows_of(value, f).astype(BF)
            line = dot_exact(grad_ffn[0:1, span], picks[f])
            early[g * 2 + f, 128:144, :] = jnp.where(sub16 == 0, line, 0.0).astype(BF)
    for k in range(1, 16):
        r, dev = p.gf(k)
        c.to(dev, early.at[r], earlyr.at[me], ors)
    own_early = c.here(early.at[me], earlyr.at[me])

    own_mixed.wait()
    landed(yret.at[pl.ds(0, 15)], yr)
    for j in range(4):
        cols = slice(j * 256, (j + 1) * 256)
        ypart[:, cols] = dot(near[1], yret[:, 1, :, cols].reshape(768, 256)).astype(BF)
    c.to(p.cp(1, 0), ypart, ypeer, ypr)
    for j in range(4):
        cols = slice(j * 256, (j + 1) * 256)
        residual[:, cols] += dot(near[0], yret[:, 0, :, cols].reshape(768, 256))

    landed(sibr.at[0], dsr.at[0])
    whole = dx[p.core, p.z].astype(F32) + sibr[p.z].astype(F32)
    for i, (_, mine, got, out) in enumerate(owned):
        owned_copies[i].wait()
        landed(got, er.at[i])
        out[...] = mine[...].astype(F32) + got[...].astype(F32)
    for src, dst in ((out_g, gate_out), (out_u, up_out), (out_d, down_out)):
        c.own(src, dst)
    own_early.wait()
    landed(earlyr.at[pl.ds(0, 15)], ors)
    before = earlyr[0].astype(F32)
    for r in range(1, 16):
        before = before + earlyr[r].astype(F32)
    for i in range(8):
        dwos[:, i * 128 : (i + 1) * 128] = before[i * 8 : (i + 1) * 8, :]

    @pl.when(jnp.logical_not(at_home))
    def _():
        pltpu.make_async_remote_copy(
            src_ref=dwos,
            dst_ref=dwol,
            send_sem=os_.at[0],
            recv_sem=os_.at[1],
            device_id=(mirror, p.f),
            device_id_type=MESH,
        ).start()

    @pl.when(at_home)
    def _():
        pltpu.make_async_copy(dwos, dwol, os_.at[2]).start()

    own_dw.wait()
    landed(dwin.at[pl.ds(0, 15)], wrs)
    total = dwin[0].astype(F32)
    for r in range(1, 16):
        total = total + dwin[r].astype(F32)
    eight = lax.broadcasted_iota(jnp.int32, (8, 128), 0)
    for t in range(8):
        d2s[t, 0:8, :] = total[t * 8 : (t + 1) * 8, :]
        turn = (128 - 8 * t) % 128
        line = jnp.broadcast_to(before[128:129, :], (8, 128))
        line = pltpu.roll(line, turn, 1) if turn else line
        lines = jnp.where(eight == 0, total[64:65, 0:128], line)
        lines = jnp.where(eight == 1, total[64:65, 128:256], lines)
        d2s[t, 8:16, 0:128] = lines
        d2s[t, 8:16, 128:256] = before[64 + t * 8 : 72 + t * 8, :]
    for k in range(1, 8):
        t, dev = p.tp(k)
        c.to(dev, d2s.at[t], d2l.at[p.t], trs)
    own_d2 = c.here(d2s.at[p.t], d2l.at[p.t])

    for k in (1, 3, 2):
        landed(zr.at[0], zrs.at[k])
        whole = whole + zr[k].astype(F32)
    xf = xv[...].astype(F32)
    factor = lax.rsqrt(jnp.mean(xf * xf, axis=1, keepdims=True) + EPS)
    n = xf * factor
    g = whole * gav[...]
    g = factor * (g - n * jnp.mean(g * n, axis=1, keepdims=True))
    grad_input[...] = grad_residual[...] + g
    c.own(grad_input, input_out)
    landed(ypeer, ypr)
    layer_output[...] = (residual[...] + ypeer[...].astype(F32)).astype(BF)
    c.own(layer_output, layer_out)

    @pl.when(jnp.logical_not(at_home))
    def _():
        landed(dwos, os_.at[0])
        landed(dwol, os_.at[1])

    @pl.when(at_home)
    def _():
        landed(dwol, os_.at[2])

    c.own(dwol, output_out)
    own_d2.wait()
    landed(d2l.at[pl.ds(0, 7)], trs)
    low8 = lanes(8) < 64
    totals = [jnp.zeros((8, 128), F32)] * 2
    for t in range(8):
        grad_query[:, t * 128 : (t + 1) * 128] = d2l[t, 0:8, 0:128]
        totals = [totals[i] + d2l[t, 8:16, i * 128 : (i + 1) * 128] for i in range(2)]
    for i in range(4):
        one, two = d2l[2 * i, 0:8, 128:256], d2l[2 * i + 1, 0:8, 128:256]
        cols = slice(i * 128, (i + 1) * 128)
        grad_key[:, cols] = jnp.where(low8, one, pltpu.roll(two, 64, 1))
        grad_value[:, cols] = jnp.where(low8, pltpu.roll(one, 64, 1), two)
    both = totals[0] + pltpu.roll(totals[0], 64, 1)
    vectors[...] = jnp.where(eight == 0, both, totals[0])
    share = jnp.zeros((8, 1), F32)
    for weights, grads in ((wqv, grad_query), (wkv, grad_key), (wvv, grad_value)):
        product = weights[...].astype(F32) * grads[...]
        share = share + jnp.sum(product, axis=1, keepdims=True)
    wide = lax.broadcasted_iota(jnp.int32, (8, 1024), 1)
    feature = ((p.g * 8 + p.t) * 2 + p.f) * 8 + lax.broadcasted_iota(jnp.int32, (8, 1024), 0)
    own_gain = jnp.sum(jnp.where(wide == feature, gav[...], 0.0), axis=1, keepdims=True)
    misc[...] = jnp.where(lanes(8) == 33, share / own_gain, totals[1])
    last = (
        (grad_query, query_out),
        (grad_key, key_out),
        (grad_value, value_out),
        (vectors, rows_out),
        (misc, misc_out),
    )
    for src, dst in last:
        c.own(src, dst)
    c.done()


def back(*operands):
    shape = jax.ShapeDtypeStruct
    v = pltpu.VMEM
    return pl.pallas_call(
        back_kernel,
        out_shape=(
            shape((128, 1024), BF),
            shape((128, 1024), F32),
            shape((8, 1024), F32),
            shape((8, 512), F32),
            shape((8, 512), F32),
            shape((8, 1024), F32),
            shape((8, 128), F32),
            shape((8, 128), F32),
            shape((1024, 128), F32),
            shape((1024, 128), F32),
            shape((128, 1024), F32),
        ),
        in_specs=[VMEM] * 2 + [HBM] * 27,
        out_specs=(HBM,) * 11,
        scratch_shapes=[
            v((128, 1024), BF),
            v((128, 1024), F32),
            v((8, 1024), F32),
            v((8, 512), F32),
            v((8, 512), F32),
            v((8, 128), F32),
            v((8, 128), F32),
            v((1024, 128), F32),
            v((1024, 128), F32),
            v((128, 1024), F32),
            v((128, 1024), F32),
            v((8, 1024), F32),
            v((1024, 128), F32),
            v((128, 1024), F32),
            v((2, 128, 768), BF),
            v((128, 1024), BF),
            v((128, 1024), BF),
            v((1024, 128), F32),
            v((1024, 128), BF),
            v((AHEAD + 1, KB, 2048), BF),
            v((8, 1024, 128), BF),
            v((2048, 128), BF),
            v((1024, 256), F32),
            v((1024, 256), BF),
            v((1024, 128), F32),
            v((1024, 128), F32),
            v((1024, 1024), BF),
            v((1024, 1024), BF),
            v((128, 1024), BF),
            v((1, 1024), F32),
            v((1, 64), F32),
            v((1, 64), F32),
            v((8, 1024), F32),
            v((8, 512), F32),
            v((8, 512), F32),
            v((1024, 128), BF),
            v((1024, 128), BF),
            v((128, 1024), BF),
            v((1024, 128), BF),
            v((1024, 128), BF),
            v((128, 1024), BF),
            v((16, 2, 48, 1024), BF),
            v((128, 1024), F32),
            v((16, 144, 128), BF),
            v((8, 128, 128), BF),
            v((2048, 128), BF),
            v((2, 8, 1024), F32),
            v((1024, 128), F32),
            v((8, 128, 1024), BF),
            v((16, 144, 128), BF),
            v((8, 1024), F32),
            v((8, 1024), F32),
            v((8, 1024, 128), BF),
            v((8, 1024, 128), BF),
            v((1024, 256), BF),
            v((2, 4, 128, 1024), BF),
            v((16, 80, 256), BF),
            v((4, 128, 1024), BF),
            v((4, 128, 1024), BF),
            v((4, 128, 1024), BF),
            v((16, 80, 256), BF),
            v((8, 16, 256), F32),
            v((8, 16, 256), F32),
            DMA((128,)),
            DMA,
            DMA((4,)),
            DMA((4,)),
            DMA,
            DMA((3,)),
            DMA((8,)),
            DMA((3,)),
            DMA,
            DMA((4,)),
            DMA((4,)),
            DMA,
            DMA,
            DMA,
            DMA((AHEAD + 1,)),
        ],
        compiler_params=params(2, VMEM_MIB),
        name="back",
    )(*operands)


def outputs_kernel(count, *refs):
    ins, outs, held = refs[:count], refs[count : 2 * count], refs[2 * count : 3 * count]
    sems = refs[-1]
    loads = [pltpu.make_async_copy(ins[i], held[i], sems.at[0, i]) for i in range(count)]
    for copy in loads:
        copy.start()
    stores = [
        pltpu.make_async_copy(held[i], outs[i], sems.at[1, i]) for i in range(count - 1)
    ]
    for i in range(count - 1):
        loads[i].wait()
        stores[i].start()
    loads[-1].wait()
    outs[-1][...] = held[-1][:, :32]
    for copy in stores:
        copy.wait()


def to_outputs(*arrays):
    count = len(arrays)
    shapes = [jax.ShapeDtypeStruct(a.shape, a.dtype) for a in arrays[:-1]]
    shapes.append(jax.ShapeDtypeStruct((8, 32), F32))
    return pl.pallas_call(
        functools.partial(outputs_kernel, count),
        out_shape=tuple(shapes),
        in_specs=[HBM] * count,
        out_specs=(HBM,) * (count - 1) + (VMEM,),
        scratch_shapes=[pltpu.VMEM(a.shape, a.dtype) for a in arrays] + [DMA((2, count))],
        compiler_params=pltpu.CompilerParams(vmem_limit_bytes=VMEM_MIB * 2**20),
        name="outputs",
    )(*arrays)


RATES = np.power(50000.0, -(np.arange(128) % 32) / 32.0).astype(np.float32).reshape(1, 128)


def local(
    layer_input,
    positions,
    routes,
    attn_gain,
    w_query,
    w_key,
    w_value,
    query_gain,
    key_gain,
    w_output,
    ffn_gain,
    w_router,
    w_gate,
    w_up,
    w_down,
    cotangent,
):
    x = layer_input[0]
    cot = cotangent[0]
    gain_a = attn_gain.reshape(1, 1024)
    gain_m = ffn_gain.reshape(1, 1024)
    gain_q = query_gain.reshape(1, 64)
    gain_k = key_gain.reshape(1, 64)
    own = (w_query, w_key, w_value, w_output, w_router)
    w_query, w_key, w_value, w_output, w_router = (w.astype(F32) for w in own)
    (outgoing, residual, wo, slots, grads, ewg, ewu, ewd, *kept) = front(
        x,
        cot,
        routes[0].T,
        positions,
        w_query,
        w_key,
        w_value,
        w_output,
        w_router,
        gain_a,
        gain_m,
        gain_q,
        gain_k,
        jnp.asarray(RATES),
        w_gate[0],
        w_up[0],
        w_down[0],
    )
    o, att, lse, kv, qp, *rest = kept
    passed = expert_rows(
        outgoing, residual, wo, slots, grads, ewg, ewu, ewd, cot, gain_m, qp, kv, lse
    )
    results = back(*passed, o, att, kv, qp, *rest, x, gain_a, gain_q, gain_k, w_query, w_key, w_value)
    vectors = results[6]
    (
        layer_output,
        grad_input,
        grad_query,
        grad_key,
        grad_value,
        grad_output,
        grad_gate,
        grad_up,
        grad_down,
        grad_router,
    ) = to_outputs(*results[:6], *results[8:], results[7])
    return (
        layer_output[None],
        grad_input[None],
        results[7][:, 33],
        grad_query,
        grad_key,
        grad_value,
        vectors[0, :64],
        vectors[1, :64],
        grad_output,
        vectors[3, :8],
        grad_router,
        grad_gate[None],
        grad_up[None],
        grad_down[None],
    )


def solution(mesh):
    rows = P(("ctx", "fsdp"), None)
    vector = P(("ctx", "fsdp"))
    tokens = P("fsdp", "ctx", None)
    return jax.shard_map(
        local,
        mesh=mesh,
        in_specs=(
            tokens,
            P("fsdp", "ctx"),
            tokens,
            P(),
            rows,
            rows,
            rows,
            P(),
            P(),
            rows,
            P(),
            rows,
            P("ctx", None, "fsdp"),
            P("ctx", None, "fsdp"),
            P("ctx", "fsdp", None),
            tokens,
        ),
        out_specs=(
            tokens,
            tokens,
            vector,
            rows,
            rows,
            rows,
            P(),
            P(),
            rows,
            vector,
            rows,
            P("ctx", None, "fsdp"),
            P("ctx", None, "fsdp"),
            P("ctx", "fsdp", None),
        ),
        check_vma=False,
    )
```
